512 devices in a mesh: rep: 32 (over z_hi, x, core), seq: 16 (over y, z_lo).
Axes of the slice: x: 4, y: 8, z: 8 (z_hi: 4, z_lo: 2; z = z_hi * 2 + z_lo), core: 2. Of those that a mesh axis runs over, the one named last changes fastest.
Arguments:
- queries: bfloat16 [32, 896, 2560], P('rep', 'seq'), may hold values from -130 to 130
- keys: bfloat16 [32, 896, 2560], P('rep', 'seq'), may hold values from -4 to 4
- values: bfloat16 [32, 896, 2560], P('rep', 'seq'), may hold values from -8 to 8
- residual: bfloat16 [32, 896, 5120], P('rep', None, 'seq'), may hold values from -3 to 3
- wo_values: bfloat16 [2, 2560, 5120], P(None, 'rep', 'seq'), may hold values from -0.0625 to 0.0625
- wo_exponents: int32 [2, 20, 40], replicated, may hold values from -1 to 2
- modulation: float32 [2, 5120], P(None, 'seq'), may hold values from 0.5 to 1.5
- expert_choice: int32 [32], replicated, may hold values from 0 to 1
- step_index: int32 [32], replicated, may hold values from 0 to 9
- lengths: int32 [32], replicated, may hold values from 224 to 896, as said below
Outputs:
- mixed: bfloat16 [32, 896, 5120], P('rep', None, 'seq')
The draws below stay inside these ranges and needn't reach their ends.
Inputs may be any that keep to these rules, and one draw needn't show every extreme that they name: `lengths`: every clip has at least 224 valid tokens, and some clip has all 896.
All inputs are finite; a program needn't handle non-finite values.
Results may differ from the reference program's by a relative error of at most 0.008.
Values may be sent and summed in bfloat16 or wider, within the bound.
A program may use at most 64 MiB of HBM per device.

```python
import math
import jax
import jax.numpy as jnp
from jax import lax

D = 5120
HEADS = 20
HEAD_DIM = 128
BLOCK = 128
STEPS = 10
HD = 2560
SEQ = 896
CLIPS = 32


def shared_keys(key):
    base = jnp.clip(jax.random.normal(key, (CLIPS, SEQ, HD), jnp.float32), -4.0, 4.0)
    position = jnp.arange(SEQ)
    paired = (position % 2 == 1) & (position < SEQ // 4)
    blended = base
    return jnp.where(paired[None, :, None], blended, base)


def draw_keys(key, part):
    result = shared_keys(key)
    return result.astype(jnp.bfloat16)


def draw_queries(key, part):
    key = jax.random.fold_in(key, 5)
    rough = jnp.clip(jax.random.normal(key, (CLIPS, SEQ, HD), jnp.float32), -4.0, 4.0) * 3.0
    return rough.astype(jnp.bfloat16)


def draw_lengths(key, part):
    key = jax.random.fold_in(key, 7)
    first, second = jax.random.split(key)
    spread = jax.random.randint(first, (CLIPS,), SEQ // 4, SEQ + 1)
    full_clip = jax.random.randint(second, (), 0, CLIPS)
    return jnp.where(jnp.arange(CLIPS) == full_clip, SEQ, spread).astype(jnp.int32)


def place_ends(array, key, smallest, high):
    index_at = [jax.random.randint(jax.random.fold_in(key, axis), (), 0, length) for axis, length in enumerate(array.shape)]
    longest = array.shape.index(max(array.shape))
    next_to = index_at[:longest] + [(index_at[longest] + 1) % array.shape[longest]] + index_at[longest + 1:]
    return array.at[tuple(index_at)].set(smallest).at[tuple(next_to)].set(high)


def shard_levels(own_key, shape, pieces, low, largest):
    def one(dim, shards_of):
        draws = jax.random.uniform(jax.random.fold_in(jax.random.fold_in(own_key, 6), dim), (shards_of,), jnp.float32, low / len(pieces), largest / len(pieces))
        return jnp.repeat(jnp.exp(draws), shape[dim] // shards_of).reshape((-1,) + (1,) * (len(shape) - dim - 1))

    factor_of = one(*pieces[0])
    for cut in pieces[1:]:
        factor_of = factor_of * one(*cut)
    return factor_of


def scatter_about(stream_key, extent, scale, reach, cuts=(), kind=jnp.bfloat16):
    values = scale * jax.random.normal(stream_key, extent, jnp.float32)
    if cuts:
        values = values * shard_levels(stream_key, extent, cuts, -0.22, 0.18)
    return jnp.clip(values, -reach, reach).astype(kind)


def setup_inputs(seed: int = 0) -> dict:
    key_of = jax.random.split(jax.random.key(seed), 11)
    queries = draw_queries(jax.random.fold_in(key_of[10], 71), 0)
    keys = draw_keys(jax.random.fold_in(key_of[10], 71), 0)
    values = scatter_about(key_of[2], (CLIPS, SEQ, HD), 2.0, 8.0, ((0, 32), (1, 16)))
    residual = scatter_about(key_of[3], (CLIPS, SEQ, D), 0.5, 3.0, ((0, 32), (2, 16)))
    wo_values = scatter_about(key_of[4], (2, HD, D), (4 * HD) ** -0.5, 0.0625, ((1, 32), (2, 16)))
    wo_exponents = place_ends(jax.random.randint(key_of[5], (2, HD // BLOCK, D // BLOCK), -1, 3), jax.random.fold_in(key_of[5], 1), -1, 2).astype(jnp.int32)
    modulation = jnp.clip(0.5 + 1.0 * jax.random.uniform(key_of[6], (2, D), jnp.float32) ** shard_levels(key_of[6], (2, D), ((1, 16),), -0.2, 0.2), 0.5, 1.5)
    expert_choice = place_ends(jax.random.randint(key_of[7], (CLIPS,), 0, 2), jax.random.fold_in(key_of[7], 1), 0, 1).astype(jnp.int32)
    step_index = place_ends(jax.random.randint(key_of[8], (CLIPS,), 0, STEPS), jax.random.fold_in(key_of[8], 1), 0, STEPS - 1).astype(jnp.int32)
    lengths = draw_lengths(jax.random.fold_in(key_of[10], 71), 0)
    return {"queries": queries, "keys": keys, "values": values, "residual": residual, "wo_values": wo_values, "wo_exponents": wo_exponents, "modulation": modulation, "expert_choice": expert_choice, "step_index": step_index, "lengths": lengths}


def time_features(step_now, columns):
    half = D // 2
    offset = (columns % half).astype(jnp.float32)
    freq = jnp.exp(-math.log(10000.0) * offset / half)
    moment = 1000.0 * (1.0 - step_now.astype(jnp.float32) / STEPS)
    angle = moment * freq
    return jnp.where(columns < half, jnp.cos(angle), jnp.sin(angle))


def block_powers(exponents):
    return jnp.left_shift(jnp.ones_like(exponents), exponents + 1).astype(jnp.float32) * 0.5


def reference(queries, keys, values, residual, wo_values, wo_exponents, modulation, expert_choice, step_index, lengths):
    def one_clip(packed):
        query, key_rows, value_rows, resid, expert, step_now, length = packed
        q_heads = query.reshape(SEQ, HEADS, HEAD_DIM).astype(jnp.float32)
        k_heads = key_rows.reshape(SEQ, HEADS, HEAD_DIM).astype(jnp.float32)
        v_heads = value_rows.reshape(SEQ, HEADS, HEAD_DIM).astype(jnp.float32)
        scores = jnp.einsum("qhd,khd->hqk", q_heads, k_heads) * (HEAD_DIM ** -0.5)
        valid = (jnp.arange(SEQ) < length)[None, None, :]
        scores = jnp.where(valid, scores, -1e30)
        top = jnp.max(scores, axis=-1, keepdims=True)
        probs = jnp.where(valid, jnp.exp(scores - top), 0.0)
        total = jnp.sum(probs, axis=-1)
        rounded = lax.optimization_barrier(probs.astype(jnp.bfloat16)).astype(jnp.float32)
        summed = jnp.einsum("hqk,khd->hqd", rounded, v_heads)
        attended = (summed / total[..., None]).transpose(1, 0, 2).reshape(SEQ, HD).astype(jnp.bfloat16)
        powers = block_powers(lax.dynamic_index_in_dim(wo_exponents, expert, 0, keepdims=False))
        scale = jnp.repeat(jnp.repeat(powers, BLOCK, axis=0), BLOCK, axis=1)
        chosen = lax.dynamic_index_in_dim(wo_values, expert, 0, keepdims=False)
        weight = (chosen.astype(jnp.float32) * scale).astype(jnp.bfloat16)
        proj = jnp.dot(attended, weight, preferred_element_type=jnp.float32)
        offset_row = lax.dynamic_index_in_dim(modulation, expert, 0, keepdims=False)
        gate = offset_row + time_features(step_now, jnp.arange(D, dtype=jnp.int32))
        return (resid.astype(jnp.float32) + gate[None, :] * proj).astype(jnp.bfloat16)

    return lax.map(one_clip, (queries, keys, values, residual, expert_choice, step_index, lengths))
```

```python
import math

import jax
import jax.numpy as jnp
import numpy as np
from jax import lax
from jax.experimental import pallas as pl
from jax.experimental.pallas import tpu as pltpu
from jax.sharding import PartitionSpec as P

D = 5120
HEADS = 20
HEAD_DIM = 128
STEPS = 10
NY = 8
NZL = 2
NX = 4
NZH = 4
NZ = NZL * NZH
ROWS = 56
SEQ = ROWS * NY * NZL
CLIPS = 2 * NX * NZH
HALF = ROWS * NY
QUART = HALF // 2
COLS = 320
DEPTH = 80
SCALE = HEAD_DIM**-0.5 * math.log2(math.e)

MESH = pl.DeviceIdType.MESH
F32 = jnp.float32
BF16 = jnp.bfloat16


def mod(value, size):
    return lax.rem(value + size, size)


def kernel(
    q_ref,
    k_ref,
    v_ref,
    res_ref,
    wo_ref,
    exps_hbm,
    mod_hbm,
    freq_hbm,
    expert_hbm,
    step_hbm,
    len_hbm,
    out_ref,
    exps_ref,
    mod_ref,
    freq_ref,
    expert_ref,
    step_ref,
    len_ref,
    pre,
    qkv,
    stage,
    wbuf,
    wo_rows,
    wch,
    dstage,
    attm,
    acc,
    psend,
    precv,
    resv,
    nat,
    stab,
    bias_ref,
    gate_ref,
    loc_sem,
    small_sem,
    as_sem,
    ar_sem,
    sr_sem,
    fs_sem,
    ks_sem,
    kr_sem,
    zs_sem,
    zr_sem,
    xs_sem,
    xr_sem,
    rs_sem,
    rr_sem,
    ds_sem,
    dr_sem,
    gs_sem,
    gr_sem,
    os_sem,
    or_sem,
):
    rep = lax.axis_index("rep")
    seq = lax.axis_index("seq")
    c = lax.rem(rep, 2)
    x = lax.rem(rep // 2, NX)
    zh = rep // (2 * NX)
    y = seq // NZL
    zl = lax.rem(seq, NZL)
    z = zh * NZL + zl

    def dev_y(yy):
        return {"rep": rep, "seq": yy * NZL + zl}

    def dev_z(zz):
        return {"rep": (zz // NZL) * (2 * NX) + x * 2 + c, "seq": y * NZL + lax.rem(zz, NZL)}

    def dev_x(xx):
        return {"rep": zh * (2 * NX) + xx * 2 + c, "seq": seq}

    partner = {"rep": rep, "seq": y * NZL + 1 - zl}
    sibling = {"rep": rep + 1 - 2 * c, "seq": seq}
    z_next, z_prev = dev_z(mod(z + 1, NZ)), dev_z(mod(z - 1, NZ))
    x_next, x_prev = dev_x(mod(x + 1, NX)), dev_x(mod(x - 1, NX))
    y_next, y_prev = dev_y(mod(y + 1, NY)), dev_y(mod(y - 1, NY))

    def send(src, dst, ss, rs, dev):
        pltpu.make_async_remote_copy(
            src_ref=src, dst_ref=dst, send_sem=ss, recv_sem=rs, device_id=dev, device_id_type=MESH
        ).start()

    def wait(ref, sem):
        pltpu.make_async_copy(ref, ref, sem).wait()

    def wslot(zz, xx):
        return wbuf.at[lax.rem(zz, NZL), :, zz // NZL, pl.ds((xx * 2 + c) * DEPTH, DEPTH), :]

    def lanes(phase, n):
        return pl.ds(0, HEAD_DIM) if phase == 0 else pl.ds(HEAD_DIM, (n - 1) * HEAD_DIM)

    def columns(yy, phase, n):
        first = (yy // 2) * 5 + (0 if n == 3 else 3) + phase
        return pl.ds(pl.multiple_of(first * HEAD_DIM, HEAD_DIM), HEAD_DIM if phase == 0 else (n - 1) * HEAD_DIM)

    small = (
        (exps_hbm, exps_ref),
        (expert_hbm, expert_ref),
        (step_hbm, step_ref),
        (len_hbm, len_ref),
        (mod_hbm, mod_ref),
        (freq_hbm.at[seq], freq_ref),
    )
    pltpu.make_async_copy(wo_ref, wo_rows, loc_sem.at[3]).start()
    for index, (source, target) in enumerate(small):
        pltpu.make_async_copy(source, target, small_sem.at[index]).start()

    barrier = pltpu.get_barrier_semaphore()
    for d in (1, 2, 3, 5, 6, 7):
        pl.semaphore_signal(barrier, inc=1, device_id=dev_y(mod(y + d, NY)), device_id_type=MESH)
    for dev in (z_next, z_prev, x_next, x_prev, sibling):
        pl.semaphore_signal(barrier, inc=1, device_id=dev, device_id_type=MESH)

    for j, ref in enumerate((q_ref, k_ref, v_ref)):
        pltpu.make_async_copy(ref.at[0], pre.at[j], loc_sem.at[j]).start()
    pltpu.make_async_copy(res_ref, resv, loc_sem.at[4]).start()
    own_w = wslot(z, x)
    twice = 2 - 4 * c
    mid_to, mid_from = mod(y + twice, NY), mod(y - twice, NY)

    for index, (source, target) in enumerate(small):
        pltpu.make_async_copy(source, target, small_sem.at[index]).wait()
    expert, expert_beside = expert_ref[rep], expert_ref[rep + 1 - 2 * c]
    for choice in range(2):
        powers = (jnp.left_shift(jnp.ones((HEADS, D // 128), jnp.int32), exps_ref[:, choice, :] + 1).astype(F32) * 0.5).astype(BF16)
        column = seq * COLS + lax.broadcasted_iota(jnp.int32, (D // 128, COLS), 1)
        hot = (column // 128 == lax.broadcasted_iota(jnp.int32, (D // 128, COLS), 0)).astype(F32).astype(BF16)
        stab[choice] = jnp.dot(powers, hot, preferred_element_type=F32)
    wait(wo_rows, loc_sem.at[3])
    for choice in range(2):
        for piece in range(DEPTH // 16):
            head = (rep * DEPTH + piece * 16) // HEAD_DIM
            rows = wo_rows[choice, piece * 16 : (piece + 1) * 16, :].astype(F32) * stab[choice, pl.ds(head, 1), :]
            place = pl.multiple_of((x * 2 + c) * DEPTH + piece * 16, 16)
            wbuf[zl, choice, zh, pl.ds(place, 16), :] = rows.astype(BF16)

    flat = lax.broadcasted_iota(jnp.int32, (1, SEQ), 1)
    upper = (flat >= HALF).astype(jnp.int32)
    within = flat - upper * HALF
    source = sum((within >= ROWS * m).astype(jnp.int32) for m in range(1, NY))
    position = within + (source + upper) * ROWS
    bias_ref[...] = jnp.where(position < len_ref[rep], 0.0, -1e30)
    angle = 1000.0 * (1.0 - step_ref[rep].astype(F32) / STEPS) * freq_ref[...]
    feature = jnp.where(seq < NY * NZL // 2, jnp.cos(angle), jnp.sin(angle))
    gate_ref[...] = mod_ref[pl.ds(expert, 1), :] + feature
    pl.semaphore_wait(barrier, 11)

    def run(n):
        def heads(d):
            return n if d % 2 == 0 else 5 - n

        def a2a(d, phase):
            to = mod(y + d, NY)
            cut = lanes(phase, heads(d))
            source = pre.at[:, :, columns(to, phase, heads(d))]
            if d == NY // 2:
                send(source, stage.at[:, :, cut], as_sem.at[phase, d], sr_sem.at[phase], dev_y(mid_to))
            else:
                send(source, qkv.at[:, zl, y, :, cut], as_sem.at[phase, d], ar_sem.at[phase, d], dev_y(to))

        def own_kv(phase):
            source = pre.at[pl.ds(1, 2), :, columns(y, phase, n)]
            target = qkv.at[pl.ds(1, 2), zl, y, :, lanes(phase, n)]
            send(source, target, ks_sem.at[phase, y], kr_sem.at[phase, y], partner)

        def mid_tick(phase):
            block = stage.at[:, :, lanes(phase, n)]
            wait(block, sr_sem.at[phase])
            target = qkv.at[:, zl, mid_from, :, lanes(phase, n)]
            send(block, target, fs_sem.at[phase], ar_sem.at[phase, NY // 2], dev_y(mid_to))

        def kv_tick(d, phase):
            source = mod(y - d, NY)
            wait(qkv.at[:, zl, source, :, lanes(phase, n)], ar_sem.at[phase, d])
            block = qkv.at[pl.ds(1, 2), zl, source, :, lanes(phase, n)]
            send(block, block, ks_sem.at[phase, source], kr_sem.at[phase, source], partner)

        def kv_done(phase):
            for source in range(NY):
                wait(qkv.at[pl.ds(1, 2), 1 - zl, source, :, lanes(phase, n)], kr_sem.at[phase, source])

        def z_tick(d):
            block = wslot(mod(z - d, NZ), x)
            wait(block, zr_sem.at[d])
            if d < NZ // 2:
                send(block, block, zs_sem.at[0, d], zr_sem.at[d + 1], z_next)
            elif d > NZ // 2 + 1:
                send(block, block, zs_sem.at[1, d], zr_sem.at[d - 1], z_prev)
            send(block, block, xs_sem.at[0, d], xr_sem.at[0, d], x_next)
            send(block, block, xs_sem.at[1, d], xr_sem.at[1, d], x_prev)

        def x_tick(d):
            zz = mod(z - d, NZ)
            left, right = wslot(zz, mod(x - 1, NX)), wslot(zz, mod(x + 1, NX))
            wait(left, xr_sem.at[0, d])
            wait(right, xr_sem.at[1, d])
            if d < NZ // 2:
                send(left, left, rs_sem.at[d], rr_sem.at[d], x_next)
            else:
                send(right, right, rs_sem.at[d], rr_sem.at[d], x_prev)

        def die_push(xx, index):
            rows = pl.ds(pl.multiple_of((xx * 2 + c) * DEPTH, 16), DEPTH)
            for place in range(NZL):
                for group in range(NZH):
                    low, high = wbuf[place, 0, group, rows, :], wbuf[place, 1, group, rows, :]
                    wch[place, group, rows, :] = jnp.where(expert == 1, high, low)
                    dstage[index, place, group] = jnp.where(expert_beside == 1, high, low)
            send(dstage.at[index], wch.at[:, :, rows, :], ds_sem.at[index], dr_sem.at[index], sibling)

        def head_rows(stream, j):
            rows = qkv[stream, :, :, :, j * HEAD_DIM : (j + 1) * HEAD_DIM].astype(F32)
            return rows.reshape(SEQ, HEAD_DIM).astype(BF16)

        def attend(j, half, keys, values):
            first = half * (NY // 2)
            query = qkv[0, zl, pl.ds(first, NY // 2), :, j * HEAD_DIM : (j + 1) * HEAD_DIM]
            query = query.astype(F32).reshape(QUART, HEAD_DIM).astype(BF16)
            scores = lax.dot_general(query, keys, (((1,), (1,)), ((), ())), preferred_element_type=F32)
            scores = scores + bias_ref[...]
            top = jnp.max(scores, axis=1, keepdims=True)
            probs = jnp.exp2((scores - top) * SCALE)
            total = jnp.sum(probs, axis=1, keepdims=True)
            summed = jnp.dot(probs.astype(BF16), values, preferred_element_type=F32)
            attm[y, half * QUART : (half + 1) * QUART, j * HEAD_DIM : (j + 1) * HEAD_DIM] = (summed / total).astype(BF16)

        def region(yy, kind, count):
            if kind == 0:
                return attm.at[yy, :, pl.ds(0, HEAD_DIM)]
            if kind in (1, 2):
                return attm.at[yy, pl.ds((kind - 1) * QUART, QUART), pl.ds(HEAD_DIM, (count - 1) * HEAD_DIM)]
            return attm.at[yy, pl.ds(0, QUART), pl.ds((kind - 2) * HEAD_DIM, HEAD_DIM)]

        def ring_send(t, direction, kind, yy):
            block = region(yy, kind, heads(t - 1))
            sems = gs_sem.at[direction, t - 1, kind], gr_sem.at[direction, t - 1, kind]
            send(block, block, *sems, (y_next, y_prev)[direction])

        def ring_wait(t, direction, kind):
            yy = mod(y - t if direction == 0 else y + t, NY)
            wait(region(yy, kind, heads(t)), gr_sem.at[direction, t - 1, kind])
            return yy

        def ring_tick(t, kind):
            for direction in range(2):
                yy = ring_wait(t, direction, kind)
                if t < NY // 2 - 1:
                    ring_send(t + 1, direction, kind, yy)
                else:
                    for last_kind in last_kinds(direction, heads(t)):
                        if last_kind == kind or (kind == 1 and last_kind in (3, 4)):
                            ring_send(t + 1, direction, last_kind, yy)

        def last_kinds(direction, count):
            if direction == 1:
                return (3, 2)
            return (0, 4) if count == 3 else (0,)

        def project(yy, count, which, rows=slice(0, HALF), fresh=False):
            first = 0 if count == 3 else 3 * HEAD_DIM
            weight = wch[zl if which == 0 else 1 - zl, yy // 2, first : first + count * HEAD_DIM, :]
            made = jnp.dot(attm[yy, rows, : count * HEAD_DIM], weight, preferred_element_type=F32)
            if fresh:
                acc[which, rows] = made
            else:
                acc[which, rows] += made

        def project_two(first, step, which):
            def one(i, _):
                project(mod(y + first + step * i, NY), heads(first), which)
                return 0

            lax.fori_loop(0, 2, one, 0)

        send(own_w, own_w, zs_sem.at[0, 0], zr_sem.at[1], z_next)
        send(own_w, own_w, zs_sem.at[1, 0], zr_sem.at[NZ - 1], z_prev)
        for j in range(3):
            wait(pre.at[j], loc_sem.at[j])
        for d in (4, 3, 5, 2, 6, 1, 7):
            a2a(d, 0)
        own_kv(0)
        send(own_w, own_w, xs_sem.at[0, 0], xr_sem.at[0, 0], x_next)
        send(own_w, own_w, xs_sem.at[1, 0], xr_sem.at[1, 0], x_prev)
        start = pl.multiple_of(((y // 2) * 5 + (0 if n == 3 else 3)) * HEAD_DIM, HEAD_DIM)
        own_block = qkv.at[:, zl, y, :, pl.ds(0, n * HEAD_DIM)]
        pltpu.make_async_copy(pre.at[:, :, pl.ds(start, n * HEAD_DIM)], own_block, loc_sem.at[5]).start()
        mid_tick(0)
        for d in (4, 3, 5):
            a2a(d, 1)
        z_tick(1)
        z_tick(7)
        x_tick(0)
        for d in (2, 6, 1, 7):
            a2a(d, 1)
        own_kv(1)
        for d in (1, 7, 2, 6, 3, 5, 4):
            kv_tick(d, 0)
        z_tick(2)
        z_tick(6)
        mid_tick(1)

        wait(own_block, loc_sem.at[5])
        kv_done(0)
        keys, values = head_rows(1, 0), head_rows(2, 0)
        for half in range(2):
            attend(0, half, keys, values)
        ring_send(1, 0, 0, y)
        ring_send(1, 1, 0, y)
        x_tick(1)
        x_tick(7)
        z_tick(3)
        z_tick(5)
        kv_tick(1, 1)
        kv_tick(7, 1)
        kv_tick(2, 1)
        kv_tick(6, 1)
        z_tick(4)
        kv_tick(3, 1)
        kv_tick(5, 1)
        kv_tick(4, 1)
        die_push(x, 0)
        ring_tick(1, 0)

        kv_done(1)
        pairs = {j: (head_rows(1, j), head_rows(2, j)) for j in range(1, n)}
        for j in range(1, n):
            attend(j, 0, *pairs[j])
        ring_send(1, 0, 1, y)
        ring_send(1, 1, 1, y)
        ring_tick(2, 0)
        x_tick(2)
        x_tick(6)
        for j in range(1, n):
            attend(j, 1, *pairs[j])
        ring_send(1, 0, 2, y)
        ring_send(1, 1, 2, y)
        x_tick(3)
        x_tick(5)
        ring_tick(1, 1)
        ring_tick(3, 0)
        ring_tick(1, 2)
        x_tick(4)
        die_push(mod(x - 1, NX), 1)
        die_push(mod(x + 1, NX), 2)
        ring_tick(2, 1)
        ring_tick(2, 2)
        far = mod(x + 2, NX)
        for d in range(NZ):
            wait(wslot(mod(z - d, NZ), far), rr_sem.at[d])
        die_push(far, 3)
        ring_tick(3, 1)
        ring_tick(3, 2)
        for index, xx in enumerate((x, mod(x - 1, NX), mod(x + 1, NX), far)):
            wait(wch.at[:, :, pl.ds((xx * 2 + 1 - c) * DEPTH, DEPTH), :], dr_sem.at[index])
        project(y, n, 1, fresh=True)
        project_two(1, 6, 1)
        project_two(2, 4, 1)
        project_two(3, 2, 1)
        project(y, n, 0, fresh=True)
        project_two(1, 6, 0)

        last = mod(y + NY // 2, NY)
        for kind in last_kinds(0, n):
            ring_wait(NY // 2, 0, kind)
        for half in range(2):
            ring_wait(NY // 2, 1, (3, 2)[half])
            rows = slice(half * QUART, (half + 1) * QUART)
            project(last, n, 1, rows)
            psend[rows] = acc[1, rows].astype(BF16)
            send(psend.at[rows], precv.at[rows], os_sem.at[half], or_sem.at[half], partner)
        project_two(2, 4, 0)
        project_two(3, 2, 0)
        project(last, n, 0)

        for phase in range(2):
            for d in range(1, NY):
                wait(qkv.at[:, zl, y, :, lanes(phase, heads(d))], as_sem.at[phase, d])
            wait(stage.at[:, :, lanes(phase, n)], fs_sem.at[phase])
            for source in range(NY):
                wait(qkv.at[pl.ds(1, 2), zl, source, :, lanes(phase, n)], ks_sem.at[phase, source])
        for t in range(1, NY // 2 + 1):
            for direction in range(2):
                for kind in (0, 1, 2) if t < NY // 2 else last_kinds(direction, heads(t - 1)):
                    wait(region(y, kind, heads(t - 1)), gs_sem.at[direction, t - 1, kind])

    pl.when(lax.rem(y, 2) == 0)(lambda: run(3))
    pl.when(lax.rem(y, 2) == 1)(lambda: run(2))

    for d in (0, 1, 2, 3):
        wait(own_w, zs_sem.at[0, d])
    for d in (0, 7, 6):
        wait(own_w, zs_sem.at[1, d])
    for d in range(NZ):
        wait(own_w, xs_sem.at[0, d])
        wait(own_w, xs_sem.at[1, d])
        wait(own_w, rs_sem.at[d])
    for index in range(NX):
        wait(dstage.at[index], ds_sem.at[index])
    wait(resv, loc_sem.at[4])
    gate = gate_ref[...]
    for block in range(NY):
        nat[pl.ds((block * NZL + zl) * ROWS, ROWS), :] = acc[0, block * ROWS : (block + 1) * ROWS] * gate
    for half in range(2):
        rows = slice(half * QUART, (half + 1) * QUART)
        wait(precv.at[rows], or_sem.at[half])
        acc[1, rows] = precv[rows].astype(F32)
        for block in range(half * NY // 2, (half + 1) * NY // 2):
            nat[pl.ds((block * NZL + 1 - zl) * ROWS, ROWS), :] = acc[1, block * ROWS : (block + 1) * ROWS] * gate
        for block in ((0, 1, 2), (3, 4, 5, 6))[half]:
            tokens = slice(block * 128, (block + 1) * 128)
            out_ref[0, :, tokens] = (resv[0, :, tokens].astype(F32) + nat[tokens, :].T).astype(BF16)
    for half in range(2):
        wait(psend.at[half * QUART : (half + 1) * QUART], os_sem.at[half])


def local(queries, keys, values, residual, wo_values, wo_exponents, modulation, expert_choice, step_index, lengths):
    offset = np.arange(D) % (D // 2)
    freq = np.exp(-math.log(10000.0) * offset / (D // 2)).astype(np.float32).reshape(D // COLS, 1, COLS)
    hbm = pl.BlockSpec(memory_space=pl.ANY)
    vmem = pl.BlockSpec(memory_space=pltpu.VMEM)
    dma = pltpu.SemaphoreType.DMA
    mixed = pl.pallas_call(
        kernel,
        out_shape=pltpu.VMEM((1, COLS, SEQ), BF16),
        in_specs=[hbm] * 11,
        out_specs=vmem,
        scratch_shapes=[
            pltpu.VMEM((HEADS, 2, D // 128), jnp.int32),
            pltpu.VMEM((2, COLS), F32),
            pltpu.VMEM((1, COLS), F32),
            pltpu.SMEM((CLIPS,), jnp.int32),
            pltpu.SMEM((CLIPS,), jnp.int32),
            pltpu.SMEM((CLIPS,), jnp.int32),
            pltpu.VMEM((3, ROWS, HEADS * HEAD_DIM), BF16),
            pltpu.VMEM((3, NZL, NY, ROWS, 3 * HEAD_DIM), BF16),
            pltpu.VMEM((3, ROWS, 3 * HEAD_DIM), BF16),
            pltpu.VMEM((NZL, 2, NZH, 2 * NX * DEPTH, COLS), BF16),
            pltpu.VMEM((2, DEPTH, COLS), BF16),
            pltpu.VMEM((NZL, NZH, 2 * NX * DEPTH, COLS), BF16),
            pltpu.VMEM((NX, NZL, NZH, DEPTH, COLS), BF16),
            pltpu.VMEM((NY, HALF, 3 * HEAD_DIM), BF16),
            pltpu.VMEM((2, HALF, COLS), F32),
            pltpu.VMEM((HALF, COLS), BF16),
            pltpu.VMEM((HALF, COLS), BF16),
            pltpu.VMEM((1, COLS, SEQ), BF16),
            pltpu.VMEM((SEQ, COLS), F32),
            pltpu.VMEM((2, HEADS, COLS), F32),
            pltpu.VMEM((1, SEQ), F32),
            pltpu.VMEM((1, COLS), F32),
            dma((6,)),
            dma((6,)),
            dma((2, NY)),
            dma((2, NY)),
            dma((2,)),
            dma((2,)),
            dma((2, NY)),
            dma((2, NY)),
            dma((2, NZ)),
            dma((NZ,)),
            dma((2, NZ)),
            dma((2, NZ)),
            dma((NZ,)),
            dma((NZ,)),
            dma((NX,)),
            dma((NX,)),
            dma((2, NY // 2, 5)),
            dma((2, NY // 2, 5)),
            dma((2,)),
            dma((2,)),
        ],
        compiler_params=pltpu.CompilerParams(
            collective_id=0, has_side_effects=True, vmem_limit_bytes=62 * 2**20
        ),
        cost_estimate=pl.CostEstimate(flops=2 * 10**9, bytes_accessed=3 * 10**6, transcendentals=10**6),
    )(
        queries,
        keys,
        values,
        jnp.swapaxes(residual, 1, 2),
        wo_values,
        jnp.swapaxes(wo_exponents, 0, 1),
        modulation,
        jnp.asarray(freq),
        expert_choice,
        step_index,
        lengths,
    )
    return jnp.swapaxes(mixed, 1, 2)


def solution(mesh):
    placed = (
        P("rep", "seq", None),
        P("rep", "seq", None),
        P("rep", "seq", None),
        P("rep", None, "seq"),
        P(None, "rep", "seq"),
        P(),
        P(None, "seq"),
        P(),
        P(),
        P(),
    )
    return jax.shard_map(
        local, mesh=mesh, in_specs=placed, out_specs=P("rep", None, "seq"), check_vma=False
    )
```

```python
import math

import jax
import jax.numpy as jnp
import numpy as np
from jax import lax
from jax.experimental import pallas as pl
from jax.experimental.pallas import tpu as pltpu
from jax.sharding import PartitionSpec as P

D = 5120
HEADS = 20
HEAD_DIM = 128
STEPS = 10
NY = 8
NZL = 2
NX = 4
NZH = 4
NZ = NZL * NZH
ROWS = 56
SEQ = ROWS * NY * NZL
CLIPS = 2 * NX * NZH
HALF = ROWS * NY
QUART = HALF // 2
COLS = 320
MAIN = 256
EDGE = COLS - MAIN
PACK = 2 * COLS
DEPTH = 80
SCALE = HEAD_DIM**-0.5 * math.log2(math.e)

OWN, OTHER, EDGES = 0, 1, 2
MESH = pl.DeviceIdType.MESH
F32 = jnp.float32
BF16 = jnp.bfloat16


def mod(value, size):
    return lax.rem(value + size, size)


def kernel(
    q_ref,
    k_ref,
    v_ref,
    res_ref,
    wo_ref,
    exps_hbm,
    mod_hbm,
    freq_hbm,
    expert_hbm,
    step_hbm,
    len_hbm,
    out_ref,
    exps_ref,
    mod_ref,
    freq_ref,
    expert_ref,
    step_ref,
    len_ref,
    pre,
    qkv,
    wbuf,
    wo_rows,
    wch,
    dstage,
    attm,
    acc,
    edge,
    psend,
    precv,
    esend,
    erecv,
    resv,
    nat,
    stab,
    bias_ref,
    gate_ref,
    loc_sem,
    small_sem,
    as_sem,
    ar_sem,
    ks_sem,
    kr_sem,
    zs_sem,
    zr_sem,
    xs_sem,
    xr_sem,
    rs_sem,
    rr_sem,
    ds_sem,
    dr_sem,
    gs_sem,
    gr_sem,
    os_sem,
    or_sem,
):
    rep = lax.axis_index("rep")
    seq = lax.axis_index("seq")
    c = lax.rem(rep, 2)
    x = lax.rem(rep // 2, NX)
    zh = rep // (2 * NX)
    y = seq // NZL
    zl = lax.rem(seq, NZL)
    z = zh * NZL + zl

    def dev_y(yy):
        return {"rep": rep, "seq": yy * NZL + zl}

    def dev_z(zz):
        return {"rep": (zz // NZL) * (2 * NX) + x * 2 + c, "seq": y * NZL + lax.rem(zz, NZL)}

    def dev_x(xx):
        return {"rep": zh * (2 * NX) + xx * 2 + c, "seq": seq}

    partner = {"rep": rep, "seq": y * NZL + 1 - zl}
    sibling = {"rep": rep + 1 - 2 * c, "seq": seq}
    z_next, z_prev = dev_z(mod(z + 1, NZ)), dev_z(mod(z - 1, NZ))
    x_next, x_prev = dev_x(mod(x + 1, NX)), dev_x(mod(x - 1, NX))
    y_next, y_prev = dev_y(mod(y + 1, NY)), dev_y(mod(y - 1, NY))

    def send(src, dst, ss, rs, dev):
        pltpu.make_async_remote_copy(
            src_ref=src, dst_ref=dst, send_sem=ss, recv_sem=rs, device_id=dev, device_id_type=MESH
        ).start()

    def wait(ref, sem):
        pltpu.make_async_copy(ref, ref, sem).wait()

    def wslot(zz, xx):
        return wbuf.at[lax.rem(zz, NZL), zz // NZL, pl.ds((xx * 2 + c) * DEPTH, DEPTH), :]

    def lanes(phase, n):
        return pl.ds(0, HEAD_DIM) if phase == 0 else pl.ds(HEAD_DIM, (n - 1) * HEAD_DIM)

    def columns(yy, phase, n):
        first = (yy // 2) * 5 + (0 if n == 3 else 3) + phase
        return pl.ds(pl.multiple_of(first * HEAD_DIM, HEAD_DIM), HEAD_DIM if phase == 0 else (n - 1) * HEAD_DIM)

    small = (
        (exps_hbm, exps_ref),
        (expert_hbm, expert_ref),
        (step_hbm, step_ref),
        (len_hbm, len_ref),
        (mod_hbm, mod_ref),
        (freq_hbm.at[seq], freq_ref),
    )
    pltpu.make_async_copy(wo_ref, wo_rows, loc_sem.at[3]).start()
    for index, (source, target) in enumerate(small):
        pltpu.make_async_copy(source, target, small_sem.at[index]).start()

    barrier = pltpu.get_barrier_semaphore()
    for d in range(1, NY):
        pl.semaphore_signal(barrier, inc=1, device_id=dev_y(mod(y + d, NY)), device_id_type=MESH)
    for dev in (z_next, z_prev, x_next, x_prev, sibling):
        pl.semaphore_signal(barrier, inc=1, device_id=dev, device_id_type=MESH)

    for j, ref in enumerate((q_ref, k_ref, v_ref)):
        pltpu.make_async_copy(ref.at[0], pre.at[j], loc_sem.at[j]).start()
    pltpu.make_async_copy(res_ref, resv, loc_sem.at[4]).start()
    own_w = wslot(z, x)

    for index, (source, target) in enumerate(small):
        pltpu.make_async_copy(source, target, small_sem.at[index]).wait()
    for choice in range(2):
        powers = (jnp.left_shift(jnp.ones((HEADS, D // 128), jnp.int32), exps_ref[:, choice, :] + 1).astype(F32) * 0.5).astype(BF16)
        column = seq * COLS + lax.broadcasted_iota(jnp.int32, (D // 128, COLS), 1)
        hot = (column // 128 == lax.broadcasted_iota(jnp.int32, (D // 128, COLS), 0)).astype(F32).astype(BF16)
        stab[choice] = jnp.dot(powers, hot, preferred_element_type=F32)
    wait(wo_rows, loc_sem.at[3])
    for choice in range(2):
        for piece in range(DEPTH // 16):
            head = (rep * DEPTH + piece * 16) // HEAD_DIM
            rows = wo_rows[choice, piece * 16 : (piece + 1) * 16, :].astype(F32) * stab[choice, pl.ds(head, 1), :]
            wo_rows[choice, piece * 16 : (piece + 1) * 16, :] = rows.astype(BF16)
    packed = jnp.zeros((DEPTH, PACK), F32)
    origin = lax.broadcasted_iota(jnp.int32, (COLS, PACK), 0)
    lane = lax.broadcasted_iota(jnp.int32, (COLS, PACK), 1)
    for choice in range(2):
        low = jnp.where(origin < MAIN, choice * MAIN + origin, 2 * MAIN + choice * EDGE + origin - MAIN)
        high = jnp.where(origin < EDGE, 2 * MAIN + (1 - choice) * EDGE + origin, choice * MAIN + origin - EDGE)
        hot = (lane == jnp.where(zl == 0, low, high)).astype(F32).astype(BF16)
        packed += jnp.dot(wo_rows[choice], hot, preferred_element_type=F32)
    wbuf[zl, zh, pl.ds(pl.multiple_of((x * 2 + c) * DEPTH, 16), DEPTH), :] = packed.astype(BF16)
    pl.semaphore_wait(barrier, 12)

    def tables():
        flat = lax.broadcasted_iota(jnp.int32, (1, SEQ), 1)
        upper = (flat >= HALF).astype(jnp.int32)
        within = flat - upper * HALF
        source = sum((within >= ROWS * m).astype(jnp.int32) for m in range(1, NY))
        position = within + (source + upper) * ROWS
        bias_ref[...] = jnp.where(position < len_ref[rep], 0.0, -1e30)
        angle = 1000.0 * (1.0 - step_ref[rep].astype(F32) / STEPS) * freq_ref[...]
        feature = jnp.where(seq < NY * NZL // 2, jnp.cos(angle), jnp.sin(angle))
        gate = mod_ref[pl.ds(expert_ref[rep], 1), :] + feature
        gate_ref[...] = jnp.broadcast_to(gate, (128, COLS)).T

    def run(n):
        def heads(d):
            return n if d % 2 == 0 else 5 - n

        def a2a(d, phase):
            to = mod(y + d, NY)
            cut = lanes(phase, heads(d))
            source = pre.at[:, :, columns(to, phase, heads(d))]
            send(source, qkv.at[:, zl, y, :, cut], as_sem.at[phase, d], ar_sem.at[phase, d], dev_y(to))

        def own_kv(phase):
            source = pre.at[pl.ds(1, 2), :, columns(y, phase, n)]
            target = qkv.at[pl.ds(1, 2), zl, y, :, lanes(phase, n)]
            send(source, target, ks_sem.at[phase, y], kr_sem.at[phase, y], partner)

        def kv_tick(d, phase):
            source = mod(y - d, NY)
            wait(qkv.at[:, zl, source, :, lanes(phase, n)], ar_sem.at[phase, d])
            block = qkv.at[pl.ds(1, 2), zl, source, :, lanes(phase, n)]
            send(block, block, ks_sem.at[phase, source], kr_sem.at[phase, source], partner)

        def kv_done(phase):
            for source in range(NY):
                wait(qkv.at[pl.ds(1, 2), 1 - zl, source, :, lanes(phase, n)], kr_sem.at[phase, source])

        def z_tick(d):
            block = wslot(mod(z - d, NZ), x)
            wait(block, zr_sem.at[d])
            if d < NZ // 2:
                send(block, block, zs_sem.at[0, d], zr_sem.at[d + 1], z_next)
            elif d > NZ // 2 + 1:
                send(block, block, zs_sem.at[1, d], zr_sem.at[d - 1], z_prev)
            send(block, block, xs_sem.at[0, d], xr_sem.at[0, d], x_next)
            send(block, block, xs_sem.at[1, d], xr_sem.at[1, d], x_prev)

        def x_tick(d):
            zz = mod(z - d, NZ)
            left, right = wslot(zz, mod(x - 1, NX)), wslot(zz, mod(x + 1, NX))
            wait(left, xr_sem.at[0, d])
            wait(right, xr_sem.at[1, d])
            if d < NZ // 2:
                send(left, left, rs_sem.at[d], rr_sem.at[d], x_next)
            else:
                send(right, right, rs_sem.at[d], rr_sem.at[d], x_prev)

        def die_push(xx, index):
            rows = pl.ds(pl.multiple_of((xx * 2 + c) * DEPTH, 16), DEPTH)
            expert, expert_beside = expert_ref[rep], expert_ref[rep + 1 - 2 * c]
            left = lax.broadcasted_iota(jnp.int32, (DEPTH, 2 * EDGE), 1) < EDGE
            for group in range(NZH):
                for place in range(NZL):
                    low, high = wbuf[place, group, rows, :MAIN], wbuf[place, group, rows, MAIN : 2 * MAIN]
                    cut = slice(place * MAIN, (place + 1) * MAIN)
                    wch[group, rows, cut] = jnp.where(expert == 1, high, low)
                    dstage[index, group, :, cut] = jnp.where(expert_beside == 1, high, low)
                edges = [wbuf[place, group, rows, 2 * MAIN :].astype(F32) for place in range(NZL)]
                low = jnp.where(left, edges[0], edges[1]).astype(BF16)
                high = jnp.where(left, edges[1], edges[0]).astype(BF16)
                wch[group, rows, 2 * MAIN :] = jnp.where(expert == 1, high, low)
                dstage[index, group, :, 2 * MAIN :] = jnp.where(expert_beside == 1, high, low)
            send(dstage.at[index], wch.at[:, rows, :], ds_sem.at[index], dr_sem.at[index], sibling)

        def head_rows(stream, j):
            rows = qkv[stream, :, :, :, j * HEAD_DIM : (j + 1) * HEAD_DIM].astype(F32)
            return rows.reshape(SEQ, HEAD_DIM).astype(BF16)

        def attend(j, half, keys, values):
            first = half * (NY // 2)
            query = qkv[0, zl, pl.ds(first, NY // 2), :, j * HEAD_DIM : (j + 1) * HEAD_DIM]
            query = query.astype(F32).reshape(QUART, HEAD_DIM).astype(BF16)
            scores = lax.dot_general(query, keys, (((1,), (1,)), ((), ())), preferred_element_type=F32)
            scores = scores + bias_ref[...]
            top = jnp.max(scores, axis=1, keepdims=True)
            probs = jnp.exp2((scores - top) * SCALE)
            total = jnp.sum(probs, axis=1, keepdims=True)
            summed = jnp.dot(probs.astype(BF16), values, preferred_element_type=F32)
            attm[y, half * QUART : (half + 1) * QUART, j * HEAD_DIM : (j + 1) * HEAD_DIM] = (summed / total).astype(BF16)

        def region(yy, kind, count):
            if kind == 0:
                return attm.at[yy, :, pl.ds(0, HEAD_DIM)]
            if kind in (1, 2):
                return attm.at[yy, pl.ds((kind - 1) * QUART, QUART), pl.ds(HEAD_DIM, (count - 1) * HEAD_DIM)]
            return attm.at[yy, pl.ds(0, QUART), pl.ds((kind - 2) * HEAD_DIM, HEAD_DIM)]

        def ring_send(t, direction, kind, yy):
            block = region(yy, kind, heads(t - 1))
            sems = gs_sem.at[direction, t - 1, kind], gr_sem.at[direction, t - 1, kind]
            send(block, block, *sems, (y_next, y_prev)[direction])

        def ring_wait(t, direction, kind):
            yy = mod(y - t if direction == 0 else y + t, NY)
            wait(region(yy, kind, heads(t)), gr_sem.at[direction, t - 1, kind])
            return yy

        def ring_tick(t, kind):
            for direction in range(2):
                yy = ring_wait(t, direction, kind)
                if t < NY // 2 - 1:
                    ring_send(t + 1, direction, kind, yy)
                else:
                    for last_kind in last_kinds(direction, heads(t)):
                        if last_kind == kind or (kind == 1 and last_kind in (3, 4)):
                            ring_send(t + 1, direction, last_kind, yy)

        def last_kinds(direction, count):
            if direction == 1:
                return (3, 2)
            return (0, 4) if count == 3 else (0,)

        def project(yy, count, part, rows=slice(0, HALF), fresh=False):
            first = 0 if count == 3 else 3 * HEAD_DIM
            if part == EDGES:
                cut, total = pl.ds(2 * MAIN, 2 * EDGE), edge
            else:
                cut, total = pl.ds(pl.multiple_of((zl if part == OWN else 1 - zl) * MAIN, MAIN), MAIN), acc.at[part]
            weight = wch[yy // 2, first : first + count * HEAD_DIM, cut]
            made = jnp.dot(attm[yy, rows, : count * HEAD_DIM], weight, preferred_element_type=F32)
            if fresh:
                total[rows] = made
            else:
                total[rows] += made

        def project_two(first, step, *parts):
            def one(i, _):
                for part in parts:
                    project(mod(y + first + step * i, NY), heads(first), part)
                return 0

            lax.fori_loop(0, 2, one, 0)

        send(own_w, own_w, zs_sem.at[0, 0], zr_sem.at[1], z_next)
        send(own_w, own_w, zs_sem.at[1, 0], zr_sem.at[NZ - 1], z_prev)
        for j in range(3):
            wait(pre.at[j], loc_sem.at[j])
        for d in (4, 3, 5, 2, 6, 1, 7):
            a2a(d, 0)
        own_kv(0)
        send(own_w, own_w, xs_sem.at[0, 0], xr_sem.at[0, 0], x_next)
        send(own_w, own_w, xs_sem.at[1, 0], xr_sem.at[1, 0], x_prev)
        start = pl.multiple_of(((y // 2) * 5 + (0 if n == 3 else 3)) * HEAD_DIM, HEAD_DIM)
        own_block = qkv.at[:, zl, y, :, pl.ds(0, n * HEAD_DIM)]
        pltpu.make_async_copy(pre.at[:, :, pl.ds(start, n * HEAD_DIM)], own_block, loc_sem.at[5]).start()
        tables()
        for d in (4, 3, 5):
            a2a(d, 1)
        z_tick(1)
        z_tick(7)
        x_tick(0)
        for d in (2, 6, 1, 7):
            a2a(d, 1)
        own_kv(1)
        for d in (1, 7, 2, 6, 3, 5, 4):
            kv_tick(d, 0)
        z_tick(2)
        z_tick(6)

        wait(own_block, loc_sem.at[5])
        kv_done(0)
        keys, values = head_rows(1, 0), head_rows(2, 0)
        for half in range(2):
            attend(0, half, keys, values)
        ring_send(1, 0, 0, y)
        ring_send(1, 1, 0, y)
        x_tick(1)
        x_tick(7)
        z_tick(3)
        z_tick(5)
        kv_tick(1, 1)
        kv_tick(7, 1)
        kv_tick(2, 1)
        kv_tick(6, 1)
        z_tick(4)
        kv_tick(3, 1)
        kv_tick(5, 1)
        kv_tick(4, 1)
        x_tick(2)
        x_tick(6)
        die_push(x, 0)
        ring_tick(1, 0)

        kv_done(1)
        pairs = {j: (head_rows(1, j), head_rows(2, j)) for j in range(1, n)}
        for j in range(1, n):
            attend(j, 0, *pairs[j])
        ring_send(1, 0, 1, y)
        ring_send(1, 1, 1, y)
        ring_tick(2, 0)
        x_tick(3)
        x_tick(5)
        for j in range(1, n):
            attend(j, 1, *pairs[j])
        ring_send(1, 0, 2, y)
        ring_send(1, 1, 2, y)
        ring_tick(1, 1)
        x_tick(4)
        ring_tick(3, 0)
        ring_tick(1, 2)
        die_push(mod(x - 1, NX), 1)
        die_push(mod(x + 1, NX), 2)
        ring_tick(2, 1)
        ring_tick(2, 2)
        far = mod(x + 2, NX)
        for d in range(NZ):
            wait(wslot(mod(z - d, NZ), far), rr_sem.at[d])
        die_push(far, 3)
        ring_tick(3, 1)
        ring_tick(3, 2)
        for index, xx in enumerate((x, mod(x - 1, NX), mod(x + 1, NX), far)):
            wait(wch.at[:, pl.ds((xx * 2 + 1 - c) * DEPTH, DEPTH), :], dr_sem.at[index])
        project(y, n, OTHER, fresh=True)
        project(y, n, EDGES, fresh=True)
        project_two(1, 6, OTHER, EDGES)
        project_two(2, 4, OTHER, EDGES)
        project_two(3, 2, OTHER, EDGES)
        project(y, n, OWN, fresh=True)

        last = mod(y + NY // 2, NY)
        turned = lax.rem(expert_ref[rep] + zl, 2) * EDGE
        left = lax.broadcasted_iota(jnp.int32, (QUART // 2, 2 * EDGE), 1) < EDGE
        for kind in last_kinds(0, n):
            ring_wait(NY // 2, 0, kind)
        for half in range(2):
            ring_wait(NY // 2, 1, (3, 2)[half])
            rows = slice(half * QUART, (half + 1) * QUART)
            project(last, n, OTHER, rows)
            psend[rows] = acc[OTHER, rows].astype(BF16)
            send(psend.at[rows], precv.at[rows], os_sem.at[0, half], or_sem.at[0, half], partner)
            project(last, n, EDGES, rows)
            top = edge[half * QUART : half * QUART + QUART // 2]
            low = edge[half * QUART + QUART // 2 : (half + 1) * QUART]
            both = jnp.where(left, pltpu.roll(top, EDGE - turned, 1), pltpu.roll(low, turned, 1))
            esend[half] = both.astype(BF16)
            send(esend.at[half], erecv.at[half], os_sem.at[1, half], or_sem.at[1, half], partner)
        project_two(1, 6, OWN)
        project_two(2, 4, OWN)
        project_two(3, 2, OWN)
        project(last, n, OWN)

        for phase in range(2):
            for d in range(1, NY):
                wait(qkv.at[:, zl, y, :, lanes(phase, heads(d))], as_sem.at[phase, d])
            for source in range(NY):
                wait(qkv.at[pl.ds(1, 2), zl, source, :, lanes(phase, n)], ks_sem.at[phase, source])
        for t in range(1, NY // 2 + 1):
            for direction in range(2):
                for kind in (0, 1, 2) if t < NY // 2 else last_kinds(direction, heads(t - 1)):
                    wait(region(y, kind, heads(t - 1)), gs_sem.at[direction, t - 1, kind])

    pl.when(lax.rem(y, 2) == 0)(lambda: run(3))
    pl.when(lax.rem(y, 2) == 1)(lambda: run(2))

    for d in (0, 1, 2, 3):
        wait(own_w, zs_sem.at[0, d])
    for d in (0, 7, 6):
        wait(own_w, zs_sem.at[1, d])
    for d in range(NZ):
        wait(own_w, xs_sem.at[0, d])
        wait(own_w, xs_sem.at[1, d])
        wait(own_w, rs_sem.at[d])
    for index in range(NX):
        wait(dstage.at[index], ds_sem.at[index])
    wait(resv, loc_sem.at[4])
    turned = lax.rem(expert_ref[rep] + zl, 2) * EDGE
    for block in range(NY):
        rows, place = slice(block * ROWS, (block + 1) * ROWS), pl.ds((block * NZL + zl) * ROWS, ROWS)
        nat[place, :MAIN] = acc[OWN, rows]
        nat[place, MAIN:] = pltpu.roll(edge[rows], turned, 1)
    main_at = pl.ds(pl.multiple_of(zl * EDGE, EDGE), MAIN)
    edge_at = pl.ds(pl.multiple_of((1 - zl) * MAIN, EDGE), EDGE)
    for half in range(2):
        rows = slice(half * QUART, (half + 1) * QUART)
        wait(precv.at[rows], or_sem.at[0, half])
        wait(erecv.at[half], or_sem.at[1, half])
        acc[OTHER, rows] = precv[rows].astype(F32)
        both = erecv[half].astype(F32)
        edge[half * QUART : half * QUART + QUART // 2] = both
        edge[half * QUART + QUART // 2 : (half + 1) * QUART] = pltpu.roll(both, EDGE, 1)
        for block in range(half * NY // 2, (half + 1) * NY // 2):
            rows, place = slice(block * ROWS, (block + 1) * ROWS), pl.ds((block * NZL + 1 - zl) * ROWS, ROWS)
            nat[place, :MAIN] = acc[OTHER, rows]
            nat[place, MAIN:] = edge[rows]
        for block in ((0, 1, 2), (3, 4, 5, 6))[half]:
            tokens = slice(block * 128, (block + 1) * 128)
            made = nat[tokens, :].T
            for at, part in ((main_at, made[:MAIN]), (edge_at, made[MAIN : MAIN + EDGE])):
                mixed = resv[0, at, tokens].astype(F32) + gate_ref[at, :] * part
                out_ref[0, at, tokens] = mixed.astype(BF16)
    for half in range(2):
        wait(psend.at[half * QUART : (half + 1) * QUART], os_sem.at[0, half])
        wait(esend.at[half], os_sem.at[1, half])


def local(queries, keys, values, residual, wo_values, wo_exponents, modulation, expert_choice, step_index, lengths):
    offset = np.arange(D) % (D // 2)
    freq = np.exp(-math.log(10000.0) * offset / (D // 2)).astype(np.float32).reshape(D // COLS, 1, COLS)
    hbm = pl.BlockSpec(memory_space=pl.ANY)
    vmem = pl.BlockSpec(memory_space=pltpu.VMEM)
    dma = pltpu.SemaphoreType.DMA
    mixed = pl.pallas_call(
        kernel,
        out_shape=pltpu.VMEM((1, COLS, SEQ), BF16),
        in_specs=[hbm] * 11,
        out_specs=vmem,
        scratch_shapes=[
            pltpu.VMEM((HEADS, 2, D // 128), jnp.int32),
            pltpu.VMEM((2, COLS), F32),
            pltpu.VMEM((1, COLS), F32),
            pltpu.SMEM((CLIPS,), jnp.int32),
            pltpu.SMEM((CLIPS,), jnp.int32),
            pltpu.SMEM((CLIPS,), jnp.int32),
            pltpu.VMEM((3, ROWS, HEADS * HEAD_DIM), BF16),
            pltpu.VMEM((3, NZL, NY, ROWS, 3 * HEAD_DIM), BF16),
            pltpu.VMEM((NZL, NZH, 2 * NX * DEPTH, PACK), BF16),
            pltpu.VMEM((2, DEPTH, COLS), BF16),
            pltpu.VMEM((NZH, 2 * NX * DEPTH, PACK), BF16),
            pltpu.VMEM((NX, NZH, DEPTH, PACK), BF16),
            pltpu.VMEM((NY, HALF, 3 * HEAD_DIM), BF16),
            pltpu.VMEM((2, HALF, MAIN), F32),
            pltpu.VMEM((HALF, 2 * EDGE), F32),
            pltpu.VMEM((HALF, MAIN), BF16),
            pltpu.VMEM((HALF, MAIN), BF16),
            pltpu.VMEM((2, QUART // 2, 2 * EDGE), BF16),
            pltpu.VMEM((2, QUART // 2, 2 * EDGE), BF16),
            pltpu.VMEM((1, COLS, SEQ), BF16),
            pltpu.VMEM((SEQ, MAIN + 2 * EDGE), F32),
            pltpu.VMEM((2, HEADS, COLS), F32),
            pltpu.VMEM((1, SEQ), F32),
            pltpu.VMEM((COLS, 128), F32),
            dma((6,)),
            dma((6,)),
            dma((2, NY)),
            dma((2, NY)),
            dma((2, NY)),
            dma((2, NY)),
            dma((2, NZ)),
            dma((NZ,)),
            dma((2, NZ)),
            dma((2, NZ)),
            dma((NZ,)),
            dma((NZ,)),
            dma((NX,)),
            dma((NX,)),
            dma((2, NY // 2, 5)),
            dma((2, NY // 2, 5)),
            dma((2, 2)),
            dma((2, 2)),
        ],
        compiler_params=pltpu.CompilerParams(
            collective_id=0, has_side_effects=True, vmem_limit_bytes=62 * 2**20
        ),
        cost_estimate=pl.CostEstimate(flops=2 * 10**9, bytes_accessed=3 * 10**6, transcendentals=10**6),
    )(
        queries,
        keys,
        values,
        jnp.swapaxes(residual, 1, 2),
        wo_values,
        jnp.swapaxes(wo_exponents, 0, 1),
        modulation,
        jnp.asarray(freq),
        expert_choice,
        step_index,
        lengths,
    )
    return jnp.swapaxes(mixed, 1, 2)


def solution(mesh):
    placed = (
        P("rep", "seq", None),
        P("rep", "seq", None),
        P("rep", "seq", None),
        P("rep", None, "seq"),
        P(None, "rep", "seq"),
        P(),
        P(None, "seq"),
        P(),
        P(),
        P(),
    )
    return jax.shard_map(
        local, mesh=mesh, in_specs=placed, out_specs=P("rep", None, "seq"), check_vma=False
    )
```

```python
import math

import jax
import jax.numpy as jnp
import numpy as np
from jax import lax
from jax.experimental import pallas as pl
from jax.experimental.pallas import tpu as pltpu
from jax.sharding import PartitionSpec as P

D = 5120
HEADS = 20
HEAD_DIM = 128
STEPS = 10
NY = 8
NZL = 2
NX = 4
NZH = 4
NZ = NZL * NZH
ROWS = 56
SEQ = ROWS * NY * NZL
CLIPS = 2 * NX * NZH
HALF = ROWS * NY
QUART = HALF // 2
COLS = 320
MAIN = 256
EDGE = COLS - MAIN
PACK = 2 * COLS
DEPTH = 80
SCALE = HEAD_DIM**-0.5 * math.log2(math.e)

OWN, OTHER, EDGES = 0, 1, 2
MESH = pl.DeviceIdType.MESH
F32 = jnp.float32
BF16 = jnp.bfloat16


def mod(value, size):
    return lax.rem(value + size, size)


def kernel(
    q_ref,
    k_ref,
    v_ref,
    res_ref,
    wo_ref,
    exps_hbm,
    mod_hbm,
    freq_hbm,
    expert_hbm,
    step_hbm,
    len_hbm,
    out_ref,
    exps_ref,
    mod_ref,
    freq_ref,
    expert_ref,
    step_ref,
    len_ref,
    pre,
    qkv,
    wbuf,
    wo_rows,
    wch,
    dstage,
    attm,
    acc,
    edge,
    psend,
    precv,
    esend,
    erecv,
    resv,
    nat,
    stab,
    bias_ref,
    gate_ref,
    loc_sem,
    small_sem,
    as_sem,
    ar_sem,
    ks_sem,
    kr_sem,
    zs_sem,
    zr_sem,
    xs_sem,
    xr_sem,
    rs_sem,
    rr_sem,
    ds_sem,
    dr_sem,
    gs_sem,
    gr_sem,
    os_sem,
    or_sem,
):
    rep = lax.axis_index("rep")
    seq = lax.axis_index("seq")
    c = lax.rem(rep, 2)
    x = lax.rem(rep // 2, NX)
    zh = rep // (2 * NX)
    y = seq // NZL
    zl = lax.rem(seq, NZL)
    z = zh * NZL + zl

    def dev_y(yy):
        return {"rep": rep, "seq": yy * NZL + zl}

    def dev_z(zz):
        return {"rep": (zz // NZL) * (2 * NX) + x * 2 + c, "seq": y * NZL + lax.rem(zz, NZL)}

    def dev_x(xx):
        return {"rep": zh * (2 * NX) + xx * 2 + c, "seq": seq}

    partner = {"rep": rep, "seq": y * NZL + 1 - zl}
    sibling = {"rep": rep + 1 - 2 * c, "seq": seq}
    z_next, z_prev = dev_z(mod(z + 1, NZ)), dev_z(mod(z - 1, NZ))
    x_next, x_prev = dev_x(mod(x + 1, NX)), dev_x(mod(x - 1, NX))
    y_next, y_prev = dev_y(mod(y + 1, NY)), dev_y(mod(y - 1, NY))

    def send(src, dst, ss, rs, dev):
        pltpu.make_async_remote_copy(
            src_ref=src, dst_ref=dst, send_sem=ss, recv_sem=rs, device_id=dev, device_id_type=MESH
        ).start()

    def wait(ref, sem):
        pltpu.make_async_copy(ref, ref, sem).wait()

    def wslot(zz, xx):
        return wbuf.at[lax.rem(zz, NZL), zz // NZL, pl.ds((xx * 2 + c) * DEPTH, DEPTH), :]

    def lanes(phase, n):
        return pl.ds(0, HEAD_DIM) if phase == 0 else pl.ds(HEAD_DIM, (n - 1) * HEAD_DIM)

    def columns(yy, phase, n):
        first = (yy // 2) * 5 + (0 if n == 3 else 3) + phase
        return pl.ds(pl.multiple_of(first * HEAD_DIM, HEAD_DIM), HEAD_DIM if phase == 0 else (n - 1) * HEAD_DIM)

    small = (
        (exps_hbm, exps_ref),
        (expert_hbm, expert_ref),
        (step_hbm, step_ref),
        (len_hbm, len_ref),
        (mod_hbm, mod_ref),
        (freq_hbm.at[seq], freq_ref),
    )
    pltpu.make_async_copy(wo_ref, wo_rows, loc_sem.at[3]).start()
    for index, (source, target) in enumerate(small):
        pltpu.make_async_copy(source, target, small_sem.at[index]).start()

    barrier = pltpu.get_barrier_semaphore()
    for d in range(1, NY):
        pl.semaphore_signal(barrier, inc=1, device_id=dev_y(mod(y + d, NY)), device_id_type=MESH)
    for dev in (z_next, z_prev, x_next, x_prev, sibling):
        pl.semaphore_signal(barrier, inc=1, device_id=dev, device_id_type=MESH)

    for j, ref in enumerate((q_ref, k_ref, v_ref)):
        pltpu.make_async_copy(ref.at[0], pre.at[j], loc_sem.at[j]).start()
    pltpu.make_async_copy(res_ref, resv, loc_sem.at[4]).start()
    own_w = wslot(z, x)

    for index, (source, target) in enumerate(small):
        pltpu.make_async_copy(source, target, small_sem.at[index]).wait()
    for choice in range(2):
        powers = (jnp.left_shift(jnp.ones((HEADS, D // 128), jnp.int32), exps_ref[:, choice, :] + 1).astype(F32) * 0.5).astype(BF16)
        column = seq * COLS + lax.broadcasted_iota(jnp.int32, (D // 128, COLS), 1)
        hot = (column // 128 == lax.broadcasted_iota(jnp.int32, (D // 128, COLS), 0)).astype(F32).astype(BF16)
        stab[choice] = jnp.dot(powers, hot, preferred_element_type=F32)
    wait(wo_rows, loc_sem.at[3])
    for choice in range(2):
        for piece in range(DEPTH // 16):
            head = (rep * DEPTH + piece * 16) // HEAD_DIM
            rows = wo_rows[choice, piece * 16 : (piece + 1) * 16, :].astype(F32) * stab[choice, pl.ds(head, 1), :]
            wo_rows[choice, piece * 16 : (piece + 1) * 16, :] = rows.astype(BF16)
    packed = jnp.zeros((DEPTH, PACK), F32)
    origin = lax.broadcasted_iota(jnp.int32, (COLS, PACK), 0)
    lane = lax.broadcasted_iota(jnp.int32, (COLS, PACK), 1)
    for choice in range(2):
        low = jnp.where(origin < MAIN, choice * MAIN + origin, 2 * MAIN + choice * EDGE + origin - MAIN)
        high = jnp.where(origin < EDGE, 2 * MAIN + (1 - choice) * EDGE + origin, choice * MAIN + origin - EDGE)
        hot = (lane == jnp.where(zl == 0, low, high)).astype(F32).astype(BF16)
        packed += jnp.dot(wo_rows[choice], hot, preferred_element_type=F32)
    wbuf[zl, zh, pl.ds(pl.multiple_of((x * 2 + c) * DEPTH, 16), DEPTH), :] = packed.astype(BF16)
    pl.semaphore_wait(barrier, 12)

    def tables():
        flat = lax.broadcasted_iota(jnp.int32, (1, SEQ), 1)
        upper = (flat >= HALF).astype(jnp.int32)
        within = flat - upper * HALF
        source = sum((within >= ROWS * m).astype(jnp.int32) for m in range(1, NY))
        position = within + (source + upper) * ROWS
        bias_ref[...] = jnp.where(position < len_ref[rep], 0.0, -1e30)
        angle = 1000.0 * (1.0 - step_ref[rep].astype(F32) / STEPS) * freq_ref[...]
        feature = jnp.where(seq < NY * NZL // 2, jnp.cos(angle), jnp.sin(angle))
        gate = mod_ref[pl.ds(expert_ref[rep], 1), :] + feature
        gate_ref[...] = jnp.broadcast_to(gate, (128, COLS)).T

    def run(n):
        def heads(d):
            return n if d % 2 == 0 else 5 - n

        def a2a(d, phase):
            to = mod(y + d, NY)
            cut = lanes(phase, heads(d))
            source = pre.at[:, :, columns(to, phase, heads(d))]
            send(source, qkv.at[:, zl, y, :, cut], as_sem.at[phase, d], ar_sem.at[phase, d], dev_y(to))

        def own_kv(phase):
            source = pre.at[pl.ds(1, 2), :, columns(y, phase, n)]
            target = qkv.at[pl.ds(1, 2), zl, y, :, lanes(phase, n)]
            send(source, target, ks_sem.at[phase, y], kr_sem.at[phase, y], partner)

        def kv_tick(d, phase):
            source = mod(y - d, NY)
            wait(qkv.at[:, zl, source, :, lanes(phase, n)], ar_sem.at[phase, d])
            block = qkv.at[pl.ds(1, 2), zl, source, :, lanes(phase, n)]
            send(block, block, ks_sem.at[phase, source], kr_sem.at[phase, source], partner)

        def kv_done(phase):
            for source in range(NY):
                wait(qkv.at[pl.ds(1, 2), 1 - zl, source, :, lanes(phase, n)], kr_sem.at[phase, source])

        def z_tick(d):
            block = wslot(mod(z - d, NZ), x)
            wait(block, zr_sem.at[d])
            if d < NZ // 2:
                send(block, block, zs_sem.at[0, d], zr_sem.at[d + 1], z_next)
            elif d > NZ // 2 + 1:
                send(block, block, zs_sem.at[1, d], zr_sem.at[d - 1], z_prev)
            send(block, block, xs_sem.at[0, d], xr_sem.at[0, d], x_next)
            send(block, block, xs_sem.at[1, d], xr_sem.at[1, d], x_prev)

        def x_tick(d):
            zz = mod(z - d, NZ)
            left, right = wslot(zz, mod(x - 1, NX)), wslot(zz, mod(x + 1, NX))
            wait(left, xr_sem.at[0, d])
            wait(right, xr_sem.at[1, d])
            if d < NZ // 2:
                send(left, left, rs_sem.at[d], rr_sem.at[d], x_next)
            else:
                send(right, right, rs_sem.at[d], rr_sem.at[d], x_prev)

        def die_push(xx, index):
            rows = pl.ds(pl.multiple_of((xx * 2 + c) * DEPTH, 16), DEPTH)
            expert, expert_beside = expert_ref[rep], expert_ref[rep + 1 - 2 * c]
            left = lax.broadcasted_iota(jnp.int32, (DEPTH, 2 * EDGE), 1) < EDGE
            for group in range(NZH):
                for place in range(NZL):
                    low, high = wbuf[place, group, rows, :MAIN], wbuf[place, group, rows, MAIN : 2 * MAIN]
                    cut = slice(place * MAIN, (place + 1) * MAIN)
                    wch[group, rows, cut] = jnp.where(expert == 1, high, low)
                    dstage[index, group, :, cut] = jnp.where(expert_beside == 1, high, low)
                edges = [wbuf[place, group, rows, 2 * MAIN :].astype(F32) for place in range(NZL)]
                low = jnp.where(left, edges[0], edges[1]).astype(BF16)
                high = jnp.where(left, edges[1], edges[0]).astype(BF16)
                wch[group, rows, 2 * MAIN :] = jnp.where(expert == 1, high, low)
                dstage[index, group, :, 2 * MAIN :] = jnp.where(expert_beside == 1, high, low)
            send(dstage.at[index], wch.at[:, rows, :], ds_sem.at[index], dr_sem.at[index], sibling)

        def head_rows(stream, j):
            rows = qkv[stream, :, :, :, j * HEAD_DIM : (j + 1) * HEAD_DIM].astype(F32)
            return rows.reshape(SEQ, HEAD_DIM).astype(BF16)

        def attend(j, half, keys, values):
            first = half * (NY // 2)
            query = qkv[0, zl, pl.ds(first, NY // 2), :, j * HEAD_DIM : (j + 1) * HEAD_DIM]
            query = query.astype(F32).reshape(QUART, HEAD_DIM).astype(BF16)
            scores = lax.dot_general(query, keys, (((1,), (1,)), ((), ())), preferred_element_type=F32)
            scores = scores + bias_ref[...]
            top = jnp.max(scores, axis=1, keepdims=True)
            probs = jnp.exp2((scores - top) * SCALE)
            total = jnp.sum(probs, axis=1, keepdims=True)
            summed = jnp.dot(probs.astype(BF16), values, preferred_element_type=F32)
            attm[y, half * QUART : (half + 1) * QUART, j * HEAD_DIM : (j + 1) * HEAD_DIM] = (summed / total).astype(BF16)

        def region(yy, kind, count):
            if kind == 0:
                return attm.at[yy, :, pl.ds(0, HEAD_DIM)]
            if kind in (1, 2):
                return attm.at[yy, pl.ds((kind - 1) * QUART, QUART), pl.ds(HEAD_DIM, (count - 1) * HEAD_DIM)]
            return attm.at[yy, pl.ds(0, QUART), pl.ds((kind - 2) * HEAD_DIM, HEAD_DIM)]

        def ring_send(t, direction, kind, yy):
            block = region(yy, kind, heads(t - 1))
            sems = gs_sem.at[direction, t - 1, kind], gr_sem.at[direction, t - 1, kind]
            send(block, block, *sems, (y_next, y_prev)[direction])

        def ring_wait(t, direction, kind):
            yy = mod(y - t if direction == 0 else y + t, NY)
            wait(region(yy, kind, heads(t)), gr_sem.at[direction, t - 1, kind])
            return yy

        def ring_tick(t, kind):
            for direction in range(2):
                yy = ring_wait(t, direction, kind)
                if t < NY // 2 - 1:
                    ring_send(t + 1, direction, kind, yy)
                else:
                    for last_kind in last_kinds(direction, heads(t)):
                        if last_kind == kind or (kind == 1 and last_kind in (3, 4)):
                            ring_send(t + 1, direction, last_kind, yy)

        def last_kinds(direction, count):
            if direction == 1:
                return (3, 2)
            return (0, 4) if count == 3 else (0,)

        def project(yy, count, part, rows=slice(0, HALF), fresh=False):
            first = 0 if count == 3 else 3 * HEAD_DIM
            if part == EDGES:
                cut, total = pl.ds(2 * MAIN, 2 * EDGE), edge
            else:
                cut, total = pl.ds(pl.multiple_of((zl if part == OWN else 1 - zl) * MAIN, MAIN), MAIN), acc.at[part]
            weight = wch[yy // 2, first : first + count * HEAD_DIM, cut]
            made = jnp.dot(attm[yy, rows, : count * HEAD_DIM], weight, preferred_element_type=F32)
            if fresh:
                total[rows] = made
            else:
                total[rows] += made

        def project_two(first, step, *parts):
            def one(i, _):
                for part in parts:
                    project(mod(y + first + step * i, NY), heads(first), part)
                return 0

            lax.fori_loop(0, 2, one, 0)

        order = (4, 3, 5, 2, 6, 1, 7)
        send(own_w, own_w, zs_sem.at[0, 0], zr_sem.at[1], z_next)
        send(own_w, own_w, zs_sem.at[1, 0], zr_sem.at[NZ - 1], z_prev)
        for j in range(3):
            wait(pre.at[j], loc_sem.at[j])
        own_kv(0)
        for d in order:
            a2a(d, 0)
        send(own_w, own_w, xs_sem.at[0, 0], xr_sem.at[0, 0], x_next)
        send(own_w, own_w, xs_sem.at[1, 0], xr_sem.at[1, 0], x_prev)
        start = pl.multiple_of(((y // 2) * 5 + (0 if n == 3 else 3)) * HEAD_DIM, HEAD_DIM)
        own_block = qkv.at[:, zl, y, :, pl.ds(0, n * HEAD_DIM)]
        pltpu.make_async_copy(pre.at[:, :, pl.ds(start, n * HEAD_DIM)], own_block, loc_sem.at[5]).start()
        tables()
        own_kv(1)
        for d in order[:3]:
            a2a(d, 1)
        z_tick(1)
        z_tick(7)
        for d in order[:3]:
            kv_tick(d, 0)
        for d in order[3:]:
            a2a(d, 1)
        x_tick(0)
        for d in order[3:]:
            kv_tick(d, 0)
        z_tick(2)
        z_tick(6)

        wait(own_block, loc_sem.at[5])
        kv_done(0)
        keys, values = head_rows(1, 0), head_rows(2, 0)
        for half in range(2):
            attend(0, half, keys, values)
        ring_send(1, 0, 0, y)
        ring_send(1, 1, 0, y)
        for d in order[:2]:
            kv_tick(d, 1)
        x_tick(1)
        x_tick(7)
        for d in order[2:4]:
            kv_tick(d, 1)
        z_tick(3)
        z_tick(5)
        for d in order[4:6]:
            kv_tick(d, 1)
        z_tick(4)
        kv_tick(order[6], 1)
        x_tick(2)
        x_tick(6)
        die_push(x, 0)
        ring_tick(1, 0)

        kv_done(1)
        pairs = {j: (head_rows(1, j), head_rows(2, j)) for j in range(1, n)}
        for j in range(1, n):
            attend(j, 0, *pairs[j])
        ring_send(1, 0, 1, y)
        ring_send(1, 1, 1, y)
        ring_tick(2, 0)
        x_tick(3)
        x_tick(5)
        for j in range(1, n):
            attend(j, 1, *pairs[j])
        ring_send(1, 0, 2, y)
        ring_send(1, 1, 2, y)
        ring_tick(1, 1)
        x_tick(4)
        ring_tick(3, 0)
        ring_tick(1, 2)
        die_push(mod(x - 1, NX), 1)
        die_push(mod(x + 1, NX), 2)
        ring_tick(2, 1)
        ring_tick(2, 2)
        far = mod(x + 2, NX)
        for d in range(NZ):
            wait(wslot(mod(z - d, NZ), far), rr_sem.at[d])
        die_push(far, 3)
        ring_tick(3, 1)
        ring_tick(3, 2)
        for index, xx in enumerate((x, mod(x - 1, NX), mod(x + 1, NX), far)):
            wait(wch.at[:, pl.ds((xx * 2 + 1 - c) * DEPTH, DEPTH), :], dr_sem.at[index])
        project(y, n, OTHER, fresh=True)
        project(y, n, EDGES, fresh=True)
        project_two(1, 6, OTHER, EDGES)
        project_two(2, 4, OTHER, EDGES)
        project_two(3, 2, OTHER, EDGES)
        project(y, n, OWN, fresh=True)

        last = mod(y + NY // 2, NY)
        turned = lax.rem(expert_ref[rep] + zl, 2) * EDGE
        left = lax.broadcasted_iota(jnp.int32, (QUART // 2, 2 * EDGE), 1) < EDGE
        for kind in last_kinds(0, n):
            ring_wait(NY // 2, 0, kind)
        for half in range(2):
            ring_wait(NY // 2, 1, (3, 2)[half])
            rows = slice(half * QUART, (half + 1) * QUART)
            project(last, n, OTHER, rows)
            psend[rows] = acc[OTHER, rows].astype(BF16)
            send(psend.at[rows], precv.at[rows], os_sem.at[0, half], or_sem.at[0, half], partner)
            project(last, n, EDGES, rows)
            top = edge[half * QUART : half * QUART + QUART // 2]
            low = edge[half * QUART + QUART // 2 : (half + 1) * QUART]
            both = jnp.where(left, pltpu.roll(top, EDGE - turned, 1), pltpu.roll(low, turned, 1))
            esend[half] = both.astype(BF16)
            send(esend.at[half], erecv.at[half], os_sem.at[1, half], or_sem.at[1, half], partner)
        project_two(1, 6, OWN)
        project_two(2, 4, OWN)
        project_two(3, 2, OWN)
        project(last, n, OWN)

        for phase in range(2):
            for d in range(1, NY):
                wait(qkv.at[:, zl, y, :, lanes(phase, heads(d))], as_sem.at[phase, d])
            for source in range(NY):
                wait(qkv.at[pl.ds(1, 2), zl, source, :, lanes(phase, n)], ks_sem.at[phase, source])
        for t in range(1, NY // 2 + 1):
            for direction in range(2):
                for kind in (0, 1, 2) if t < NY // 2 else last_kinds(direction, heads(t - 1)):
                    wait(region(y, kind, heads(t - 1)), gs_sem.at[direction, t - 1, kind])

    pl.when(lax.rem(y, 2) == 0)(lambda: run(3))
    pl.when(lax.rem(y, 2) == 1)(lambda: run(2))

    for d in (0, 1, 2, 3):
        wait(own_w, zs_sem.at[0, d])
    for d in (0, 7, 6):
        wait(own_w, zs_sem.at[1, d])
    for d in range(NZ):
        wait(own_w, xs_sem.at[0, d])
        wait(own_w, xs_sem.at[1, d])
        wait(own_w, rs_sem.at[d])
    for index in range(NX):
        wait(dstage.at[index], ds_sem.at[index])
    wait(resv, loc_sem.at[4])
    turned = lax.rem(expert_ref[rep] + zl, 2) * EDGE
    for block in range(NY):
        rows, place = slice(block * ROWS, (block + 1) * ROWS), pl.ds((block * NZL + zl) * ROWS, ROWS)
        nat[place, :MAIN] = acc[OWN, rows]
        nat[place, MAIN:] = pltpu.roll(edge[rows], turned, 1)
    main_at = pl.ds(pl.multiple_of(zl * EDGE, EDGE), MAIN)
    edge_at = pl.ds(pl.multiple_of((1 - zl) * MAIN, EDGE), EDGE)
    for half in range(2):
        rows = slice(half * QUART, (half + 1) * QUART)
        wait(precv.at[rows], or_sem.at[0, half])
        wait(erecv.at[half], or_sem.at[1, half])
        acc[OTHER, rows] = precv[rows].astype(F32)
        both = erecv[half].astype(F32)
        edge[half * QUART : half * QUART + QUART // 2] = both
        edge[half * QUART + QUART // 2 : (half + 1) * QUART] = pltpu.roll(both, EDGE, 1)
        for block in range(half * NY // 2, (half + 1) * NY // 2):
            rows, place = slice(block * ROWS, (block + 1) * ROWS), pl.ds((block * NZL + 1 - zl) * ROWS, ROWS)
            nat[place, :MAIN] = acc[OTHER, rows]
            nat[place, MAIN:] = edge[rows]
        for block in ((0, 1, 2), (3, 4, 5, 6))[half]:
            tokens = slice(block * 128, (block + 1) * 128)
            made = nat[tokens, :].T
            for at, part in ((main_at, made[:MAIN]), (edge_at, made[MAIN : MAIN + EDGE])):
                mixed = resv[0, at, tokens].astype(F32) + gate_ref[at, :] * part
                out_ref[0, at, tokens] = mixed.astype(BF16)
    for half in range(2):
        wait(psend.at[half * QUART : (half + 1) * QUART], os_sem.at[0, half])
        wait(esend.at[half], os_sem.at[1, half])


def local(queries, keys, values, residual, wo_values, wo_exponents, modulation, expert_choice, step_index, lengths):
    offset = np.arange(D) % (D // 2)
    freq = np.exp(-math.log(10000.0) * offset / (D // 2)).astype(np.float32).reshape(D // COLS, 1, COLS)
    hbm = pl.BlockSpec(memory_space=pl.ANY)
    vmem = pl.BlockSpec(memory_space=pltpu.VMEM)
    dma = pltpu.SemaphoreType.DMA
    mixed = pl.pallas_call(
        kernel,
        out_shape=pltpu.VMEM((1, COLS, SEQ), BF16),
        in_specs=[hbm] * 11,
        out_specs=vmem,
        scratch_shapes=[
            pltpu.VMEM((HEADS, 2, D // 128), jnp.int32),
            pltpu.VMEM((2, COLS), F32),
            pltpu.VMEM((1, COLS), F32),
            pltpu.SMEM((CLIPS,), jnp.int32),
            pltpu.SMEM((CLIPS,), jnp.int32),
            pltpu.SMEM((CLIPS,), jnp.int32),
            pltpu.VMEM((3, ROWS, HEADS * HEAD_DIM), BF16),
            pltpu.VMEM((3, NZL, NY, ROWS, 3 * HEAD_DIM), BF16),
            pltpu.VMEM((NZL, NZH, 2 * NX * DEPTH, PACK), BF16),
            pltpu.VMEM((2, DEPTH, COLS), BF16),
            pltpu.VMEM((NZH, 2 * NX * DEPTH, PACK), BF16),
            pltpu.VMEM((NX, NZH, DEPTH, PACK), BF16),
            pltpu.VMEM((NY, HALF, 3 * HEAD_DIM), BF16),
            pltpu.VMEM((2, HALF, MAIN), F32),
            pltpu.VMEM((HALF, 2 * EDGE), F32),
            pltpu.VMEM((HALF, MAIN), BF16),
            pltpu.VMEM((HALF, MAIN), BF16),
            pltpu.VMEM((2, QUART // 2, 2 * EDGE), BF16),
            pltpu.VMEM((2, QUART // 2, 2 * EDGE), BF16),
            pltpu.VMEM((1, COLS, SEQ), BF16),
            pltpu.VMEM((SEQ, MAIN + 2 * EDGE), F32),
            pltpu.VMEM((2, HEADS, COLS), F32),
            pltpu.VMEM((1, SEQ), F32),
            pltpu.VMEM((COLS, 128), F32),
            dma((6,)),
            dma((6,)),
            dma((2, NY)),
            dma((2, NY)),
            dma((2, NY)),
            dma((2, NY)),
            dma((2, NZ)),
            dma((NZ,)),
            dma((2, NZ)),
            dma((2, NZ)),
            dma((NZ,)),
            dma((NZ,)),
            dma((NX,)),
            dma((NX,)),
            dma((2, NY // 2, 5)),
            dma((2, NY // 2, 5)),
            dma((2, 2)),
            dma((2, 2)),
        ],
        compiler_params=pltpu.CompilerParams(
            collective_id=0, has_side_effects=True, vmem_limit_bytes=62 * 2**20
        ),
        cost_estimate=pl.CostEstimate(flops=2 * 10**9, bytes_accessed=3 * 10**6, transcendentals=10**6),
    )(
        queries,
        keys,
        values,
        jnp.swapaxes(residual, 1, 2),
        wo_values,
        jnp.swapaxes(wo_exponents, 0, 1),
        modulation,
        jnp.asarray(freq),
        expert_choice,
        step_index,
        lengths,
    )
    return jnp.swapaxes(mixed, 1, 2)


def solution(mesh):
    placed = (
        P("rep", "seq", None),
        P("rep", "seq", None),
        P("rep", "seq", None),
        P("rep", None, "seq"),
        P(None, "rep", "seq"),
        P(),
        P(None, "seq"),
        P(),
        P(),
        P(),
    )
    return jax.shard_map(
        local, mesh=mesh, in_specs=placed, out_specs=P("rep", None, "seq"), check_vma=False
    )
```

```python
import math

import jax
import jax.numpy as jnp
import numpy as np
from jax import lax
from jax.experimental import pallas as pl
from jax.experimental.pallas import tpu as pltpu
from jax.sharding import PartitionSpec as P

D = 5120
HEADS = 20
HEAD_DIM = 128
STEPS = 10
NY = 8
NZL = 2
NX = 4
NZH = 4
NZ = NZL * NZH
ROWS = 56
SEQ = ROWS * NY * NZL
CLIPS = 2 * NX * NZH
HALF = ROWS * NY
QUART = HALF // 2
COLS = 320
MAIN = 256
EDGE = COLS - MAIN
PACK = 2 * COLS
DEPTH = 80
SCALE = HEAD_DIM**-0.5 * math.log2(math.e)

OWN, OTHER, EDGES = 0, 1, 2
MESH = pl.DeviceIdType.MESH
F32 = jnp.float32
BF16 = jnp.bfloat16


def mod(value, size):
    return lax.rem(value + size, size)


def kernel(
    q_ref,
    k_ref,
    v_ref,
    res_ref,
    wo_ref,
    exps_hbm,
    mod_hbm,
    freq_hbm,
    expert_hbm,
    step_hbm,
    len_hbm,
    out_ref,
    exps_ref,
    mod_ref,
    freq_ref,
    expert_ref,
    step_ref,
    len_ref,
    pre,
    qkv,
    wbuf,
    wo_rows,
    wch,
    dstage,
    attm,
    acc,
    edge,
    psend,
    precv,
    esend,
    erecv,
    resv,
    nat,
    stab,
    bias_ref,
    gate_ref,
    loc_sem,
    small_sem,
    as_sem,
    ar_sem,
    ks_sem,
    kr_sem,
    zs_sem,
    zr_sem,
    xs_sem,
    xr_sem,
    rs_sem,
    rr_sem,
    ds_sem,
    dr_sem,
    gs_sem,
    gr_sem,
    os_sem,
    or_sem,
):
    rep = lax.axis_index("rep")
    seq = lax.axis_index("seq")
    c = lax.rem(rep, 2)
    x = lax.rem(rep // 2, NX)
    zh = rep // (2 * NX)
    y = seq // NZL
    zl = lax.rem(seq, NZL)
    z = zh * NZL + zl

    def dev_y(yy):
        return {"rep": rep, "seq": yy * NZL + zl}

    def dev_z(zz):
        return {"rep": (zz // NZL) * (2 * NX) + x * 2 + c, "seq": y * NZL + lax.rem(zz, NZL)}

    def dev_x(xx):
        return {"rep": zh * (2 * NX) + xx * 2 + c, "seq": seq}

    partner = {"rep": rep, "seq": y * NZL + 1 - zl}
    sibling = {"rep": rep + 1 - 2 * c, "seq": seq}
    z_next, z_prev = dev_z(mod(z + 1, NZ)), dev_z(mod(z - 1, NZ))
    x_next, x_prev = dev_x(mod(x + 1, NX)), dev_x(mod(x - 1, NX))
    y_next, y_prev = dev_y(mod(y + 1, NY)), dev_y(mod(y - 1, NY))

    def send(src, dst, ss, rs, dev):
        pltpu.make_async_remote_copy(
            src_ref=src, dst_ref=dst, send_sem=ss, recv_sem=rs, device_id=dev, device_id_type=MESH
        ).start()

    def wait(ref, sem):
        pltpu.make_async_copy(ref, ref, sem).wait()

    def wslot(zz, xx):
        return wbuf.at[lax.rem(zz, NZL), zz // NZL, pl.ds((xx * 2 + c) * DEPTH, DEPTH), :]

    def lanes(phase, n):
        return pl.ds(0, (n - 1) * HEAD_DIM) if phase == 0 else pl.ds((n - 1) * HEAD_DIM, HEAD_DIM)

    def columns(yy, phase, n):
        first = (yy // 2) * 5 + (0 if n == 3 else 3) + phase * (n - 1)
        return pl.ds(pl.multiple_of(first * HEAD_DIM, HEAD_DIM), (n - 1) * HEAD_DIM if phase == 0 else HEAD_DIM)

    small = (
        (exps_hbm, exps_ref),
        (expert_hbm, expert_ref),
        (step_hbm, step_ref),
        (len_hbm, len_ref),
        (mod_hbm, mod_ref),
        (freq_hbm.at[seq], freq_ref),
    )
    pltpu.make_async_copy(wo_ref, wo_rows, loc_sem.at[3]).start()
    for index, (source, target) in enumerate(small):
        pltpu.make_async_copy(source, target, small_sem.at[index]).start()

    barrier = pltpu.get_barrier_semaphore()
    for d in range(1, NY):
        pl.semaphore_signal(barrier, inc=1, device_id=dev_y(mod(y + d, NY)), device_id_type=MESH)
    for dev in (z_next, z_prev, x_next, x_prev, sibling):
        pl.semaphore_signal(barrier, inc=1, device_id=dev, device_id_type=MESH)

    for j, ref in enumerate((q_ref, k_ref, v_ref)):
        pltpu.make_async_copy(ref.at[0], pre.at[j], loc_sem.at[j]).start()
    pltpu.make_async_copy(res_ref, resv, loc_sem.at[4]).start()
    own_w = wslot(z, x)

    for index, (source, target) in enumerate(small):
        pltpu.make_async_copy(source, target, small_sem.at[index]).wait()
    for choice in range(2):
        powers = (jnp.left_shift(jnp.ones((HEADS, D // 128), jnp.int32), exps_ref[:, choice, :] + 1).astype(F32) * 0.5).astype(BF16)
        column = seq * COLS + lax.broadcasted_iota(jnp.int32, (D // 128, COLS), 1)
        hot = (column // 128 == lax.broadcasted_iota(jnp.int32, (D // 128, COLS), 0)).astype(F32).astype(BF16)
        stab[choice] = jnp.dot(powers, hot, preferred_element_type=F32)
    wait(wo_rows, loc_sem.at[3])
    for choice in range(2):
        for piece in range(DEPTH // 16):
            head = (rep * DEPTH + piece * 16) // HEAD_DIM
            rows = wo_rows[choice, piece * 16 : (piece + 1) * 16, :].astype(F32) * stab[choice, pl.ds(head, 1), :]
            wo_rows[choice, piece * 16 : (piece + 1) * 16, :] = rows.astype(BF16)
    packed = jnp.zeros((DEPTH, PACK), F32)
    origin = lax.broadcasted_iota(jnp.int32, (COLS, PACK), 0)
    lane = lax.broadcasted_iota(jnp.int32, (COLS, PACK), 1)
    for choice in range(2):
        low = jnp.where(origin < MAIN, choice * MAIN + origin, 2 * MAIN + choice * EDGE + origin - MAIN)
        high = jnp.where(origin < EDGE, 2 * MAIN + (1 - choice) * EDGE + origin, choice * MAIN + origin - EDGE)
        hot = (lane == jnp.where(zl == 0, low, high)).astype(F32).astype(BF16)
        packed += jnp.dot(wo_rows[choice], hot, preferred_element_type=F32)
    wbuf[zl, zh, pl.ds(pl.multiple_of((x * 2 + c) * DEPTH, 16), DEPTH), :] = packed.astype(BF16)
    pl.semaphore_wait(barrier, 12)

    def tables():
        flat = lax.broadcasted_iota(jnp.int32, (1, SEQ), 1)
        upper = (flat >= HALF).astype(jnp.int32)
        within = flat - upper * HALF
        source = sum((within >= ROWS * m).astype(jnp.int32) for m in range(1, NY))
        position = within + (source + upper) * ROWS
        bias_ref[...] = jnp.where(position < len_ref[rep], 0.0, -1e30)
        angle = 1000.0 * (1.0 - step_ref[rep].astype(F32) / STEPS) * freq_ref[...]
        feature = jnp.where(seq < NY * NZL // 2, jnp.cos(angle), jnp.sin(angle))
        gate = mod_ref[pl.ds(expert_ref[rep], 1), :] + feature
        gate_ref[...] = jnp.broadcast_to(gate, (128, COLS)).T

    def run(n):
        def heads(d):
            return n if d % 2 == 0 else 5 - n

        def a2a(d, phase):
            to = mod(y + d, NY)
            cut = lanes(phase, heads(d))
            source = pre.at[:, :, columns(to, phase, heads(d))]
            send(source, qkv.at[:, zl, y, :, cut], as_sem.at[phase, d], ar_sem.at[phase, d], dev_y(to))

        def own_kv(phase):
            source = pre.at[pl.ds(1, 2), :, columns(y, phase, n)]
            target = qkv.at[pl.ds(1, 2), zl, y, :, lanes(phase, n)]
            send(source, target, ks_sem.at[phase, y], kr_sem.at[phase, y], partner)

        def kv_tick(d, phase):
            source = mod(y - d, NY)
            wait(qkv.at[:, zl, source, :, lanes(phase, n)], ar_sem.at[phase, d])
            block = qkv.at[pl.ds(1, 2), zl, source, :, lanes(phase, n)]
            send(block, block, ks_sem.at[phase, source], kr_sem.at[phase, source], partner)

        def kv_done(phase):
            for source in range(NY):
                wait(qkv.at[pl.ds(1, 2), 1 - zl, source, :, lanes(phase, n)], kr_sem.at[phase, source])

        def z_tick(d):
            block = wslot(mod(z - d, NZ), x)
            wait(block, zr_sem.at[d])
            if d < NZ // 2:
                send(block, block, zs_sem.at[0, d], zr_sem.at[d + 1], z_next)
            elif d > NZ // 2 + 1:
                send(block, block, zs_sem.at[1, d], zr_sem.at[d - 1], z_prev)
            send(block, block, xs_sem.at[0, d], xr_sem.at[0, d], x_next)
            send(block, block, xs_sem.at[1, d], xr_sem.at[1, d], x_prev)

        def x_tick(d):
            zz = mod(z - d, NZ)
            left, right = wslot(zz, mod(x - 1, NX)), wslot(zz, mod(x + 1, NX))
            wait(left, xr_sem.at[0, d])
            wait(right, xr_sem.at[1, d])
            if d < NZ // 2:
                send(left, left, rs_sem.at[d], rr_sem.at[d], x_next)
            else:
                send(right, right, rs_sem.at[d], rr_sem.at[d], x_prev)

        def die_push(xx, index):
            rows = pl.ds(pl.multiple_of((xx * 2 + c) * DEPTH, 16), DEPTH)
            expert, expert_beside = expert_ref[rep], expert_ref[rep + 1 - 2 * c]
            left = lax.broadcasted_iota(jnp.int32, (DEPTH, 2 * EDGE), 1) < EDGE
            for group in range(NZH):
                for place in range(NZL):
                    low, high = wbuf[place, group, rows, :MAIN], wbuf[place, group, rows, MAIN : 2 * MAIN]
                    cut = slice(place * MAIN, (place + 1) * MAIN)
                    wch[group, rows, cut] = jnp.where(expert == 1, high, low)
                    dstage[index, group, :, cut] = jnp.where(expert_beside == 1, high, low)
                edges = [wbuf[place, group, rows, 2 * MAIN :].astype(F32) for place in range(NZL)]
                low = jnp.where(left, edges[0], edges[1]).astype(BF16)
                high = jnp.where(left, edges[1], edges[0]).astype(BF16)
                wch[group, rows, 2 * MAIN :] = jnp.where(expert == 1, high, low)
                dstage[index, group, :, 2 * MAIN :] = jnp.where(expert_beside == 1, high, low)
            send(dstage.at[index], wch.at[:, rows, :], ds_sem.at[index], dr_sem.at[index], sibling)

        def head_rows(stream, j):
            rows = qkv[stream, :, :, :, j * HEAD_DIM : (j + 1) * HEAD_DIM].astype(F32)
            return rows.reshape(SEQ, HEAD_DIM).astype(BF16)

        def attend(j, half, keys, values):
            first = half * (NY // 2)
            query = qkv[0, zl, pl.ds(first, NY // 2), :, j * HEAD_DIM : (j + 1) * HEAD_DIM]
            query = query.astype(F32).reshape(QUART, HEAD_DIM).astype(BF16)
            scores = lax.dot_general(query, keys, (((1,), (1,)), ((), ())), preferred_element_type=F32)
            scores = scores + bias_ref[...]
            top = jnp.max(scores, axis=1, keepdims=True)
            probs = jnp.exp2((scores - top) * SCALE)
            total = jnp.sum(probs, axis=1, keepdims=True)
            summed = jnp.dot(probs.astype(BF16), values, preferred_element_type=F32)
            attm[y, half * QUART : (half + 1) * QUART, j * HEAD_DIM : (j + 1) * HEAD_DIM] = (summed / total).astype(BF16)

        def kinds(count):
            return (0, 1, 2, 3) if count == 3 else (0, 2, 3)

        def last_kinds(direction, count):
            return ((0, 2), (1, 3))[direction] if count == 3 else ((0,), (2, 3))[direction]

        def region(yy, kind, count):
            if kind < 2:
                return attm.at[yy, :, pl.ds(kind * HEAD_DIM, HEAD_DIM)]
            return attm.at[yy, pl.ds((kind - 2) * QUART, QUART), pl.ds((count - 1) * HEAD_DIM, HEAD_DIM)]

        def ring_send(t, direction, kind, yy):
            block = region(yy, kind, heads(t - 1))
            sems = gs_sem.at[direction, t - 1, kind], gr_sem.at[direction, t - 1, kind]
            send(block, block, *sems, (y_next, y_prev)[direction])

        def ring_start(kind):
            for direction in range(2):
                ring_send(1, direction, kind, y)

        def ring_wait(t, direction, kind):
            yy = mod(y - t if direction == 0 else y + t, NY)
            wait(region(yy, kind, heads(t)), gr_sem.at[direction, t - 1, kind])
            return yy

        def ring_tick(t, kind):
            if kind not in kinds(heads(t)):
                return
            for direction in range(2):
                yy = ring_wait(t, direction, kind)
                if t < NY // 2 - 1 or kind in last_kinds(direction, heads(t)):
                    ring_send(t + 1, direction, kind, yy)

        def project(yy, count, part, rows=slice(0, HALF), fresh=False):
            first = 0 if count == 3 else 3 * HEAD_DIM
            if part == EDGES:
                cut, total = pl.ds(2 * MAIN, 2 * EDGE), edge
            else:
                cut, total = pl.ds(pl.multiple_of((zl if part == OWN else 1 - zl) * MAIN, MAIN), MAIN), acc.at[part]
            weight = wch[yy // 2, first : first + count * HEAD_DIM, cut]
            made = jnp.dot(attm[yy, rows, : count * HEAD_DIM], weight, preferred_element_type=F32)
            if fresh:
                total[rows] = made
            else:
                total[rows] += made

        def project_two(first, step, *parts):
            def one(i, _):
                for part in parts:
                    project(mod(y + first + step * i, NY), heads(first), part)
                return 0

            lax.fori_loop(0, 2, one, 0)

        order = (4, 3, 5, 2, 6, 1, 7)
        send(own_w, own_w, zs_sem.at[0, 0], zr_sem.at[1], z_next)
        send(own_w, own_w, zs_sem.at[1, 0], zr_sem.at[NZ - 1], z_prev)
        for j in range(3):
            wait(pre.at[j], loc_sem.at[j])
        own_kv(0)
        for d in order:
            a2a(d, 0)
        send(own_w, own_w, xs_sem.at[0, 0], xr_sem.at[0, 0], x_next)
        send(own_w, own_w, xs_sem.at[1, 0], xr_sem.at[1, 0], x_prev)
        start = pl.multiple_of(((y // 2) * 5 + (0 if n == 3 else 3)) * HEAD_DIM, HEAD_DIM)
        own_block = qkv.at[:, zl, y, :, pl.ds(0, n * HEAD_DIM)]
        pltpu.make_async_copy(pre.at[:, :, pl.ds(start, n * HEAD_DIM)], own_block, loc_sem.at[5]).start()
        tables()
        own_kv(1)
        for d in order[:3]:
            a2a(d, 1)
        z_tick(1)
        z_tick(7)
        for d in order[:3]:
            kv_tick(d, 0)
        for d in order[3:]:
            a2a(d, 1)
        x_tick(0)
        z_tick(2)
        z_tick(6)
        for d in order[3:5]:
            kv_tick(d, 0)
        x_tick(1)
        x_tick(7)
        for d in order[5:]:
            kv_tick(d, 0)
        z_tick(3)
        z_tick(5)

        wait(own_block, loc_sem.at[5])
        kv_done(0)
        for j in range(n - 1):
            keys, values = head_rows(1, j), head_rows(2, j)
            for half in range(2):
                attend(j, half, keys, values)
            ring_start(j)
            for d in order[:2] if j == 0 else order[2:4]:
                kv_tick(d, 1)
            if j == 0:
                z_tick(4)
        for d in order[2 * (n - 1) :]:
            kv_tick(d, 1)
        x_tick(2)
        x_tick(6)
        ring_tick(1, 0)
        die_push(x, 0)

        kv_done(1)
        keys, values = head_rows(1, n - 1), head_rows(2, n - 1)
        attend(n - 1, 0, keys, values)
        ring_start(2)
        ring_tick(1, 1)
        attend(n - 1, 1, keys, values)
        ring_start(3)
        ring_tick(2, 0)
        x_tick(3)
        x_tick(5)
        ring_tick(2, 1)
        ring_tick(1, 2)
        ring_tick(1, 3)
        x_tick(4)
        die_push(mod(x - 1, NX), 1)
        die_push(mod(x + 1, NX), 2)
        ring_tick(3, 0)
        ring_tick(2, 2)
        ring_tick(2, 3)
        ring_tick(3, 1)
        far = mod(x + 2, NX)
        for d in range(NZ):
            wait(wslot(mod(z - d, NZ), far), rr_sem.at[d])
        die_push(far, 3)
        ring_tick(3, 2)
        ring_tick(3, 3)
        for index, xx in enumerate((x, mod(x - 1, NX), mod(x + 1, NX), far)):
            wait(wch.at[:, pl.ds((xx * 2 + 1 - c) * DEPTH, DEPTH), :], dr_sem.at[index])
        project(y, n, OTHER, fresh=True)
        project(y, n, EDGES, fresh=True)
        project_two(1, 6, OTHER, EDGES)
        project_two(2, 4, OTHER, EDGES)
        project_two(3, 2, OTHER, EDGES)
        project(y, n, OWN, fresh=True)

        last = mod(y + NY // 2, NY)
        turned = lax.rem(expert_ref[rep] + zl, 2) * EDGE
        left = lax.broadcasted_iota(jnp.int32, (QUART // 2, 2 * EDGE), 1) < EDGE
        for half in range(2):
            for kind in ((0, 1, 2) if n == 3 else (0, 2)) if half == 0 else (3,):
                ring_wait(NY // 2, 0 if kind in last_kinds(0, n) else 1, kind)
            rows = slice(half * QUART, (half + 1) * QUART)
            project(last, n, OTHER, rows)
            psend[rows] = acc[OTHER, rows].astype(BF16)
            send(psend.at[rows], precv.at[rows], os_sem.at[0, half], or_sem.at[0, half], partner)
            project(last, n, EDGES, rows)
            top = edge[half * QUART : half * QUART + QUART // 2]
            low = edge[half * QUART + QUART // 2 : (half + 1) * QUART]
            both = jnp.where(left, pltpu.roll(top, EDGE - turned, 1), pltpu.roll(low, turned, 1))
            esend[half] = both.astype(BF16)
            send(esend.at[half], erecv.at[half], os_sem.at[1, half], or_sem.at[1, half], partner)
        project_two(1, 6, OWN)
        project_two(2, 4, OWN)
        project_two(3, 2, OWN)
        project(last, n, OWN)

        for phase in range(2):
            for d in range(1, NY):
                wait(qkv.at[:, zl, y, :, lanes(phase, heads(d))], as_sem.at[phase, d])
            for source in range(NY):
                wait(qkv.at[pl.ds(1, 2), zl, source, :, lanes(phase, n)], ks_sem.at[phase, source])
        for t in range(1, NY // 2 + 1):
            for direction in range(2):
                for kind in kinds(heads(t - 1)) if t < NY // 2 else last_kinds(direction, heads(t - 1)):
                    wait(region(y, kind, heads(t - 1)), gs_sem.at[direction, t - 1, kind])

    pl.when(lax.rem(y, 2) == 0)(lambda: run(3))
    pl.when(lax.rem(y, 2) == 1)(lambda: run(2))

    for d in (0, 1, 2, 3):
        wait(own_w, zs_sem.at[0, d])
    for d in (0, 7, 6):
        wait(own_w, zs_sem.at[1, d])
    for d in range(NZ):
        wait(own_w, xs_sem.at[0, d])
        wait(own_w, xs_sem.at[1, d])
        wait(own_w, rs_sem.at[d])
    for index in range(NX):
        wait(dstage.at[index], ds_sem.at[index])
    wait(resv, loc_sem.at[4])
    turned = lax.rem(expert_ref[rep] + zl, 2) * EDGE
    for block in range(NY):
        rows, place = slice(block * ROWS, (block + 1) * ROWS), pl.ds((block * NZL + zl) * ROWS, ROWS)
        nat[place, :MAIN] = acc[OWN, rows]
        nat[place, MAIN:] = pltpu.roll(edge[rows], turned, 1)
    main_at = pl.ds(pl.multiple_of(zl * EDGE, EDGE), MAIN)
    edge_at = pl.ds(pl.multiple_of((1 - zl) * MAIN, EDGE), EDGE)
    for half in range(2):
        rows = slice(half * QUART, (half + 1) * QUART)
        wait(precv.at[rows], or_sem.at[0, half])
        wait(erecv.at[half], or_sem.at[1, half])
        acc[OTHER, rows] = precv[rows].astype(F32)
        both = erecv[half].astype(F32)
        edge[half * QUART : half * QUART + QUART // 2] = both
        edge[half * QUART + QUART // 2 : (half + 1) * QUART] = pltpu.roll(both, EDGE, 1)
        for block in range(half * NY // 2, (half + 1) * NY // 2):
            rows, place = slice(block * ROWS, (block + 1) * ROWS), pl.ds((block * NZL + 1 - zl) * ROWS, ROWS)
            nat[place, :MAIN] = acc[OTHER, rows]
            nat[place, MAIN:] = edge[rows]
        for block in ((0, 1, 2), (3, 4, 5, 6))[half]:
            tokens = slice(block * 128, (block + 1) * 128)
            made = nat[tokens, :].T
            for at, part in ((main_at, made[:MAIN]), (edge_at, made[MAIN : MAIN + EDGE])):
                mixed = resv[0, at, tokens].astype(F32) + gate_ref[at, :] * part
                out_ref[0, at, tokens] = mixed.astype(BF16)
    for half in range(2):
        wait(psend.at[half * QUART : (half + 1) * QUART], os_sem.at[0, half])
        wait(esend.at[half], os_sem.at[1, half])


def local(queries, keys, values, residual, wo_values, wo_exponents, modulation, expert_choice, step_index, lengths):
    offset = np.arange(D) % (D // 2)
    freq = np.exp(-math.log(10000.0) * offset / (D // 2)).astype(np.float32).reshape(D // COLS, 1, COLS)
    hbm = pl.BlockSpec(memory_space=pl.ANY)
    vmem = pl.BlockSpec(memory_space=pltpu.VMEM)
    dma = pltpu.SemaphoreType.DMA
    mixed = pl.pallas_call(
        kernel,
        out_shape=pltpu.VMEM((1, COLS, SEQ), BF16),
        in_specs=[hbm] * 11,
        out_specs=vmem,
        scratch_shapes=[
            pltpu.VMEM((HEADS, 2, D // 128), jnp.int32),
            pltpu.VMEM((2, COLS), F32),
            pltpu.VMEM((1, COLS), F32),
            pltpu.SMEM((CLIPS,), jnp.int32),
            pltpu.SMEM((CLIPS,), jnp.int32),
            pltpu.SMEM((CLIPS,), jnp.int32),
            pltpu.VMEM((3, ROWS, HEADS * HEAD_DIM), BF16),
            pltpu.VMEM((3, NZL, NY, ROWS, 3 * HEAD_DIM), BF16),
            pltpu.VMEM((NZL, NZH, 2 * NX * DEPTH, PACK), BF16),
            pltpu.VMEM((2, DEPTH, COLS), BF16),
            pltpu.VMEM((NZH, 2 * NX * DEPTH, PACK), BF16),
            pltpu.VMEM((NX, NZH, DEPTH, PACK), BF16),
            pltpu.VMEM((NY, HALF, 3 * HEAD_DIM), BF16),
            pltpu.VMEM((2, HALF, MAIN), F32),
            pltpu.VMEM((HALF, 2 * EDGE), F32),
            pltpu.VMEM((HALF, MAIN), BF16),
            pltpu.VMEM((HALF, MAIN), BF16),
            pltpu.VMEM((2, QUART // 2, 2 * EDGE), BF16),
            pltpu.VMEM((2, QUART // 2, 2 * EDGE), BF16),
            pltpu.VMEM((1, COLS, SEQ), BF16),
            pltpu.VMEM((SEQ, MAIN + 2 * EDGE), F32),
            pltpu.VMEM((2, HEADS, COLS), F32),
            pltpu.VMEM((1, SEQ), F32),
            pltpu.VMEM((COLS, 128), F32),
            dma((6,)),
            dma((6,)),
            dma((2, NY)),
            dma((2, NY)),
            dma((2, NY)),
            dma((2, NY)),
            dma((2, NZ)),
            dma((NZ,)),
            dma((2, NZ)),
            dma((2, NZ)),
            dma((NZ,)),
            dma((NZ,)),
            dma((NX,)),
            dma((NX,)),
            dma((2, NY // 2, 5)),
            dma((2, NY // 2, 5)),
            dma((2, 2)),
            dma((2, 2)),
        ],
        compiler_params=pltpu.CompilerParams(
            collective_id=0, has_side_effects=True, vmem_limit_bytes=62 * 2**20
        ),
        cost_estimate=pl.CostEstimate(flops=2 * 10**9, bytes_accessed=3 * 10**6, transcendentals=10**6),
    )(
        queries,
        keys,
        values,
        jnp.swapaxes(residual, 1, 2),
        wo_values,
        jnp.swapaxes(wo_exponents, 0, 1),
        modulation,
        jnp.asarray(freq),
        expert_choice,
        step_index,
        lengths,
    )
    return jnp.swapaxes(mixed, 1, 2)


def solution(mesh):
    placed = (
        P("rep", "seq", None),
        P("rep", "seq", None),
        P("rep", "seq", None),
        P("rep", None, "seq"),
        P(None, "rep", "seq"),
        P(),
        P(None, "seq"),
        P(),
        P(),
        P(),
    )
    return jax.shard_map(
        local, mesh=mesh, in_specs=placed, out_specs=P("rep", None, "seq"), check_vma=False
    )
```

```python
import math

import jax
import jax.numpy as jnp
import numpy as np
from jax import lax
from jax.experimental import pallas as pl
from jax.experimental.pallas import tpu as pltpu
from jax.sharding import PartitionSpec as P

D = 5120
HEADS = 20
HEAD_DIM = 128
STEPS = 10
NY = 8
NZL = 2
NX = 4
NZH = 4
NZ = NZL * NZH
ROWS = 56
SEQ = ROWS * NY * NZL
CLIPS = 2 * NX * NZH
HALF = ROWS * NY
QUART = HALF // 2
COLS = 320
MAIN = 256
EDGE = COLS - MAIN
PACK = 2 * COLS
DEPTH = 80
SCALE = HEAD_DIM**-0.5 * math.log2(math.e)

OWN, OTHER, EDGES = 0, 1, 2
MESH = pl.DeviceIdType.MESH
F32 = jnp.float32
BF16 = jnp.bfloat16


def mod(value, size):
    return lax.rem(value + size, size)


def kernel(
    q_ref,
    k_ref,
    v_ref,
    res_ref,
    wo_ref,
    exps_hbm,
    mod_hbm,
    freq_hbm,
    expert_hbm,
    step_hbm,
    len_hbm,
    out_ref,
    exps_ref,
    mod_ref,
    freq_ref,
    expert_ref,
    step_ref,
    len_ref,
    pre,
    qkv,
    wbuf,
    wo_rows,
    wch,
    dstage,
    attm,
    acc,
    edge,
    psend,
    precv,
    esend,
    erecv,
    resv,
    nat,
    stab,
    bias_ref,
    gate_ref,
    loc_sem,
    small_sem,
    as_sem,
    ar_sem,
    ks_sem,
    kr_sem,
    zs_sem,
    zr_sem,
    xs_sem,
    xr_sem,
    rs_sem,
    rr_sem,
    ds_sem,
    dr_sem,
    gs_sem,
    gr_sem,
    os_sem,
    or_sem,
):
    rep = lax.axis_index("rep")
    seq = lax.axis_index("seq")
    c = lax.rem(rep, 2)
    x = lax.rem(rep // 2, NX)
    zh = rep // (2 * NX)
    y = seq // NZL
    zl = lax.rem(seq, NZL)
    z = zh * NZL + zl

    def dev_y(yy):
        return {"rep": rep, "seq": yy * NZL + zl}

    def dev_z(zz):
        return {"rep": (zz // NZL) * (2 * NX) + x * 2 + c, "seq": y * NZL + lax.rem(zz, NZL)}

    def dev_x(xx):
        return {"rep": zh * (2 * NX) + xx * 2 + c, "seq": seq}

    partner = {"rep": rep, "seq": y * NZL + 1 - zl}
    sibling = {"rep": rep + 1 - 2 * c, "seq": seq}
    z_next, z_prev = dev_z(mod(z + 1, NZ)), dev_z(mod(z - 1, NZ))
    x_next, x_prev = dev_x(mod(x + 1, NX)), dev_x(mod(x - 1, NX))
    y_next, y_prev = dev_y(mod(y + 1, NY)), dev_y(mod(y - 1, NY))

    def send(src, dst, ss, rs, dev):
        pltpu.make_async_remote_copy(
            src_ref=src, dst_ref=dst, send_sem=ss, recv_sem=rs, device_id=dev, device_id_type=MESH
        ).start()

    def wait(ref, sem):
        pltpu.make_async_copy(ref, ref, sem).wait()

    def wslot(zz, xx):
        return wbuf.at[lax.rem(zz, NZL), zz // NZL, pl.ds((xx * 2 + c) * DEPTH, DEPTH), :]

    def lanes(phase, n):
        return pl.ds(0, (n - 1) * HEAD_DIM) if phase == 0 else pl.ds((n - 1) * HEAD_DIM, HEAD_DIM)

    def columns(yy, phase, n):
        first = (yy // 2) * 5 + (0 if n == 3 else 3) + phase * (n - 1)
        return pl.ds(pl.multiple_of(first * HEAD_DIM, HEAD_DIM), (n - 1) * HEAD_DIM if phase == 0 else HEAD_DIM)

    small = (
        (exps_hbm, exps_ref),
        (expert_hbm, expert_ref),
        (step_hbm, step_ref),
        (len_hbm, len_ref),
        (mod_hbm, mod_ref),
        (freq_hbm.at[seq], freq_ref),
    )
    pltpu.make_async_copy(wo_ref, wo_rows, loc_sem.at[3]).start()
    for index, (source, target) in enumerate(small):
        pltpu.make_async_copy(source, target, small_sem.at[index]).start()

    barrier = pltpu.get_barrier_semaphore()
    for d in range(1, NY):
        pl.semaphore_signal(barrier, inc=1, device_id=dev_y(mod(y + d, NY)), device_id_type=MESH)
    for dev in (z_next, z_prev, x_next, x_prev, sibling):
        pl.semaphore_signal(barrier, inc=1, device_id=dev, device_id_type=MESH)

    for j, ref in enumerate((q_ref, k_ref, v_ref)):
        pltpu.make_async_copy(ref.at[0], pre.at[j], loc_sem.at[j]).start()
    pltpu.make_async_copy(res_ref, resv, loc_sem.at[4]).start()
    own_w = wslot(z, x)

    for index, (source, target) in enumerate(small):
        pltpu.make_async_copy(source, target, small_sem.at[index]).wait()
    for choice in range(2):
        powers = (jnp.left_shift(jnp.ones((HEADS, D // 128), jnp.int32), exps_ref[:, choice, :] + 1).astype(F32) * 0.5).astype(BF16)
        column = seq * COLS + lax.broadcasted_iota(jnp.int32, (D // 128, COLS), 1)
        hot = (column // 128 == lax.broadcasted_iota(jnp.int32, (D // 128, COLS), 0)).astype(F32).astype(BF16)
        stab[choice] = jnp.dot(powers, hot, preferred_element_type=F32)
    wait(wo_rows, loc_sem.at[3])
    for choice in range(2):
        for piece in range(DEPTH // 16):
            head = (rep * DEPTH + piece * 16) // HEAD_DIM
            rows = wo_rows[choice, piece * 16 : (piece + 1) * 16, :].astype(F32) * stab[choice, pl.ds(head, 1), :]
            wo_rows[choice, piece * 16 : (piece + 1) * 16, :] = rows.astype(BF16)
    packed = jnp.zeros((DEPTH, PACK), F32)
    origin = lax.broadcasted_iota(jnp.int32, (COLS, PACK), 0)
    lane = lax.broadcasted_iota(jnp.int32, (COLS, PACK), 1)
    for choice in range(2):
        low = jnp.where(origin < MAIN, choice * MAIN + origin, 2 * MAIN + choice * EDGE + origin - MAIN)
        high = jnp.where(origin < EDGE, 2 * MAIN + (1 - choice) * EDGE + origin, choice * MAIN + origin - EDGE)
        hot = (lane == jnp.where(zl == 0, low, high)).astype(F32).astype(BF16)
        packed += jnp.dot(wo_rows[choice], hot, preferred_element_type=F32)
    wbuf[zl, zh, pl.ds(pl.multiple_of((x * 2 + c) * DEPTH, 16), DEPTH), :] = packed.astype(BF16)
    pl.semaphore_wait(barrier, 12)

    def tables():
        flat = lax.broadcasted_iota(jnp.int32, (1, SEQ), 1)
        upper = (flat >= HALF).astype(jnp.int32)
        within = flat - upper * HALF
        source = sum((within >= ROWS * m).astype(jnp.int32) for m in range(1, NY))
        position = within + (source + upper) * ROWS
        bias_ref[...] = jnp.where(position < len_ref[rep], 0.0, -1e30)
        angle = 1000.0 * (1.0 - step_ref[rep].astype(F32) / STEPS) * freq_ref[...]
        feature = jnp.where(seq < NY * NZL // 2, jnp.cos(angle), jnp.sin(angle))
        gate = mod_ref[pl.ds(expert_ref[rep], 1), :] + feature
        gate_ref[...] = jnp.broadcast_to(gate, (128, COLS)).T

    def run(n):
        def heads(d):
            return n if d % 2 == 0 else 5 - n

        def a2a(d, phase):
            to = mod(y + d, NY)
            cut = lanes(phase, heads(d))
            source = pre.at[:, :, columns(to, phase, heads(d))]
            send(source, qkv.at[:, zl, y, :, cut], as_sem.at[phase, d], ar_sem.at[phase, d], dev_y(to))

        def own_kv(phase):
            source = pre.at[pl.ds(1, 2), :, columns(y, phase, n)]
            target = qkv.at[pl.ds(1, 2), zl, y, :, lanes(phase, n)]
            send(source, target, ks_sem.at[phase, y], kr_sem.at[phase, y], partner)

        def kv_tick(d, phase):
            source = mod(y - d, NY)
            wait(qkv.at[:, zl, source, :, lanes(phase, n)], ar_sem.at[phase, d])
            block = qkv.at[pl.ds(1, 2), zl, source, :, lanes(phase, n)]
            send(block, block, ks_sem.at[phase, source], kr_sem.at[phase, source], partner)

        def kv_done(phase):
            for source in range(NY):
                wait(qkv.at[pl.ds(1, 2), 1 - zl, source, :, lanes(phase, n)], kr_sem.at[phase, source])

        def z_tick(d):
            block = wslot(mod(z - d, NZ), x)
            wait(block, zr_sem.at[d])
            if d < NZ // 2:
                send(block, block, zs_sem.at[0, d], zr_sem.at[d + 1], z_next)
            elif d > NZ // 2 + 1:
                send(block, block, zs_sem.at[1, d], zr_sem.at[d - 1], z_prev)
            send(block, block, xs_sem.at[0, d], xr_sem.at[0, d], x_next)
            send(block, block, xs_sem.at[1, d], xr_sem.at[1, d], x_prev)

        def x_tick(d):
            zz = mod(z - d, NZ)
            left, right = wslot(zz, mod(x - 1, NX)), wslot(zz, mod(x + 1, NX))
            wait(left, xr_sem.at[0, d])
            wait(right, xr_sem.at[1, d])
            if d < NZ // 2:
                send(left, left, rs_sem.at[d], rr_sem.at[d], x_next)
            else:
                send(right, right, rs_sem.at[d], rr_sem.at[d], x_prev)

        def die_push(xx, index):
            rows = pl.ds(pl.multiple_of((xx * 2 + c) * DEPTH, 16), DEPTH)
            expert, expert_beside = expert_ref[rep], expert_ref[rep + 1 - 2 * c]
            left = lax.broadcasted_iota(jnp.int32, (DEPTH, 2 * EDGE), 1) < EDGE
            for group in range(NZH):
                for place in range(NZL):
                    low, high = wbuf[place, group, rows, :MAIN], wbuf[place, group, rows, MAIN : 2 * MAIN]
                    cut = slice(place * MAIN, (place + 1) * MAIN)
                    wch[group, rows, cut] = jnp.where(expert == 1, high, low)
                    dstage[index, group, :, cut] = jnp.where(expert_beside == 1, high, low)
                edges = [wbuf[place, group, rows, 2 * MAIN :].astype(F32) for place in range(NZL)]
                low = jnp.where(left, edges[0], edges[1]).astype(BF16)
                high = jnp.where(left, edges[1], edges[0]).astype(BF16)
                wch[group, rows, 2 * MAIN :] = jnp.where(expert == 1, high, low)
                dstage[index, group, :, 2 * MAIN :] = jnp.where(expert_beside == 1, high, low)
            send(dstage.at[index], wch.at[:, rows, :], ds_sem.at[index], dr_sem.at[index], sibling)

        def head_rows(stream, j):
            rows = qkv[stream, :, :, :, j * HEAD_DIM : (j + 1) * HEAD_DIM].astype(F32)
            return rows.reshape(SEQ, HEAD_DIM).astype(BF16)

        def attend(j, half, keys, values):
            first = half * (NY // 2)
            query = qkv[0, zl, pl.ds(first, NY // 2), :, j * HEAD_DIM : (j + 1) * HEAD_DIM]
            query = query.astype(F32).reshape(QUART, HEAD_DIM).astype(BF16)
            scores = lax.dot_general(query, keys, (((1,), (1,)), ((), ())), preferred_element_type=F32)
            scores = scores + bias_ref[...]
            top = jnp.max(scores, axis=1, keepdims=True)
            probs = jnp.exp2((scores - top) * SCALE)
            total = jnp.sum(probs, axis=1, keepdims=True)
            summed = jnp.dot(probs.astype(BF16), values, preferred_element_type=F32)
            attm[y, half * QUART : (half + 1) * QUART, j * HEAD_DIM : (j + 1) * HEAD_DIM] = (summed / total).astype(BF16)

        def kinds(count):
            return (0, 1, 2, 3) if count == 3 else (0, 2, 3)

        def last_kinds(direction, count):
            return ((0, 2), (1, 3))[direction] if count == 3 else ((0,), (2, 3))[direction]

        def region(yy, kind, count):
            if kind < 2:
                return attm.at[yy, :, pl.ds(kind * HEAD_DIM, HEAD_DIM)]
            return attm.at[yy, pl.ds((kind - 2) * QUART, QUART), pl.ds((count - 1) * HEAD_DIM, HEAD_DIM)]

        def ring_send(t, direction, kind, yy):
            block = region(yy, kind, heads(t - 1))
            sems = gs_sem.at[direction, t - 1, kind], gr_sem.at[direction, t - 1, kind]
            send(block, block, *sems, (y_next, y_prev)[direction])

        def ring_start(kind):
            for direction in range(2):
                ring_send(1, direction, kind, y)

        def ring_wait(t, direction, kind):
            yy = mod(y - t if direction == 0 else y + t, NY)
            wait(region(yy, kind, heads(t)), gr_sem.at[direction, t - 1, kind])
            return yy

        def ring_tick(t, kind):
            if kind not in kinds(heads(t)):
                return
            for direction in range(2):
                yy = ring_wait(t, direction, kind)
                if t < NY // 2 - 1 or kind in last_kinds(direction, heads(t)):
                    ring_send(t + 1, direction, kind, yy)

        def project(yy, count, part, rows=slice(0, HALF), fresh=False):
            first = 0 if count == 3 else 3 * HEAD_DIM
            if part == EDGES:
                cut, total = pl.ds(2 * MAIN, 2 * EDGE), edge
            else:
                cut, total = pl.ds(pl.multiple_of((zl if part == OWN else 1 - zl) * MAIN, MAIN), MAIN), acc.at[part]
            weight = wch[yy // 2, first : first + count * HEAD_DIM, cut]
            made = jnp.dot(attm[yy, rows, : count * HEAD_DIM], weight, preferred_element_type=F32)
            if fresh:
                total[rows] = made
            else:
                total[rows] += made

        def project_two(first, step, *parts):
            def one(i, _):
                for part in parts:
                    project(mod(y + first + step * i, NY), heads(first), part)
                return 0

            lax.fori_loop(0, 2, one, 0)

        order = (4, 3, 5, 2, 6, 1, 7)
        send(own_w, own_w, zs_sem.at[0, 0], zr_sem.at[1], z_next)
        send(own_w, own_w, zs_sem.at[1, 0], zr_sem.at[NZ - 1], z_prev)
        for j in range(3):
            wait(pre.at[j], loc_sem.at[j])
        own_kv(0)
        for d in order:
            a2a(d, 0)
        send(own_w, own_w, xs_sem.at[0, 0], xr_sem.at[0, 0], x_next)
        send(own_w, own_w, xs_sem.at[1, 0], xr_sem.at[1, 0], x_prev)
        start = pl.multiple_of(((y // 2) * 5 + (0 if n == 3 else 3)) * HEAD_DIM, HEAD_DIM)
        own_block = qkv.at[:, zl, y, :, pl.ds(0, n * HEAD_DIM)]
        pltpu.make_async_copy(pre.at[:, :, pl.ds(start, n * HEAD_DIM)], own_block, loc_sem.at[5]).start()
        tables()
        own_kv(1)
        for d in order[:3]:
            a2a(d, 1)
        z_tick(1)
        z_tick(7)
        for d in order[:3]:
            kv_tick(d, 0)
        for d in order[3:]:
            a2a(d, 1)
        z_tick(2)
        z_tick(6)
        for d in order[3:]:
            kv_tick(d, 0)
        z_tick(3)
        z_tick(5)

        wait(own_block, loc_sem.at[5])
        kv_done(0)
        for j in range(n - 1):
            keys, values = head_rows(1, j), head_rows(2, j)
            for half in range(2):
                attend(j, half, keys, values)
            ring_start(j)
            for d in order[:2] if j == 0 else order[2:4]:
                kv_tick(d, 1)
            if j == 0:
                z_tick(4)
                x_tick(0)
                x_tick(1)
                x_tick(7)
        for d in order[2 * (n - 1) :]:
            kv_tick(d, 1)
        x_tick(2)
        x_tick(6)
        ring_tick(1, 0)
        die_push(x, 0)

        kv_done(1)
        keys, values = head_rows(1, n - 1), head_rows(2, n - 1)
        attend(n - 1, 0, keys, values)
        ring_start(2)
        ring_tick(1, 1)
        attend(n - 1, 1, keys, values)
        ring_start(3)
        ring_tick(2, 0)
        x_tick(3)
        x_tick(5)
        ring_tick(2, 1)
        ring_tick(1, 2)
        ring_tick(1, 3)
        x_tick(4)
        for phase in range(2):
            for d in range(1, NY):
                wait(qkv.at[:, zl, y, :, lanes(phase, heads(d))], as_sem.at[phase, d])
            for source in range(NY):
                wait(qkv.at[pl.ds(1, 2), zl, source, :, lanes(phase, n)], ks_sem.at[phase, source])
        die_push(mod(x - 1, NX), 1)
        die_push(mod(x + 1, NX), 2)
        ring_tick(3, 0)
        ring_tick(2, 2)
        ring_tick(2, 3)
        ring_tick(3, 1)
        far = mod(x + 2, NX)
        for d in range(NZ):
            wait(wslot(mod(z - d, NZ), far), rr_sem.at[d])
        die_push(far, 3)
        ring_tick(3, 2)
        ring_tick(3, 3)
        for index, xx in enumerate((x, mod(x - 1, NX), mod(x + 1, NX), far)):
            wait(wch.at[:, pl.ds((xx * 2 + 1 - c) * DEPTH, DEPTH), :], dr_sem.at[index])
        project(y, n, OTHER, fresh=True)
        project(y, n, EDGES, fresh=True)
        project_two(1, 6, OTHER, EDGES)
        project_two(2, 4, OTHER, EDGES)
        project_two(3, 2, OTHER, EDGES)
        project(y, n, OWN, fresh=True)

        last = mod(y + NY // 2, NY)
        turned = lax.rem(expert_ref[rep] + zl, 2) * EDGE
        left = lax.broadcasted_iota(jnp.int32, (QUART // 2, 2 * EDGE), 1) < EDGE
        for half in range(2):
            for kind in ((0, 1, 2) if n == 3 else (0, 2)) if half == 0 else (3,):
                ring_wait(NY // 2, 0 if kind in last_kinds(0, n) else 1, kind)
            rows = slice(half * QUART, (half + 1) * QUART)
            project(last, n, OTHER, rows)
            psend[rows] = acc[OTHER, rows].astype(BF16)
            send(psend.at[rows], precv.at[rows], os_sem.at[0, half], or_sem.at[0, half], partner)
            project(last, n, EDGES, rows)
            top = edge[half * QUART : half * QUART + QUART // 2]
            low = edge[half * QUART + QUART // 2 : (half + 1) * QUART]
            both = jnp.where(left, pltpu.roll(top, EDGE - turned, 1), pltpu.roll(low, turned, 1))
            esend[half] = both.astype(BF16)
            send(esend.at[half], erecv.at[half], os_sem.at[1, half], or_sem.at[1, half], partner)
        project_two(1, 6, OWN)
        project_two(2, 4, OWN)
        project_two(3, 2, OWN)
        project(last, n, OWN)

        for t in range(1, NY // 2 + 1):
            for direction in range(2):
                for kind in kinds(heads(t - 1)) if t < NY // 2 else last_kinds(direction, heads(t - 1)):
                    wait(region(y, kind, heads(t - 1)), gs_sem.at[direction, t - 1, kind])

    pl.when(lax.rem(y, 2) == 0)(lambda: run(3))
    pl.when(lax.rem(y, 2) == 1)(lambda: run(2))

    for d in (0, 1, 2, 3):
        wait(own_w, zs_sem.at[0, d])
    for d in (0, 7, 6):
        wait(own_w, zs_sem.at[1, d])
    for d in range(NZ):
        wait(own_w, xs_sem.at[0, d])
        wait(own_w, xs_sem.at[1, d])
        wait(own_w, rs_sem.at[d])
    for index in range(NX):
        wait(dstage.at[index], ds_sem.at[index])
    wait(resv, loc_sem.at[4])
    turned = lax.rem(expert_ref[rep] + zl, 2) * EDGE
    for block in range(NY):
        rows, place = slice(block * ROWS, (block + 1) * ROWS), pl.ds((block * NZL + zl) * ROWS, ROWS)
        nat[place, :MAIN] = acc[OWN, rows]
        nat[place, MAIN:] = pltpu.roll(edge[rows], turned, 1)
    main_at = pl.ds(pl.multiple_of(zl * EDGE, EDGE), MAIN)
    edge_at = pl.ds(pl.multiple_of((1 - zl) * MAIN, EDGE), EDGE)
    for half in range(2):
        rows = slice(half * QUART, (half + 1) * QUART)
        wait(precv.at[rows], or_sem.at[0, half])
        wait(erecv.at[half], or_sem.at[1, half])
        acc[OTHER, rows] = precv[rows].astype(F32)
        both = erecv[half].astype(F32)
        edge[half * QUART : half * QUART + QUART // 2] = both
        edge[half * QUART + QUART // 2 : (half + 1) * QUART] = pltpu.roll(both, EDGE, 1)
        for block in range(half * NY // 2, (half + 1) * NY // 2):
            rows, place = slice(block * ROWS, (block + 1) * ROWS), pl.ds((block * NZL + 1 - zl) * ROWS, ROWS)
            nat[place, :MAIN] = acc[OTHER, rows]
            nat[place, MAIN:] = edge[rows]
        for block in ((0, 1, 2), (3, 4, 5, 6))[half]:
            tokens = slice(block * 128, (block + 1) * 128)
            made = nat[tokens, :].T
            for at, part in ((main_at, made[:MAIN]), (edge_at, made[MAIN : MAIN + EDGE])):
                mixed = resv[0, at, tokens].astype(F32) + gate_ref[at, :] * part
                out_ref[0, at, tokens] = mixed.astype(BF16)
    for half in range(2):
        wait(psend.at[half * QUART : (half + 1) * QUART], os_sem.at[0, half])
        wait(esend.at[half], os_sem.at[1, half])


def local(queries, keys, values, residual, wo_values, wo_exponents, modulation, expert_choice, step_index, lengths):
    offset = np.arange(D) % (D // 2)
    freq = np.exp(-math.log(10000.0) * offset / (D // 2)).astype(np.float32).reshape(D // COLS, 1, COLS)
    hbm = pl.BlockSpec(memory_space=pl.ANY)
    vmem = pl.BlockSpec(memory_space=pltpu.VMEM)
    dma = pltpu.SemaphoreType.DMA
    mixed = pl.pallas_call(
        kernel,
        out_shape=pltpu.VMEM((1, COLS, SEQ), BF16),
        in_specs=[hbm] * 11,
        out_specs=vmem,
        scratch_shapes=[
            pltpu.VMEM((HEADS, 2, D // 128), jnp.int32),
            pltpu.VMEM((2, COLS), F32),
            pltpu.VMEM((1, COLS), F32),
            pltpu.SMEM((CLIPS,), jnp.int32),
            pltpu.SMEM((CLIPS,), jnp.int32),
            pltpu.SMEM((CLIPS,), jnp.int32),
            pltpu.VMEM((3, ROWS, HEADS * HEAD_DIM), BF16),
            pltpu.VMEM((3, NZL, NY, ROWS, 3 * HEAD_DIM), BF16),
            pltpu.VMEM((NZL, NZH, 2 * NX * DEPTH, PACK), BF16),
            pltpu.VMEM((2, DEPTH, COLS), BF16),
            pltpu.VMEM((NZH, 2 * NX * DEPTH, PACK), BF16),
            pltpu.VMEM((NX, NZH, DEPTH, PACK), BF16),
            pltpu.VMEM((NY, HALF, 3 * HEAD_DIM), BF16),
            pltpu.VMEM((2, HALF, MAIN), F32),
            pltpu.VMEM((HALF, 2 * EDGE), F32),
            pltpu.VMEM((HALF, MAIN), BF16),
            pltpu.VMEM((HALF, MAIN), BF16),
            pltpu.VMEM((2, QUART // 2, 2 * EDGE), BF16),
            pltpu.VMEM((2, QUART // 2, 2 * EDGE), BF16),
            pltpu.VMEM((1, COLS, SEQ), BF16),
            pltpu.VMEM((SEQ, MAIN + 2 * EDGE), F32),
            pltpu.VMEM((2, HEADS, COLS), F32),
            pltpu.VMEM((1, SEQ), F32),
            pltpu.VMEM((COLS, 128), F32),
            dma((6,)),
            dma((6,)),
            dma((2, NY)),
            dma((2, NY)),
            dma((2, NY)),
            dma((2, NY)),
            dma((2, NZ)),
            dma((NZ,)),
            dma((2, NZ)),
            dma((2, NZ)),
            dma((NZ,)),
            dma((NZ,)),
            dma((NX,)),
            dma((NX,)),
            dma((2, NY // 2, 5)),
            dma((2, NY // 2, 5)),
            dma((2, 2)),
            dma((2, 2)),
        ],
        compiler_params=pltpu.CompilerParams(
            collective_id=0, has_side_effects=True, vmem_limit_bytes=62 * 2**20
        ),
        cost_estimate=pl.CostEstimate(flops=2 * 10**9, bytes_accessed=3 * 10**6, transcendentals=10**6),
    )(
        queries,
        keys,
        values,
        jnp.swapaxes(residual, 1, 2),
        wo_values,
        jnp.swapaxes(wo_exponents, 0, 1),
        modulation,
        jnp.asarray(freq),
        expert_choice,
        step_index,
        lengths,
    )
    return jnp.swapaxes(mixed, 1, 2)


def solution(mesh):
    placed = (
        P("rep", "seq", None),
        P("rep", "seq", None),
        P("rep", "seq", None),
        P("rep", None, "seq"),
        P(None, "rep", "seq"),
        P(),
        P(None, "seq"),
        P(),
        P(),
        P(),
    )
    return jax.shard_map(
        local, mesh=mesh, in_specs=placed, out_specs=P("rep", None, "seq"), check_vma=False
    )
```

```python
import math

import jax
import jax.numpy as jnp
import numpy as np
from jax import lax
from jax.experimental import pallas as pl
from jax.experimental.pallas import tpu as pltpu
from jax.sharding import PartitionSpec as P

D = 5120
HEADS = 20
HEAD_DIM = 128
STEPS = 10
NY = 8
NZL = 2
NX = 4
NZH = 4
NZ = NZL * NZH
ROWS = 56
SEQ = ROWS * NY * NZL
CLIPS = 2 * NX * NZH
HALF = ROWS * NY
QUART = HALF // 2
COLS = 320
MAIN = 256
EDGE = COLS - MAIN
PACK = 2 * COLS
DEPTH = 80
SCALE = HEAD_DIM**-0.5 * math.log2(math.e)

OWN, OTHER, EDGES = 0, 1, 2
MESH = pl.DeviceIdType.MESH
F32 = jnp.float32
BF16 = jnp.bfloat16


def mod(value, size):
    return lax.rem(value + size, size)


def kernel(
    q_ref,
    k_ref,
    v_ref,
    res_ref,
    wo_ref,
    exps_hbm,
    mod_hbm,
    freq_hbm,
    expert_hbm,
    step_hbm,
    len_hbm,
    out_ref,
    exps_ref,
    mod_ref,
    freq_ref,
    expert_ref,
    step_ref,
    len_ref,
    pre,
    qkv,
    wbuf,
    wo_rows,
    wch,
    dstage,
    attm,
    acc,
    edge,
    psend,
    precv,
    esend,
    erecv,
    resv,
    nat,
    stab,
    bias_ref,
    gate_ref,
    loc_sem,
    small_sem,
    as_sem,
    ar_sem,
    ks_sem,
    kr_sem,
    zs_sem,
    zr_sem,
    xs_sem,
    xr_sem,
    rs_sem,
    rr_sem,
    ds_sem,
    dr_sem,
    gs_sem,
    gr_sem,
    os_sem,
    or_sem,
):
    rep = lax.axis_index("rep")
    seq = lax.axis_index("seq")
    c = lax.rem(rep, 2)
    x = lax.rem(rep // 2, NX)
    zh = rep // (2 * NX)
    y = seq // NZL
    zl = lax.rem(seq, NZL)
    z = zh * NZL + zl

    def dev_y(yy):
        return {"rep": rep, "seq": yy * NZL + zl}

    def dev_z(zz):
        return {"rep": (zz // NZL) * (2 * NX) + x * 2 + c, "seq": y * NZL + lax.rem(zz, NZL)}

    def dev_x(xx):
        return {"rep": zh * (2 * NX) + xx * 2 + c, "seq": seq}

    partner = {"rep": rep, "seq": y * NZL + 1 - zl}
    sibling = {"rep": rep + 1 - 2 * c, "seq": seq}
    z_next, z_prev = dev_z(mod(z + 1, NZ)), dev_z(mod(z - 1, NZ))
    x_next, x_prev = dev_x(mod(x + 1, NX)), dev_x(mod(x - 1, NX))
    y_next, y_prev = dev_y(mod(y + 1, NY)), dev_y(mod(y - 1, NY))

    def send(src, dst, ss, rs, dev):
        pltpu.make_async_remote_copy(
            src_ref=src, dst_ref=dst, send_sem=ss, recv_sem=rs, device_id=dev, device_id_type=MESH
        ).start()

    def wait(ref, sem):
        pltpu.make_async_copy(ref, ref, sem).wait()

    def wslot(zz, xx):
        return wbuf.at[lax.rem(zz, NZL), zz // NZL, pl.ds((xx * 2 + c) * DEPTH, DEPTH), :]

    def lanes(phase, n):
        return pl.ds(0, (n - 1) * HEAD_DIM) if phase == 0 else pl.ds((n - 1) * HEAD_DIM, HEAD_DIM)

    def columns(yy, phase, n):
        first = (yy // 2) * 5 + (0 if n == 3 else 3) + phase * (n - 1)
        return pl.ds(pl.multiple_of(first * HEAD_DIM, HEAD_DIM), (n - 1) * HEAD_DIM if phase == 0 else HEAD_DIM)

    small = (
        (exps_hbm, exps_ref),
        (expert_hbm, expert_ref),
        (step_hbm, step_ref),
        (len_hbm, len_ref),
        (mod_hbm, mod_ref),
        (freq_hbm.at[seq], freq_ref),
    )
    pltpu.make_async_copy(wo_ref, wo_rows, loc_sem.at[3]).start()
    for index, (source, target) in enumerate(small):
        pltpu.make_async_copy(source, target, small_sem.at[index]).start()

    barrier = pltpu.get_barrier_semaphore()
    for d in range(1, NY):
        pl.semaphore_signal(barrier, inc=1, device_id=dev_y(mod(y + d, NY)), device_id_type=MESH)
    for dev in (z_next, z_prev, x_next, x_prev, sibling):
        pl.semaphore_signal(barrier, inc=1, device_id=dev, device_id_type=MESH)

    for j, ref in enumerate((q_ref, k_ref, v_ref)):
        pltpu.make_async_copy(ref.at[0], pre.at[j], loc_sem.at[j]).start()
    pltpu.make_async_copy(res_ref, resv, loc_sem.at[4]).start()
    own_w = wslot(z, x)

    pl.semaphore_wait(barrier, 12)

    def pack_own():
        for index, (source, target) in enumerate(small):
            pltpu.make_async_copy(source, target, small_sem.at[index]).wait()
        for choice in range(2):
            powers = (jnp.left_shift(jnp.ones((HEADS, D // 128), jnp.int32), exps_ref[:, choice, :] + 1).astype(F32) * 0.5).astype(BF16)
            column = seq * COLS + lax.broadcasted_iota(jnp.int32, (D // 128, COLS), 1)
            hot = (column // 128 == lax.broadcasted_iota(jnp.int32, (D // 128, COLS), 0)).astype(F32).astype(BF16)
            stab[choice] = jnp.dot(powers, hot, preferred_element_type=F32)
        wait(wo_rows, loc_sem.at[3])
        for choice in range(2):
            for piece in range(DEPTH // 16):
                head = (rep * DEPTH + piece * 16) // HEAD_DIM
                rows = wo_rows[choice, piece * 16 : (piece + 1) * 16, :].astype(F32) * stab[choice, pl.ds(head, 1), :]
                wo_rows[choice, piece * 16 : (piece + 1) * 16, :] = rows.astype(BF16)
        packed = jnp.zeros((DEPTH, PACK), F32)
        origin = lax.broadcasted_iota(jnp.int32, (COLS, PACK), 0)
        lane = lax.broadcasted_iota(jnp.int32, (COLS, PACK), 1)
        for choice in range(2):
            low = jnp.where(origin < MAIN, choice * MAIN + origin, 2 * MAIN + choice * EDGE + origin - MAIN)
            high = jnp.where(origin < EDGE, 2 * MAIN + (1 - choice) * EDGE + origin, choice * MAIN + origin - EDGE)
            hot = (lane == jnp.where(zl == 0, low, high)).astype(F32).astype(BF16)
            packed += jnp.dot(wo_rows[choice], hot, preferred_element_type=F32)
        wbuf[zl, zh, pl.ds(pl.multiple_of((x * 2 + c) * DEPTH, 16), DEPTH), :] = packed.astype(BF16)

    def tables():
        flat = lax.broadcasted_iota(jnp.int32, (1, SEQ), 1)
        upper = (flat >= HALF).astype(jnp.int32)
        within = flat - upper * HALF
        source = sum((within >= ROWS * m).astype(jnp.int32) for m in range(1, NY))
        position = within + (source + upper) * ROWS
        bias_ref[...] = jnp.where(position < len_ref[rep], 0.0, -1e30)
        angle = 1000.0 * (1.0 - step_ref[rep].astype(F32) / STEPS) * freq_ref[...]
        feature = jnp.where(seq < NY * NZL // 2, jnp.cos(angle), jnp.sin(angle))
        gate = mod_ref[pl.ds(expert_ref[rep], 1), :] + feature
        gate_ref[...] = jnp.broadcast_to(gate, (128, COLS)).T

    def run(n):
        def heads(d):
            return n if d % 2 == 0 else 5 - n

        def a2a(d, phase):
            to = mod(y + d, NY)
            cut = lanes(phase, heads(d))
            source = pre.at[:, :, columns(to, phase, heads(d))]
            send(source, qkv.at[:, zl, y, :, cut], as_sem.at[phase, d], ar_sem.at[phase, d], dev_y(to))

        def own_kv(phase):
            source = pre.at[pl.ds(1, 2), :, columns(y, phase, n)]
            target = qkv.at[pl.ds(1, 2), zl, y, :, lanes(phase, n)]
            send(source, target, ks_sem.at[phase, y], kr_sem.at[phase, y], partner)

        def kv_tick(d, phase):
            source = mod(y - d, NY)
            wait(qkv.at[:, zl, source, :, lanes(phase, n)], ar_sem.at[phase, d])
            block = qkv.at[pl.ds(1, 2), zl, source, :, lanes(phase, n)]
            send(block, block, ks_sem.at[phase, source], kr_sem.at[phase, source], partner)

        def kv_done(phase):
            for source in range(NY):
                wait(qkv.at[pl.ds(1, 2), 1 - zl, source, :, lanes(phase, n)], kr_sem.at[phase, source])

        def z_tick(d):
            block = wslot(mod(z - d, NZ), x)
            wait(block, zr_sem.at[d])
            if d < NZ // 2:
                send(block, block, zs_sem.at[0, d], zr_sem.at[d + 1], z_next)
            elif d > NZ // 2 + 1:
                send(block, block, zs_sem.at[1, d], zr_sem.at[d - 1], z_prev)
            send(block, block, xs_sem.at[0, d], xr_sem.at[0, d], x_next)
            send(block, block, xs_sem.at[1, d], xr_sem.at[1, d], x_prev)

        def x_tick(d):
            zz = mod(z - d, NZ)
            left, right = wslot(zz, mod(x - 1, NX)), wslot(zz, mod(x + 1, NX))
            wait(left, xr_sem.at[0, d])
            wait(right, xr_sem.at[1, d])
            if d < NZ // 2:
                send(left, left, rs_sem.at[d], rr_sem.at[d], x_next)
            else:
                send(right, right, rs_sem.at[d], rr_sem.at[d], x_prev)

        def die_push(xx, index):
            rows = pl.ds(pl.multiple_of((xx * 2 + c) * DEPTH, 16), DEPTH)
            expert, expert_beside = expert_ref[rep], expert_ref[rep + 1 - 2 * c]
            left = lax.broadcasted_iota(jnp.int32, (DEPTH, 2 * EDGE), 1) < EDGE
            for group in range(NZH):
                for place in range(NZL):
                    low, high = wbuf[place, group, rows, :MAIN], wbuf[place, group, rows, MAIN : 2 * MAIN]
                    cut = slice(place * MAIN, (place + 1) * MAIN)
                    wch[group, rows, cut] = jnp.where(expert == 1, high, low)
                    dstage[index, group, :, cut] = jnp.where(expert_beside == 1, high, low)
                edges = [wbuf[place, group, rows, 2 * MAIN :].astype(F32) for place in range(NZL)]
                low = jnp.where(left, edges[0], edges[1]).astype(BF16)
                high = jnp.where(left, edges[1], edges[0]).astype(BF16)
                wch[group, rows, 2 * MAIN :] = jnp.where(expert == 1, high, low)
                dstage[index, group, :, 2 * MAIN :] = jnp.where(expert_beside == 1, high, low)
            send(dstage.at[index], wch.at[:, rows, :], ds_sem.at[index], dr_sem.at[index], sibling)

        def head_rows(stream, j):
            rows = qkv[stream, :, :, :, j * HEAD_DIM : (j + 1) * HEAD_DIM].astype(F32)
            return rows.reshape(SEQ, HEAD_DIM).astype(BF16)

        def attend(j, half, keys, values):
            first = half * (NY // 2)
            query = qkv[0, zl, pl.ds(first, NY // 2), :, j * HEAD_DIM : (j + 1) * HEAD_DIM]
            query = query.astype(F32).reshape(QUART, HEAD_DIM).astype(BF16)
            scores = lax.dot_general(query, keys, (((1,), (1,)), ((), ())), preferred_element_type=F32)
            scores = scores + bias_ref[...]
            top = jnp.max(scores, axis=1, keepdims=True)
            probs = jnp.exp2((scores - top) * SCALE)
            total = jnp.sum(probs, axis=1, keepdims=True)
            summed = jnp.dot(probs.astype(BF16), values, preferred_element_type=F32)
            attm[y, half * QUART : (half + 1) * QUART, j * HEAD_DIM : (j + 1) * HEAD_DIM] = (summed / total).astype(BF16)

        def kinds(count):
            return (0, 1, 2, 3) if count == 3 else (0, 2, 3)

        def last_kinds(direction, count):
            return ((0, 2), (1, 3))[direction] if count == 3 else ((0,), (2, 3))[direction]

        def region(yy, kind, count):
            if kind < 2:
                return attm.at[yy, :, pl.ds(kind * HEAD_DIM, HEAD_DIM)]
            return attm.at[yy, pl.ds((kind - 2) * QUART, QUART), pl.ds((count - 1) * HEAD_DIM, HEAD_DIM)]

        def ring_send(t, direction, kind, yy):
            block = region(yy, kind, heads(t - 1))
            sems = gs_sem.at[direction, t - 1, kind], gr_sem.at[direction, t - 1, kind]
            send(block, block, *sems, (y_next, y_prev)[direction])

        def ring_start(kind):
            for direction in range(2):
                ring_send(1, direction, kind, y)

        def ring_wait(t, direction, kind):
            yy = mod(y - t if direction == 0 else y + t, NY)
            wait(region(yy, kind, heads(t)), gr_sem.at[direction, t - 1, kind])
            return yy

        def ring_tick(t, kind):
            if kind not in kinds(heads(t)):
                return
            for direction in range(2):
                yy = ring_wait(t, direction, kind)
                if t < NY // 2 - 1 or kind in last_kinds(direction, heads(t)):
                    ring_send(t + 1, direction, kind, yy)

        def project(yy, count, part, rows=slice(0, HALF), fresh=False):
            first = 0 if count == 3 else 3 * HEAD_DIM
            if part == EDGES:
                cut, total = pl.ds(2 * MAIN, 2 * EDGE), edge
            else:
                cut, total = pl.ds(pl.multiple_of((zl if part == OWN else 1 - zl) * MAIN, MAIN), MAIN), acc.at[part]
            weight = wch[yy // 2, first : first + count * HEAD_DIM, cut]
            made = jnp.dot(attm[yy, rows, : count * HEAD_DIM], weight, preferred_element_type=F32)
            if fresh:
                total[rows] = made
            else:
                total[rows] += made

        def project_two(first, step, *parts):
            def one(i, _):
                for part in parts:
                    project(mod(y + first + step * i, NY), heads(first), part)
                return 0

            lax.fori_loop(0, 2, one, 0)

        order = (4, 3, 5, 2, 6, 1, 7)
        for j in range(3):
            wait(pre.at[j], loc_sem.at[j])
        own_kv(0)
        for d in order:
            a2a(d, 0)
        pack_own()
        send(own_w, own_w, zs_sem.at[0, 0], zr_sem.at[1], z_next)
        send(own_w, own_w, zs_sem.at[1, 0], zr_sem.at[NZ - 1], z_prev)
        send(own_w, own_w, xs_sem.at[0, 0], xr_sem.at[0, 0], x_next)
        send(own_w, own_w, xs_sem.at[1, 0], xr_sem.at[1, 0], x_prev)
        start = pl.multiple_of(((y // 2) * 5 + (0 if n == 3 else 3)) * HEAD_DIM, HEAD_DIM)
        own_block = qkv.at[:, zl, y, :, pl.ds(0, n * HEAD_DIM)]
        pltpu.make_async_copy(pre.at[:, :, pl.ds(start, n * HEAD_DIM)], own_block, loc_sem.at[5]).start()
        tables()
        own_kv(1)
        for d in order[:3]:
            a2a(d, 1)
        z_tick(1)
        z_tick(7)
        for d in order[:3]:
            kv_tick(d, 0)
        for d in order[3:]:
            a2a(d, 1)
        z_tick(2)
        z_tick(6)
        for d in order[3:]:
            kv_tick(d, 0)
        z_tick(3)
        z_tick(5)

        wait(own_block, loc_sem.at[5])
        kv_done(0)
        for j in range(n - 1):
            keys, values = head_rows(1, j), head_rows(2, j)
            for half in range(2):
                attend(j, half, keys, values)
            ring_start(j)
            for d in order[:2] if j == 0 else order[2:4]:
                kv_tick(d, 1)
            if j == 0:
                z_tick(4)
                x_tick(0)
                x_tick(1)
                x_tick(7)
        for d in order[2 * (n - 1) :]:
            kv_tick(d, 1)
        x_tick(2)
        x_tick(6)
        ring_tick(1, 0)
        die_push(x, 0)

        kv_done(1)
        keys, values = head_rows(1, n - 1), head_rows(2, n - 1)
        attend(n - 1, 0, keys, values)
        ring_start(2)
        ring_tick(1, 1)
        attend(n - 1, 1, keys, values)
        ring_start(3)
        ring_tick(2, 0)
        x_tick(3)
        x_tick(5)
        ring_tick(2, 1)
        ring_tick(1, 2)
        x_tick(4)
        ring_tick(1, 3)
        ring_tick(3, 0)
        ring_tick(3, 1)
        die_push(mod(x - 1, NX), 1)
        die_push(mod(x + 1, NX), 2)
        ring_tick(2, 2)
        ring_tick(2, 3)
        far = mod(x + 2, NX)
        for d in range(NZ):
            wait(wslot(mod(z - d, NZ), far), rr_sem.at[d])
        die_push(far, 3)
        for phase in range(2):
            for d in range(1, NY):
                wait(qkv.at[:, zl, y, :, lanes(phase, heads(d))], as_sem.at[phase, d])
            for source in range(NY):
                wait(qkv.at[pl.ds(1, 2), zl, source, :, lanes(phase, n)], ks_sem.at[phase, source])
        ring_tick(3, 2)
        ring_tick(3, 3)
        for index, xx in enumerate((x, mod(x - 1, NX), mod(x + 1, NX), far)):
            wait(wch.at[:, pl.ds((xx * 2 + 1 - c) * DEPTH, DEPTH), :], dr_sem.at[index])
        project(y, n, OTHER, fresh=True)
        project(y, n, EDGES, fresh=True)
        project_two(1, 6, OTHER, EDGES)
        project_two(2, 4, OTHER, EDGES)
        project_two(3, 2, OTHER, EDGES)
        project(y, n, OWN, fresh=True)

        last = mod(y + NY // 2, NY)
        turned = lax.rem(expert_ref[rep] + zl, 2) * EDGE
        left = lax.broadcasted_iota(jnp.int32, (QUART // 2, 2 * EDGE), 1) < EDGE
        for half in range(2):
            for kind in ((0, 1, 2) if n == 3 else (0, 2)) if half == 0 else (3,):
                ring_wait(NY // 2, 0 if kind in last_kinds(0, n) else 1, kind)
            rows = slice(half * QUART, (half + 1) * QUART)
            project(last, n, OTHER, rows)
            psend[rows] = acc[OTHER, rows].astype(BF16)
            send(psend.at[rows], precv.at[rows], os_sem.at[0, half], or_sem.at[0, half], partner)
            project(last, n, EDGES, rows)
            top = edge[half * QUART : half * QUART + QUART // 2]
            low = edge[half * QUART + QUART // 2 : (half + 1) * QUART]
            both = jnp.where(left, pltpu.roll(top, EDGE - turned, 1), pltpu.roll(low, turned, 1))
            esend[half] = both.astype(BF16)
            send(esend.at[half], erecv.at[half], os_sem.at[1, half], or_sem.at[1, half], partner)
        project_two(1, 6, OWN)
        project_two(2, 4, OWN)
        project_two(3, 2, OWN)
        project(last, n, OWN)

        for t in range(1, NY // 2 + 1):
            for direction in range(2):
                for kind in kinds(heads(t - 1)) if t < NY // 2 else last_kinds(direction, heads(t - 1)):
                    wait(region(y, kind, heads(t - 1)), gs_sem.at[direction, t - 1, kind])

    pl.when(lax.rem(y, 2) == 0)(lambda: run(3))
    pl.when(lax.rem(y, 2) == 1)(lambda: run(2))

    for d in (0, 1, 2, 3):
        wait(own_w, zs_sem.at[0, d])
    for d in (0, 7, 6):
        wait(own_w, zs_sem.at[1, d])
    for d in range(NZ):
        wait(own_w, xs_sem.at[0, d])
        wait(own_w, xs_sem.at[1, d])
        wait(own_w, rs_sem.at[d])
    for index in range(NX):
        wait(dstage.at[index], ds_sem.at[index])
    wait(resv, loc_sem.at[4])
    turned = lax.rem(expert_ref[rep] + zl, 2) * EDGE
    for block in range(NY):
        rows, place = slice(block * ROWS, (block + 1) * ROWS), pl.ds((block * NZL + zl) * ROWS, ROWS)
        nat[place, :MAIN] = acc[OWN, rows]
        nat[place, MAIN:] = pltpu.roll(edge[rows], turned, 1)
    main_at = pl.ds(pl.multiple_of(zl * EDGE, EDGE), MAIN)
    edge_at = pl.ds(pl.multiple_of((1 - zl) * MAIN, EDGE), EDGE)
    for half in range(2):
        rows = slice(half * QUART, (half + 1) * QUART)
        wait(precv.at[rows], or_sem.at[0, half])
        wait(erecv.at[half], or_sem.at[1, half])
        acc[OTHER, rows] = precv[rows].astype(F32)
        both = erecv[half].astype(F32)
        edge[half * QUART : half * QUART + QUART // 2] = both
        edge[half * QUART + QUART // 2 : (half + 1) * QUART] = pltpu.roll(both, EDGE, 1)
        for block in range(half * NY // 2, (half + 1) * NY // 2):
            rows, place = slice(block * ROWS, (block + 1) * ROWS), pl.ds((block * NZL + 1 - zl) * ROWS, ROWS)
            nat[place, :MAIN] = acc[OTHER, rows]
            nat[place, MAIN:] = edge[rows]
        for block in ((0, 1, 2), (3, 4, 5, 6))[half]:
            tokens = slice(block * 128, (block + 1) * 128)
            made = nat[tokens, :].T
            for at, part in ((main_at, made[:MAIN]), (edge_at, made[MAIN : MAIN + EDGE])):
                mixed = resv[0, at, tokens].astype(F32) + gate_ref[at, :] * part
                out_ref[0, at, tokens] = mixed.astype(BF16)
    for half in range(2):
        wait(psend.at[half * QUART : (half + 1) * QUART], os_sem.at[0, half])
        wait(esend.at[half], os_sem.at[1, half])


def local(queries, keys, values, residual, wo_values, wo_exponents, modulation, expert_choice, step_index, lengths):
    offset = np.arange(D) % (D // 2)
    freq = np.exp(-math.log(10000.0) * offset / (D // 2)).astype(np.float32).reshape(D // COLS, 1, COLS)
    hbm = pl.BlockSpec(memory_space=pl.ANY)
    vmem = pl.BlockSpec(memory_space=pltpu.VMEM)
    dma = pltpu.SemaphoreType.DMA
    mixed = pl.pallas_call(
        kernel,
        out_shape=pltpu.VMEM((1, COLS, SEQ), BF16),
        in_specs=[hbm] * 11,
        out_specs=vmem,
        scratch_shapes=[
            pltpu.VMEM((HEADS, 2, D // 128), jnp.int32),
            pltpu.VMEM((2, COLS), F32),
            pltpu.VMEM((1, COLS), F32),
            pltpu.SMEM((CLIPS,), jnp.int32),
            pltpu.SMEM((CLIPS,), jnp.int32),
            pltpu.SMEM((CLIPS,), jnp.int32),
            pltpu.VMEM((3, ROWS, HEADS * HEAD_DIM), BF16),
            pltpu.VMEM((3, NZL, NY, ROWS, 3 * HEAD_DIM), BF16),
            pltpu.VMEM((NZL, NZH, 2 * NX * DEPTH, PACK), BF16),
            pltpu.VMEM((2, DEPTH, COLS), BF16),
            pltpu.VMEM((NZH, 2 * NX * DEPTH, PACK), BF16),
            pltpu.VMEM((NX, NZH, DEPTH, PACK), BF16),
            pltpu.VMEM((NY, HALF, 3 * HEAD_DIM), BF16),
            pltpu.VMEM((2, HALF, MAIN), F32),
            pltpu.VMEM((HALF, 2 * EDGE), F32),
            pltpu.VMEM((HALF, MAIN), BF16),
            pltpu.VMEM((HALF, MAIN), BF16),
            pltpu.VMEM((2, QUART // 2, 2 * EDGE), BF16),
            pltpu.VMEM((2, QUART // 2, 2 * EDGE), BF16),
            pltpu.VMEM((1, COLS, SEQ), BF16),
            pltpu.VMEM((SEQ, MAIN + 2 * EDGE), F32),
            pltpu.VMEM((2, HEADS, COLS), F32),
            pltpu.VMEM((1, SEQ), F32),
            pltpu.VMEM((COLS, 128), F32),
            dma((6,)),
            dma((6,)),
            dma((2, NY)),
            dma((2, NY)),
            dma((2, NY)),
            dma((2, NY)),
            dma((2, NZ)),
            dma((NZ,)),
            dma((2, NZ)),
            dma((2, NZ)),
            dma((NZ,)),
            dma((NZ,)),
            dma((NX,)),
            dma((NX,)),
            dma((2, NY // 2, 5)),
            dma((2, NY // 2, 5)),
            dma((2, 2)),
            dma((2, 2)),
        ],
        compiler_params=pltpu.CompilerParams(
            collective_id=0, has_side_effects=True, vmem_limit_bytes=62 * 2**20
        ),
        cost_estimate=pl.CostEstimate(flops=2 * 10**9, bytes_accessed=3 * 10**6, transcendentals=10**6),
    )(
        queries,
        keys,
        values,
        jnp.swapaxes(residual, 1, 2),
        wo_values,
        jnp.swapaxes(wo_exponents, 0, 1),
        modulation,
        jnp.asarray(freq),
        expert_choice,
        step_index,
        lengths,
    )
    return jnp.swapaxes(mixed, 1, 2)


def solution(mesh):
    placed = (
        P("rep", "seq", None),
        P("rep", "seq", None),
        P("rep", "seq", None),
        P("rep", None, "seq"),
        P(None, "rep", "seq"),
        P(),
        P(None, "seq"),
        P(),
        P(),
        P(),
    )
    return jax.shard_map(
        local, mesh=mesh, in_specs=placed, out_specs=P("rep", None, "seq"), check_vma=False
    )
```

```python
import math

import jax
import jax.numpy as jnp
import numpy as np
from jax import lax
from jax.experimental import pallas as pl
from jax.experimental.pallas import tpu as pltpu
from jax.sharding import PartitionSpec as P

D = 5120
HEADS = 20
HEAD_DIM = 128
STEPS = 10
NY = 8
NZL = 2
NX = 4
NZH = 4
NZ = NZL * NZH
ROWS = 56
SEQ = ROWS * NY * NZL
CLIPS = 2 * NX * NZH
HALF = ROWS * NY
QUART = HALF // 2
COLS = 320
MAIN = 256
EDGE = COLS - MAIN
PACK = 2 * COLS
DEPTH = 80
SCALE = HEAD_DIM**-0.5 * math.log2(math.e)

OWN, OTHER, EDGES = 0, 1, 2
MESH = pl.DeviceIdType.MESH
F32 = jnp.float32
BF16 = jnp.bfloat16


def mod(value, size):
    return lax.rem(value + size, size)


def kernel(
    q_ref,
    k_ref,
    v_ref,
    res_ref,
    wo_ref,
    exps_hbm,
    mod_hbm,
    freq_hbm,
    expert_hbm,
    step_hbm,
    len_hbm,
    out_ref,
    exps_ref,
    mod_ref,
    freq_ref,
    expert_ref,
    step_ref,
    len_ref,
    pre,
    qkv,
    stage,
    wbuf,
    wo_rows,
    wch,
    dstage,
    attm,
    acc,
    edge,
    psend,
    precv,
    esend,
    erecv,
    resv,
    nat,
    stab,
    bias_ref,
    gate_ref,
    loc_sem,
    small_sem,
    as_sem,
    ar_sem,
    sr_sem,
    fs_sem,
    ks_sem,
    kr_sem,
    zs_sem,
    zr_sem,
    xs_sem,
    xr_sem,
    rs_sem,
    rr_sem,
    ds_sem,
    dr_sem,
    gs_sem,
    gr_sem,
    os_sem,
    or_sem,
):
    rep = lax.axis_index("rep")
    seq = lax.axis_index("seq")
    c = lax.rem(rep, 2)
    x = lax.rem(rep // 2, NX)
    zh = rep // (2 * NX)
    y = seq // NZL
    zl = lax.rem(seq, NZL)
    z = zh * NZL + zl

    def dev_y(yy):
        return {"rep": rep, "seq": yy * NZL + zl}

    def dev_z(zz):
        return {"rep": (zz // NZL) * (2 * NX) + x * 2 + c, "seq": y * NZL + lax.rem(zz, NZL)}

    def dev_x(xx):
        return {"rep": zh * (2 * NX) + xx * 2 + c, "seq": seq}

    partner = {"rep": rep, "seq": y * NZL + 1 - zl}
    sibling = {"rep": rep + 1 - 2 * c, "seq": seq}
    z_next, z_prev = dev_z(mod(z + 1, NZ)), dev_z(mod(z - 1, NZ))
    x_next, x_prev = dev_x(mod(x + 1, NX)), dev_x(mod(x - 1, NX))
    y_next, y_prev = dev_y(mod(y + 1, NY)), dev_y(mod(y - 1, NY))

    def send(src, dst, ss, rs, dev):
        pltpu.make_async_remote_copy(
            src_ref=src, dst_ref=dst, send_sem=ss, recv_sem=rs, device_id=dev, device_id_type=MESH
        ).start()

    def wait(ref, sem):
        pltpu.make_async_copy(ref, ref, sem).wait()

    def wslot(zz, xx):
        return wbuf.at[lax.rem(zz, NZL), zz // NZL, pl.ds((xx * 2 + c) * DEPTH, DEPTH), :]

    def lanes(phase, n):
        return pl.ds(0, (n - 1) * HEAD_DIM) if phase == 0 else pl.ds((n - 1) * HEAD_DIM, HEAD_DIM)

    def columns(yy, phase, n):
        first = (yy // 2) * 5 + (0 if n == 3 else 3) + phase * (n - 1)
        return pl.ds(pl.multiple_of(first * HEAD_DIM, HEAD_DIM), (n - 1) * HEAD_DIM if phase == 0 else HEAD_DIM)

    small = (
        (exps_hbm, exps_ref),
        (expert_hbm, expert_ref),
        (step_hbm, step_ref),
        (len_hbm, len_ref),
        (mod_hbm, mod_ref),
        (freq_hbm.at[seq], freq_ref),
    )
    pltpu.make_async_copy(wo_ref, wo_rows, loc_sem.at[3]).start()
    for index, (source, target) in enumerate(small):
        pltpu.make_async_copy(source, target, small_sem.at[index]).start()

    barrier = pltpu.get_barrier_semaphore()
    for d in range(1, NY):
        pl.semaphore_signal(barrier, inc=1, device_id=dev_y(mod(y + d, NY)), device_id_type=MESH)
    for dev in (z_next, z_prev, x_next, x_prev, sibling):
        pl.semaphore_signal(barrier, inc=1, device_id=dev, device_id_type=MESH)

    for j, ref in enumerate((q_ref, k_ref, v_ref)):
        pltpu.make_async_copy(ref.at[0], pre.at[j], loc_sem.at[j]).start()
    pltpu.make_async_copy(res_ref, resv, loc_sem.at[4]).start()
    own_w = wslot(z, x)

    pl.semaphore_wait(barrier, 12)

    def pack_own():
        for index, (source, target) in enumerate(small):
            pltpu.make_async_copy(source, target, small_sem.at[index]).wait()
        for choice in range(2):
            powers = (jnp.left_shift(jnp.ones((HEADS, D // 128), jnp.int32), exps_ref[:, choice, :] + 1).astype(F32) * 0.5).astype(BF16)
            column = seq * COLS + lax.broadcasted_iota(jnp.int32, (D // 128, COLS), 1)
            hot = (column // 128 == lax.broadcasted_iota(jnp.int32, (D // 128, COLS), 0)).astype(F32).astype(BF16)
            stab[choice] = jnp.dot(powers, hot, preferred_element_type=F32)
        wait(wo_rows, loc_sem.at[3])
        for choice in range(2):
            for piece in range(DEPTH // 16):
                head = (rep * DEPTH + piece * 16) // HEAD_DIM
                rows = wo_rows[choice, piece * 16 : (piece + 1) * 16, :].astype(F32) * stab[choice, pl.ds(head, 1), :]
                wo_rows[choice, piece * 16 : (piece + 1) * 16, :] = rows.astype(BF16)
        packed = jnp.zeros((DEPTH, PACK), F32)
        origin = lax.broadcasted_iota(jnp.int32, (COLS, PACK), 0)
        lane = lax.broadcasted_iota(jnp.int32, (COLS, PACK), 1)
        for choice in range(2):
            low = jnp.where(origin < MAIN, choice * MAIN + origin, 2 * MAIN + choice * EDGE + origin - MAIN)
            high = jnp.where(origin < EDGE, 2 * MAIN + (1 - choice) * EDGE + origin, choice * MAIN + origin - EDGE)
            hot = (lane == jnp.where(zl == 0, low, high)).astype(F32).astype(BF16)
            packed += jnp.dot(wo_rows[choice], hot, preferred_element_type=F32)
        wbuf[zl, zh, pl.ds(pl.multiple_of((x * 2 + c) * DEPTH, 16), DEPTH), :] = packed.astype(BF16)

    def tables():
        flat = lax.broadcasted_iota(jnp.int32, (1, SEQ), 1)
        upper = (flat >= HALF).astype(jnp.int32)
        within = flat - upper * HALF
        source = sum((within >= ROWS * m).astype(jnp.int32) for m in range(1, NY))
        position = within + (source + upper) * ROWS
        bias_ref[...] = jnp.where(position < len_ref[rep], 0.0, -1e30)
        angle = 1000.0 * (1.0 - step_ref[rep].astype(F32) / STEPS) * freq_ref[...]
        feature = jnp.where(seq < NY * NZL // 2, jnp.cos(angle), jnp.sin(angle))
        gate = mod_ref[pl.ds(expert_ref[rep], 1), :] + feature
        gate_ref[...] = jnp.broadcast_to(gate, (128, COLS)).T

    twice = 2 - 4 * c
    mid_to, mid_from = mod(y + twice, NY), mod(y - twice, NY)

    def run(n):
        def heads(d):
            return n if d % 2 == 0 else 5 - n

        def a2a(d, phase):
            to = mod(y + d, NY)
            cut = lanes(phase, heads(d))
            source = pre.at[:, :, columns(to, phase, heads(d))]
            if d == NY // 2:
                send(source, stage.at[:, :, cut], as_sem.at[phase, d], sr_sem.at[phase], dev_y(mid_to))
            else:
                send(source, qkv.at[:, zl, y, :, cut], as_sem.at[phase, d], ar_sem.at[phase, d], dev_y(to))

        def own_kv(phase):
            source = pre.at[pl.ds(1, 2), :, columns(y, phase, n)]
            target = qkv.at[pl.ds(1, 2), zl, y, :, lanes(phase, n)]
            send(source, target, ks_sem.at[phase, y], kr_sem.at[phase, y], partner)

        def mid_tick(phase):
            block = stage.at[:, :, lanes(phase, n)]
            wait(block, sr_sem.at[phase])
            target = qkv.at[:, zl, mid_from, :, lanes(phase, n)]
            send(block, target, fs_sem.at[phase], ar_sem.at[phase, NY // 2], dev_y(mid_to))

        def kv_tick(d, phase):
            source = mod(y - d, NY)
            wait(qkv.at[:, zl, source, :, lanes(phase, n)], ar_sem.at[phase, d])
            block = qkv.at[pl.ds(1, 2), zl, source, :, lanes(phase, n)]
            send(block, block, ks_sem.at[phase, source], kr_sem.at[phase, source], partner)

        def kv_done(phase):
            for source in range(NY):
                wait(qkv.at[pl.ds(1, 2), 1 - zl, source, :, lanes(phase, n)], kr_sem.at[phase, source])

        def z_tick(d):
            block = wslot(mod(z - d, NZ), x)
            wait(block, zr_sem.at[d])
            if d < NZ // 2:
                send(block, block, zs_sem.at[0, d], zr_sem.at[d + 1], z_next)
            elif d > NZ // 2 + 1:
                send(block, block, zs_sem.at[1, d], zr_sem.at[d - 1], z_prev)
            send(block, block, xs_sem.at[0, d], xr_sem.at[0, d], x_next)
            send(block, block, xs_sem.at[1, d], xr_sem.at[1, d], x_prev)

        def x_tick(d):
            zz = mod(z - d, NZ)
            left, right = wslot(zz, mod(x - 1, NX)), wslot(zz, mod(x + 1, NX))
            wait(left, xr_sem.at[0, d])
            wait(right, xr_sem.at[1, d])
            if d < NZ // 2:
                send(left, left, rs_sem.at[d], rr_sem.at[d], x_next)
            else:
                send(right, right, rs_sem.at[d], rr_sem.at[d], x_prev)

        def die_push(xx, index):
            rows = pl.ds(pl.multiple_of((xx * 2 + c) * DEPTH, 16), DEPTH)
            expert, expert_beside = expert_ref[rep], expert_ref[rep + 1 - 2 * c]
            left = lax.broadcasted_iota(jnp.int32, (DEPTH, 2 * EDGE), 1) < EDGE
            for group in range(NZH):
                for place in range(NZL):
                    low, high = wbuf[place, group, rows, :MAIN], wbuf[place, group, rows, MAIN : 2 * MAIN]
                    cut = slice(place * MAIN, (place + 1) * MAIN)
                    wch[group, rows, cut] = jnp.where(expert == 1, high, low)
                    dstage[index, group, :, cut] = jnp.where(expert_beside == 1, high, low)
                edges = [wbuf[place, group, rows, 2 * MAIN :].astype(F32) for place in range(NZL)]
                low = jnp.where(left, edges[0], edges[1]).astype(BF16)
                high = jnp.where(left, edges[1], edges[0]).astype(BF16)
                wch[group, rows, 2 * MAIN :] = jnp.where(expert == 1, high, low)
                dstage[index, group, :, 2 * MAIN :] = jnp.where(expert_beside == 1, high, low)
            send(dstage.at[index], wch.at[:, rows, :], ds_sem.at[index], dr_sem.at[index], sibling)

        def head_rows(stream, j):
            rows = qkv[stream, :, :, :, j * HEAD_DIM : (j + 1) * HEAD_DIM].astype(F32)
            return rows.reshape(SEQ, HEAD_DIM).astype(BF16)

        def attend(j, half, keys, values):
            first = half * (NY // 2)
            query = qkv[0, zl, pl.ds(first, NY // 2), :, j * HEAD_DIM : (j + 1) * HEAD_DIM]
            query = query.astype(F32).reshape(QUART, HEAD_DIM).astype(BF16)
            scores = lax.dot_general(query, keys, (((1,), (1,)), ((), ())), preferred_element_type=F32)
            scores = scores + bias_ref[...]
            top = jnp.max(scores, axis=1, keepdims=True)
            probs = jnp.exp2((scores - top) * SCALE)
            total = jnp.sum(probs, axis=1, keepdims=True)
            summed = jnp.dot(probs.astype(BF16), values, preferred_element_type=F32)
            attm[y, half * QUART : (half + 1) * QUART, j * HEAD_DIM : (j + 1) * HEAD_DIM] = (summed / total).astype(BF16)

        def kinds(count):
            return (0, 1, 2, 3) if count == 3 else (0, 2, 3)

        def last_kinds(direction, count):
            return ((0, 2), (1, 3))[direction] if count == 3 else ((0,), (2, 3))[direction]

        def region(yy, kind, count):
            if kind < 2:
                return attm.at[yy, :, pl.ds(kind * HEAD_DIM, HEAD_DIM)]
            return attm.at[yy, pl.ds((kind - 2) * QUART, QUART), pl.ds((count - 1) * HEAD_DIM, HEAD_DIM)]

        def ring_send(t, direction, kind, yy):
            block = region(yy, kind, heads(t - 1))
            sems = gs_sem.at[direction, t - 1, kind], gr_sem.at[direction, t - 1, kind]
            send(block, block, *sems, (y_next, y_prev)[direction])

        def ring_start(kind):
            for direction in range(2):
                ring_send(1, direction, kind, y)

        def ring_wait(t, direction, kind):
            yy = mod(y - t if direction == 0 else y + t, NY)
            wait(region(yy, kind, heads(t)), gr_sem.at[direction, t - 1, kind])
            return yy

        def ring_tick(t, kind):
            if kind not in kinds(heads(t)):
                return
            for direction in range(2):
                yy = ring_wait(t, direction, kind)
                if t < NY // 2 - 1 or kind in last_kinds(direction, heads(t)):
                    ring_send(t + 1, direction, kind, yy)

        def project(yy, count, part, rows=slice(0, HALF), fresh=False):
            first = 0 if count == 3 else 3 * HEAD_DIM
            if part == EDGES:
                cut, total = pl.ds(2 * MAIN, 2 * EDGE), edge
            else:
                cut, total = pl.ds(pl.multiple_of((zl if part == OWN else 1 - zl) * MAIN, MAIN), MAIN), acc.at[part]
            weight = wch[yy // 2, first : first + count * HEAD_DIM, cut]
            made = jnp.dot(attm[yy, rows, : count * HEAD_DIM], weight, preferred_element_type=F32)
            if fresh:
                total[rows] = made
            else:
                total[rows] += made

        def project_two(first, step, *parts):
            def one(i, _):
                for part in parts:
                    project(mod(y + first + step * i, NY), heads(first), part)
                return 0

            lax.fori_loop(0, 2, one, 0)

        order, served = (4, 3, 5, 2, 6, 1, 7), (3, 5, 2, 6, 1, 7, 4)
        for j in range(3):
            wait(pre.at[j], loc_sem.at[j])
        own_kv(0)
        for d in order:
            a2a(d, 0)
        pack_own()
        send(own_w, own_w, zs_sem.at[0, 0], zr_sem.at[1], z_next)
        send(own_w, own_w, zs_sem.at[1, 0], zr_sem.at[NZ - 1], z_prev)
        send(own_w, own_w, xs_sem.at[0, 0], xr_sem.at[0, 0], x_next)
        send(own_w, own_w, xs_sem.at[1, 0], xr_sem.at[1, 0], x_prev)
        start = pl.multiple_of(((y // 2) * 5 + (0 if n == 3 else 3)) * HEAD_DIM, HEAD_DIM)
        own_block = qkv.at[:, zl, y, :, pl.ds(0, n * HEAD_DIM)]
        pltpu.make_async_copy(pre.at[:, :, pl.ds(start, n * HEAD_DIM)], own_block, loc_sem.at[5]).start()
        tables()
        mid_tick(0)
        own_kv(1)
        for d in order[:3]:
            a2a(d, 1)
        z_tick(1)
        z_tick(7)
        for d in served[:3]:
            kv_tick(d, 0)
        for d in order[3:]:
            a2a(d, 1)
        z_tick(2)
        z_tick(6)
        for d in served[3:]:
            kv_tick(d, 0)
        mid_tick(1)
        z_tick(3)
        z_tick(5)

        wait(own_block, loc_sem.at[5])
        kv_done(0)
        for j in range(n - 1):
            keys, values = head_rows(1, j), head_rows(2, j)
            for half in range(2):
                attend(j, half, keys, values)
            ring_start(j)
            for d in served[:2] if j == 0 else served[2:4]:
                kv_tick(d, 1)
            if j == 0:
                z_tick(4)
                x_tick(0)
                x_tick(1)
                x_tick(7)
        for d in served[2 * (n - 1) :]:
            kv_tick(d, 1)
        x_tick(2)
        x_tick(6)
        ring_tick(1, 0)
        die_push(x, 0)

        kv_done(1)
        keys, values = head_rows(1, n - 1), head_rows(2, n - 1)
        attend(n - 1, 0, keys, values)
        ring_start(2)
        ring_tick(1, 1)
        attend(n - 1, 1, keys, values)
        ring_start(3)
        ring_tick(2, 0)
        x_tick(3)
        x_tick(5)
        ring_tick(2, 1)
        ring_tick(1, 2)
        x_tick(4)
        ring_tick(1, 3)
        ring_tick(3, 0)
        ring_tick(3, 1)
        die_push(mod(x - 1, NX), 1)
        die_push(mod(x + 1, NX), 2)
        ring_tick(2, 2)
        ring_tick(2, 3)
        far = mod(x + 2, NX)
        for d in range(NZ):
            wait(wslot(mod(z - d, NZ), far), rr_sem.at[d])
        die_push(far, 3)
        for phase in range(2):
            for d in range(1, NY):
                wait(qkv.at[:, zl, y, :, lanes(phase, heads(d))], as_sem.at[phase, d])
            wait(stage.at[:, :, lanes(phase, n)], fs_sem.at[phase])
            for source in range(NY):
                wait(qkv.at[pl.ds(1, 2), zl, source, :, lanes(phase, n)], ks_sem.at[phase, source])
        ring_tick(3, 2)
        ring_tick(3, 3)
        for index, xx in enumerate((x, mod(x - 1, NX), mod(x + 1, NX), far)):
            wait(wch.at[:, pl.ds((xx * 2 + 1 - c) * DEPTH, DEPTH), :], dr_sem.at[index])
        project(y, n, OTHER, fresh=True)
        project(y, n, EDGES, fresh=True)
        project_two(1, 6, OTHER, EDGES)
        project_two(2, 4, OTHER, EDGES)
        project_two(3, 2, OTHER, EDGES)
        project(y, n, OWN, fresh=True)

        last = mod(y + NY // 2, NY)
        turned = lax.rem(expert_ref[rep] + zl, 2) * EDGE
        left = lax.broadcasted_iota(jnp.int32, (QUART // 2, 2 * EDGE), 1) < EDGE
        for half in range(2):
            for kind in ((0, 1, 2) if n == 3 else (0, 2)) if half == 0 else (3,):
                ring_wait(NY // 2, 0 if kind in last_kinds(0, n) else 1, kind)
            rows = slice(half * QUART, (half + 1) * QUART)
            project(last, n, OTHER, rows)
            psend[rows] = acc[OTHER, rows].astype(BF16)
            send(psend.at[rows], precv.at[rows], os_sem.at[0, half], or_sem.at[0, half], partner)
            project(last, n, EDGES, rows)
            top = edge[half * QUART : half * QUART + QUART // 2]
            low = edge[half * QUART + QUART // 2 : (half + 1) * QUART]
            both = jnp.where(left, pltpu.roll(top, EDGE - turned, 1), pltpu.roll(low, turned, 1))
            esend[half] = both.astype(BF16)
            send(esend.at[half], erecv.at[half], os_sem.at[1, half], or_sem.at[1, half], partner)
        project_two(1, 6, OWN)
        project_two(2, 4, OWN)
        project_two(3, 2, OWN)
        project(last, n, OWN)

        for t in range(1, NY // 2 + 1):
            for direction in range(2):
                for kind in kinds(heads(t - 1)) if t < NY // 2 else last_kinds(direction, heads(t - 1)):
                    wait(region(y, kind, heads(t - 1)), gs_sem.at[direction, t - 1, kind])

    pl.when(lax.rem(y, 2) == 0)(lambda: run(3))
    pl.when(lax.rem(y, 2) == 1)(lambda: run(2))

    for d in (0, 1, 2, 3):
        wait(own_w, zs_sem.at[0, d])
    for d in (0, 7, 6):
        wait(own_w, zs_sem.at[1, d])
    for d in range(NZ):
        wait(own_w, xs_sem.at[0, d])
        wait(own_w, xs_sem.at[1, d])
        wait(own_w, rs_sem.at[d])
    for index in range(NX):
        wait(dstage.at[index], ds_sem.at[index])
    wait(resv, loc_sem.at[4])
    turned = lax.rem(expert_ref[rep] + zl, 2) * EDGE
    for block in range(NY):
        rows, place = slice(block * ROWS, (block + 1) * ROWS), pl.ds((block * NZL + zl) * ROWS, ROWS)
        nat[place, :MAIN] = acc[OWN, rows]
        nat[place, MAIN:] = pltpu.roll(edge[rows], turned, 1)
    main_at = pl.ds(pl.multiple_of(zl * EDGE, EDGE), MAIN)
    edge_at = pl.ds(pl.multiple_of((1 - zl) * MAIN, EDGE), EDGE)
    for half in range(2):
        rows = slice(half * QUART, (half + 1) * QUART)
        wait(precv.at[rows], or_sem.at[0, half])
        wait(erecv.at[half], or_sem.at[1, half])
        acc[OTHER, rows] = precv[rows].astype(F32)
        both = erecv[half].astype(F32)
        edge[half * QUART : half * QUART + QUART // 2] = both
        edge[half * QUART + QUART // 2 : (half + 1) * QUART] = pltpu.roll(both, EDGE, 1)
        for block in range(half * NY // 2, (half + 1) * NY // 2):
            rows, place = slice(block * ROWS, (block + 1) * ROWS), pl.ds((block * NZL + 1 - zl) * ROWS, ROWS)
            nat[place, :MAIN] = acc[OTHER, rows]
            nat[place, MAIN:] = edge[rows]
        for block in ((0, 1, 2), (3, 4, 5, 6))[half]:
            tokens = slice(block * 128, (block + 1) * 128)
            made = nat[tokens, :].T
            for at, part in ((main_at, made[:MAIN]), (edge_at, made[MAIN : MAIN + EDGE])):
                mixed = resv[0, at, tokens].astype(F32) + gate_ref[at, :] * part
                out_ref[0, at, tokens] = mixed.astype(BF16)
    for half in range(2):
        wait(psend.at[half * QUART : (half + 1) * QUART], os_sem.at[0, half])
        wait(esend.at[half], os_sem.at[1, half])


def local(queries, keys, values, residual, wo_values, wo_exponents, modulation, expert_choice, step_index, lengths):
    offset = np.arange(D) % (D // 2)
    freq = np.exp(-math.log(10000.0) * offset / (D // 2)).astype(np.float32).reshape(D // COLS, 1, COLS)
    hbm = pl.BlockSpec(memory_space=pl.ANY)
    vmem = pl.BlockSpec(memory_space=pltpu.VMEM)
    dma = pltpu.SemaphoreType.DMA
    mixed = pl.pallas_call(
        kernel,
        out_shape=pltpu.VMEM((1, COLS, SEQ), BF16),
        in_specs=[hbm] * 11,
        out_specs=vmem,
        scratch_shapes=[
            pltpu.VMEM((HEADS, 2, D // 128), jnp.int32),
            pltpu.VMEM((2, COLS), F32),
            pltpu.VMEM((1, COLS), F32),
            pltpu.SMEM((CLIPS,), jnp.int32),
            pltpu.SMEM((CLIPS,), jnp.int32),
            pltpu.SMEM((CLIPS,), jnp.int32),
            pltpu.VMEM((3, ROWS, HEADS * HEAD_DIM), BF16),
            pltpu.VMEM((3, NZL, NY, ROWS, 3 * HEAD_DIM), BF16),
            pltpu.VMEM((3, ROWS, 3 * HEAD_DIM), BF16),
            pltpu.VMEM((NZL, NZH, 2 * NX * DEPTH, PACK), BF16),
            pltpu.VMEM((2, DEPTH, COLS), BF16),
            pltpu.VMEM((NZH, 2 * NX * DEPTH, PACK), BF16),
            pltpu.VMEM((NX, NZH, DEPTH, PACK), BF16),
            pltpu.VMEM((NY, HALF, 3 * HEAD_DIM), BF16),
            pltpu.VMEM((2, HALF, MAIN), F32),
            pltpu.VMEM((HALF, 2 * EDGE), F32),
            pltpu.VMEM((HALF, MAIN), BF16),
            pltpu.VMEM((HALF, MAIN), BF16),
            pltpu.VMEM((2, QUART // 2, 2 * EDGE), BF16),
            pltpu.VMEM((2, QUART // 2, 2 * EDGE), BF16),
            pltpu.VMEM((1, COLS, SEQ), BF16),
            pltpu.VMEM((SEQ, MAIN + 2 * EDGE), F32),
            pltpu.VMEM((2, HEADS, COLS), F32),
            pltpu.VMEM((1, SEQ), F32),
            pltpu.VMEM((COLS, 128), F32),
            dma((6,)),
            dma((6,)),
            dma((2, NY)),
            dma((2, NY)),
            dma((2,)),
            dma((2,)),
            dma((2, NY)),
            dma((2, NY)),
            dma((2, NZ)),
            dma((NZ,)),
            dma((2, NZ)),
            dma((2, NZ)),
            dma((NZ,)),
            dma((NZ,)),
            dma((NX,)),
            dma((NX,)),
            dma((2, NY // 2, 5)),
            dma((2, NY // 2, 5)),
            dma((2, 2)),
            dma((2, 2)),
        ],
        compiler_params=pltpu.CompilerParams(
            collective_id=0, has_side_effects=True, vmem_limit_bytes=62 * 2**20
        ),
        cost_estimate=pl.CostEstimate(flops=2 * 10**9, bytes_accessed=3 * 10**6, transcendentals=10**6),
    )(
        queries,
        keys,
        values,
        jnp.swapaxes(residual, 1, 2),
        wo_values,
        jnp.swapaxes(wo_exponents, 0, 1),
        modulation,
        jnp.asarray(freq),
        expert_choice,
        step_index,
        lengths,
    )
    return jnp.swapaxes(mixed, 1, 2)


def solution(mesh):
    placed = (
        P("rep", "seq", None),
        P("rep", "seq", None),
        P("rep", "seq", None),
        P("rep", None, "seq"),
        P(None, "rep", "seq"),
        P(),
        P(None, "seq"),
        P(),
        P(),
        P(),
    )
    return jax.shard_map(
        local, mesh=mesh, in_specs=placed, out_specs=P("rep", None, "seq"), check_vma=False
    )
```

```python
import math

import jax
import jax.numpy as jnp
import numpy as np
from jax import lax
from jax.experimental import pallas as pl
from jax.experimental.pallas import tpu as pltpu
from jax.sharding import PartitionSpec as P

D = 5120
HEADS = 20
HEAD_DIM = 128
STEPS = 10
NY = 8
NZL = 2
NX = 4
NZH = 4
NZ = NZL * NZH
ROWS = 56
SEQ = ROWS * NY * NZL
CLIPS = 2 * NX * NZH
HALF = ROWS * NY
QUART = HALF // 2
COLS = 320
MAIN = 256
EDGE = COLS - MAIN
PACK = 2 * COLS
DEPTH = 80
SCALE = HEAD_DIM**-0.5 * math.log2(math.e)

OWN, OTHER, EDGES = 0, 1, 2
MESH = pl.DeviceIdType.MESH
F32 = jnp.float32
BF16 = jnp.bfloat16


def mod(value, size):
    return lax.rem(value + size, size)


def kernel(
    q_ref,
    k_ref,
    v_ref,
    res_ref,
    wo_ref,
    exps_hbm,
    mod_hbm,
    freq_hbm,
    expert_hbm,
    step_hbm,
    len_hbm,
    out_ref,
    exps_ref,
    mod_ref,
    freq_ref,
    expert_ref,
    step_ref,
    len_ref,
    pre,
    qkv,
    wbuf,
    wo_rows,
    wch,
    dstage,
    attm,
    acc,
    edge,
    psend,
    precv,
    esend,
    erecv,
    resv,
    nat,
    stab,
    bias_ref,
    gate_ref,
    loc_sem,
    small_sem,
    as_sem,
    ar_sem,
    ks_sem,
    kr_sem,
    zs_sem,
    zr_sem,
    xs_sem,
    xr_sem,
    rs_sem,
    rr_sem,
    ds_sem,
    dr_sem,
    gs_sem,
    gr_sem,
    os_sem,
    or_sem,
):
    rep = lax.axis_index("rep")
    seq = lax.axis_index("seq")
    c = lax.rem(rep, 2)
    x = lax.rem(rep // 2, NX)
    zh = rep // (2 * NX)
    y = seq // NZL
    zl = lax.rem(seq, NZL)
    z = zh * NZL + zl

    def dev_y(yy):
        return {"rep": rep, "seq": yy * NZL + zl}

    def dev_z(zz):
        return {"rep": (zz // NZL) * (2 * NX) + x * 2 + c, "seq": y * NZL + lax.rem(zz, NZL)}

    def dev_x(xx):
        return {"rep": zh * (2 * NX) + xx * 2 + c, "seq": seq}

    partner = {"rep": rep, "seq": y * NZL + 1 - zl}
    sibling = {"rep": rep + 1 - 2 * c, "seq": seq}
    z_next, z_prev = dev_z(mod(z + 1, NZ)), dev_z(mod(z - 1, NZ))
    x_next, x_prev = dev_x(mod(x + 1, NX)), dev_x(mod(x - 1, NX))
    y_next, y_prev = dev_y(mod(y + 1, NY)), dev_y(mod(y - 1, NY))

    def send(src, dst, ss, rs, dev):
        pltpu.make_async_remote_copy(
            src_ref=src, dst_ref=dst, send_sem=ss, recv_sem=rs, device_id=dev, device_id_type=MESH
        ).start()

    def wait(ref, sem):
        pltpu.make_async_copy(ref, ref, sem).wait()

    def wslot(zz, xx):
        return wbuf.at[lax.rem(zz, NZL), zz // NZL, pl.ds((xx * 2 + c) * DEPTH, DEPTH), :]

    def lanes(phase, n):
        return pl.ds(0, (n - 1) * HEAD_DIM) if phase == 0 else pl.ds((n - 1) * HEAD_DIM, HEAD_DIM)

    def columns(yy, phase, n):
        first = (yy // 2) * 5 + (0 if n == 3 else 3) + phase * (n - 1)
        return pl.ds(pl.multiple_of(first * HEAD_DIM, HEAD_DIM), (n - 1) * HEAD_DIM if phase == 0 else HEAD_DIM)

    small = (
        (exps_hbm, exps_ref),
        (expert_hbm, expert_ref),
        (step_hbm, step_ref),
        (len_hbm, len_ref),
        (mod_hbm, mod_ref),
        (freq_hbm.at[seq], freq_ref),
    )
    pltpu.make_async_copy(wo_ref, wo_rows, loc_sem.at[3]).start()
    for index, (source, target) in enumerate(small):
        pltpu.make_async_copy(source, target, small_sem.at[index]).start()

    barrier = pltpu.get_barrier_semaphore()
    for d in range(1, NY):
        pl.semaphore_signal(barrier, inc=1, device_id=dev_y(mod(y + d, NY)), device_id_type=MESH)
    for dev in (z_next, z_prev, x_next, x_prev, sibling):
        pl.semaphore_signal(barrier, inc=1, device_id=dev, device_id_type=MESH)

    for j, ref in enumerate((q_ref, k_ref, v_ref)):
        pltpu.make_async_copy(ref.at[0], pre.at[j], loc_sem.at[j]).start()
    pltpu.make_async_copy(res_ref, resv, loc_sem.at[4]).start()
    own_w = wslot(z, x)

    pl.semaphore_wait(barrier, 12)

    def pack_own():
        for index, (source, target) in enumerate(small):
            pltpu.make_async_copy(source, target, small_sem.at[index]).wait()
        for choice in range(2):
            powers = (jnp.left_shift(jnp.ones((HEADS, D // 128), jnp.int32), exps_ref[:, choice, :] + 1).astype(F32) * 0.5).astype(BF16)
            column = seq * COLS + lax.broadcasted_iota(jnp.int32, (D // 128, COLS), 1)
            hot = (column // 128 == lax.broadcasted_iota(jnp.int32, (D // 128, COLS), 0)).astype(F32).astype(BF16)
            stab[choice] = jnp.dot(powers, hot, preferred_element_type=F32)
        wait(wo_rows, loc_sem.at[3])
        for choice in range(2):
            for piece in range(DEPTH // 16):
                head = (rep * DEPTH + piece * 16) // HEAD_DIM
                rows = wo_rows[choice, piece * 16 : (piece + 1) * 16, :].astype(F32) * stab[choice, pl.ds(head, 1), :]
                wo_rows[choice, piece * 16 : (piece + 1) * 16, :] = rows.astype(BF16)
        packed = jnp.zeros((DEPTH, PACK), F32)
        origin = lax.broadcasted_iota(jnp.int32, (COLS, PACK), 0)
        lane = lax.broadcasted_iota(jnp.int32, (COLS, PACK), 1)
        for choice in range(2):
            low = jnp.where(origin < MAIN, choice * MAIN + origin, 2 * MAIN + choice * EDGE + origin - MAIN)
            high = jnp.where(origin < EDGE, 2 * MAIN + (1 - choice) * EDGE + origin, choice * MAIN + origin - EDGE)
            hot = (lane == jnp.where(zl == 0, low, high)).astype(F32).astype(BF16)
            packed += jnp.dot(wo_rows[choice], hot, preferred_element_type=F32)
        wbuf[zl, zh, pl.ds(pl.multiple_of((x * 2 + c) * DEPTH, 16), DEPTH), :] = packed.astype(BF16)

    def tables():
        flat = lax.broadcasted_iota(jnp.int32, (1, SEQ), 1)
        upper = (flat >= HALF).astype(jnp.int32)
        within = flat - upper * HALF
        source = sum((within >= ROWS * m).astype(jnp.int32) for m in range(1, NY))
        position = within + (source + upper) * ROWS
        bias_ref[...] = jnp.where(position < len_ref[rep], 0.0, -1e30)
        angle = 1000.0 * (1.0 - step_ref[rep].astype(F32) / STEPS) * freq_ref[...]
        feature = jnp.where(seq < NY * NZL // 2, jnp.cos(angle), jnp.sin(angle))
        gate = mod_ref[pl.ds(expert_ref[rep], 1), :] + feature
        gate_ref[...] = jnp.broadcast_to(gate, (128, COLS)).T

    def run(n):
        def heads(d):
            return n if d % 2 == 0 else 5 - n

        def a2a(d, phase):
            to = mod(y + d, NY)
            cut = lanes(phase, heads(d))
            source = pre.at[:, :, columns(to, phase, heads(d))]
            send(source, qkv.at[:, zl, y, :, cut], as_sem.at[phase, d], ar_sem.at[phase, d], dev_y(to))

        def own_kv(phase):
            source = pre.at[pl.ds(1, 2), :, columns(y, phase, n)]
            target = qkv.at[pl.ds(1, 2), zl, y, :, lanes(phase, n)]
            send(source, target, ks_sem.at[phase, y], kr_sem.at[phase, y], partner)

        def kv_tick(d, phase):
            source = mod(y - d, NY)
            wait(qkv.at[:, zl, source, :, lanes(phase, n)], ar_sem.at[phase, d])
            block = qkv.at[pl.ds(1, 2), zl, source, :, lanes(phase, n)]
            send(block, block, ks_sem.at[phase, source], kr_sem.at[phase, source], partner)

        def kv_done(phase):
            for source in range(NY):
                wait(qkv.at[pl.ds(1, 2), 1 - zl, source, :, lanes(phase, n)], kr_sem.at[phase, source])

        def z_tick(d):
            block = wslot(mod(z - d, NZ), x)
            wait(block, zr_sem.at[d])
            if d < NZ // 2:
                send(block, block, zs_sem.at[0, d], zr_sem.at[d + 1], z_next)
            elif d > NZ // 2 + 1:
                send(block, block, zs_sem.at[1, d], zr_sem.at[d - 1], z_prev)
            send(block, block, xs_sem.at[0, d], xr_sem.at[0, d], x_next)
            send(block, block, xs_sem.at[1, d], xr_sem.at[1, d], x_prev)

        def x_tick(d):
            zz = mod(z - d, NZ)
            left, right = wslot(zz, mod(x - 1, NX)), wslot(zz, mod(x + 1, NX))
            wait(left, xr_sem.at[0, d])
            wait(right, xr_sem.at[1, d])
            if d < NZ // 2:
                send(left, left, rs_sem.at[d], rr_sem.at[d], x_next)
            else:
                send(right, right, rs_sem.at[d], rr_sem.at[d], x_prev)

        def die_push(xx, index):
            rows = pl.ds(pl.multiple_of((xx * 2 + c) * DEPTH, 16), DEPTH)
            expert, expert_beside = expert_ref[rep], expert_ref[rep + 1 - 2 * c]
            left = lax.broadcasted_iota(jnp.int32, (DEPTH, 2 * EDGE), 1) < EDGE
            for group in range(NZH):
                for place in range(NZL):
                    low, high = wbuf[place, group, rows, :MAIN], wbuf[place, group, rows, MAIN : 2 * MAIN]
                    cut = slice(place * MAIN, (place + 1) * MAIN)
                    wch[group, rows, cut] = jnp.where(expert == 1, high, low)
                    dstage[index, group, :, cut] = jnp.where(expert_beside == 1, high, low)
                edges = [wbuf[place, group, rows, 2 * MAIN :].astype(F32) for place in range(NZL)]
                low = jnp.where(left, edges[0], edges[1]).astype(BF16)
                high = jnp.where(left, edges[1], edges[0]).astype(BF16)
                wch[group, rows, 2 * MAIN :] = jnp.where(expert == 1, high, low)
                dstage[index, group, :, 2 * MAIN :] = jnp.where(expert_beside == 1, high, low)
            send(dstage.at[index], wch.at[:, rows, :], ds_sem.at[index], dr_sem.at[index], sibling)

        def head_rows(stream, j):
            rows = qkv[stream, :, :, :, j * HEAD_DIM : (j + 1) * HEAD_DIM].astype(F32)
            return rows.reshape(SEQ, HEAD_DIM).astype(BF16)

        def attend(j, half, keys, values):
            first = half * (NY // 2)
            query = qkv[0, zl, pl.ds(first, NY // 2), :, j * HEAD_DIM : (j + 1) * HEAD_DIM]
            query = query.astype(F32).reshape(QUART, HEAD_DIM).astype(BF16)
            scores = lax.dot_general(query, keys, (((1,), (1,)), ((), ())), preferred_element_type=F32)
            scores = scores + bias_ref[...]
            top = jnp.max(scores, axis=1, keepdims=True)
            probs = jnp.exp2((scores - top) * SCALE)
            total = jnp.sum(probs, axis=1, keepdims=True)
            summed = jnp.dot(probs.astype(BF16), values, preferred_element_type=F32)
            attm[y, half * QUART : (half + 1) * QUART, j * HEAD_DIM : (j + 1) * HEAD_DIM] = (summed / total).astype(BF16)

        def kinds(count):
            return (0, 1, 2, 3) if count == 3 else (0, 2, 3)

        def last_kinds(direction, count):
            return ((0, 2), (1, 3))[direction] if count == 3 else ((0,), (2, 3))[direction]

        def region(yy, kind, count):
            if kind < 2:
                return attm.at[yy, :, pl.ds(kind * HEAD_DIM, HEAD_DIM)]
            return attm.at[yy, pl.ds((kind - 2) * QUART, QUART), pl.ds((count - 1) * HEAD_DIM, HEAD_DIM)]

        def ring_send(t, direction, kind, yy):
            block = region(yy, kind, heads(t - 1))
            sems = gs_sem.at[direction, t - 1, kind], gr_sem.at[direction, t - 1, kind]
            send(block, block, *sems, (y_next, y_prev)[direction])

        def ring_start(kind):
            for direction in range(2):
                ring_send(1, direction, kind, y)

        def ring_wait(t, direction, kind):
            yy = mod(y - t if direction == 0 else y + t, NY)
            wait(region(yy, kind, heads(t)), gr_sem.at[direction, t - 1, kind])
            return yy

        def ring_tick(t, kind):
            if kind not in kinds(heads(t)):
                return
            for direction in range(2):
                yy = ring_wait(t, direction, kind)
                if t < NY // 2 - 1 or kind in last_kinds(direction, heads(t)):
                    ring_send(t + 1, direction, kind, yy)

        def project(yy, count, part, rows=slice(0, HALF), fresh=False):
            first = 0 if count == 3 else 3 * HEAD_DIM
            if part == EDGES:
                cut, total = pl.ds(2 * MAIN, 2 * EDGE), edge
            else:
                cut, total = pl.ds(pl.multiple_of((zl if part == OWN else 1 - zl) * MAIN, MAIN), MAIN), acc.at[part]
            weight = wch[yy // 2, first : first + count * HEAD_DIM, cut]
            made = jnp.dot(attm[yy, rows, : count * HEAD_DIM], weight, preferred_element_type=F32)
            if fresh:
                total[rows] = made
            else:
                total[rows] += made

        def project_two(first, step, *parts):
            def one(i, _):
                for part in parts:
                    project(mod(y + first + step * i, NY), heads(first), part)
                return 0

            lax.fori_loop(0, 2, one, 0)

        order = (4, 3, 5, 2, 6, 1, 7)
        for j in range(3):
            wait(pre.at[j], loc_sem.at[j])
        own_kv(0)
        for d in order:
            a2a(d, 0)
        pack_own()
        send(own_w, own_w, zs_sem.at[0, 0], zr_sem.at[1], z_next)
        send(own_w, own_w, zs_sem.at[1, 0], zr_sem.at[NZ - 1], z_prev)
        send(own_w, own_w, xs_sem.at[0, 0], xr_sem.at[0, 0], x_next)
        send(own_w, own_w, xs_sem.at[1, 0], xr_sem.at[1, 0], x_prev)
        start = pl.multiple_of(((y // 2) * 5 + (0 if n == 3 else 3)) * HEAD_DIM, HEAD_DIM)
        own_block = qkv.at[:, zl, y, :, pl.ds(0, n * HEAD_DIM)]
        pltpu.make_async_copy(pre.at[:, :, pl.ds(start, n * HEAD_DIM)], own_block, loc_sem.at[5]).start()
        tables()
        own_kv(1)
        for d in order:
            a2a(d, 1)
        z_tick(1)
        z_tick(7)
        for d in order[:3]:
            kv_tick(d, 0)
        z_tick(2)
        z_tick(6)
        for d in order[3:]:
            kv_tick(d, 0)
        z_tick(3)
        z_tick(5)

        wait(own_block, loc_sem.at[5])
        kv_done(0)
        for j in range(n - 1):
            keys, values = head_rows(1, j), head_rows(2, j)
            for half in range(2):
                attend(j, half, keys, values)
            ring_start(j)
            for d in order[:2] if j == 0 else order[2:4]:
                kv_tick(d, 1)
            if j == 0:
                z_tick(4)
                x_tick(0)
                x_tick(1)
                x_tick(7)
        for d in order[2 * (n - 1) :]:
            kv_tick(d, 1)
        x_tick(2)
        x_tick(6)
        ring_tick(1, 0)
        die_push(x, 0)

        kv_done(1)
        keys, values = head_rows(1, n - 1), head_rows(2, n - 1)
        attend(n - 1, 0, keys, values)
        ring_start(2)
        ring_tick(1, 1)
        attend(n - 1, 1, keys, values)
        ring_start(3)
        ring_tick(2, 0)
        x_tick(3)
        x_tick(5)
        ring_tick(2, 1)
        ring_tick(1, 2)
        x_tick(4)
        ring_tick(1, 3)
        ring_tick(3, 0)
        ring_tick(3, 1)
        die_push(mod(x - 1, NX), 1)
        die_push(mod(x + 1, NX), 2)
        ring_tick(2, 2)
        ring_tick(2, 3)
        far = mod(x + 2, NX)
        for d in range(NZ):
            wait(wslot(mod(z - d, NZ), far), rr_sem.at[d])
        die_push(far, 3)
        for phase in range(2):
            for d in range(1, NY):
                wait(qkv.at[:, zl, y, :, lanes(phase, heads(d))], as_sem.at[phase, d])
            for source in range(NY):
                wait(qkv.at[pl.ds(1, 2), zl, source, :, lanes(phase, n)], ks_sem.at[phase, source])
        ring_tick(3, 2)
        ring_tick(3, 3)
        for index, xx in enumerate((x, mod(x - 1, NX), mod(x + 1, NX), far)):
            wait(wch.at[:, pl.ds((xx * 2 + 1 - c) * DEPTH, DEPTH), :], dr_sem.at[index])
        project(y, n, OTHER, fresh=True)
        project(y, n, EDGES, fresh=True)
        project_two(1, 6, OTHER, EDGES)
        project_two(2, 4, OTHER, EDGES)
        project_two(3, 2, OTHER, EDGES)
        project(y, n, OWN, fresh=True)

        last = mod(y + NY // 2, NY)
        turned = lax.rem(expert_ref[rep] + zl, 2) * EDGE
        left = lax.broadcasted_iota(jnp.int32, (QUART // 2, 2 * EDGE), 1) < EDGE
        for half in range(2):
            for kind in ((0, 1, 2) if n == 3 else (0, 2)) if half == 0 else (3,):
                ring_wait(NY // 2, 0 if kind in last_kinds(0, n) else 1, kind)
            rows = slice(half * QUART, (half + 1) * QUART)
            project(last, n, OTHER, rows)
            psend[rows] = acc[OTHER, rows].astype(BF16)
            send(psend.at[rows], precv.at[rows], os_sem.at[0, half], or_sem.at[0, half], partner)
            project(last, n, EDGES, rows)
            top = edge[half * QUART : half * QUART + QUART // 2]
            low = edge[half * QUART + QUART // 2 : (half + 1) * QUART]
            both = jnp.where(left, pltpu.roll(top, EDGE - turned, 1), pltpu.roll(low, turned, 1))
            esend[half] = both.astype(BF16)
            send(esend.at[half], erecv.at[half], os_sem.at[1, half], or_sem.at[1, half], partner)
        project_two(1, 6, OWN)
        project_two(2, 4, OWN)
        project_two(3, 2, OWN)
        project(last, n, OWN)

        for t in range(1, NY // 2 + 1):
            for direction in range(2):
                for kind in kinds(heads(t - 1)) if t < NY // 2 else last_kinds(direction, heads(t - 1)):
                    wait(region(y, kind, heads(t - 1)), gs_sem.at[direction, t - 1, kind])

    pl.when(lax.rem(y, 2) == 0)(lambda: run(3))
    pl.when(lax.rem(y, 2) == 1)(lambda: run(2))

    for d in (0, 1, 2, 3):
        wait(own_w, zs_sem.at[0, d])
    for d in (0, 7, 6):
        wait(own_w, zs_sem.at[1, d])
    for d in range(NZ):
        wait(own_w, xs_sem.at[0, d])
        wait(own_w, xs_sem.at[1, d])
        wait(own_w, rs_sem.at[d])
    for index in range(NX):
        wait(dstage.at[index], ds_sem.at[index])
    wait(resv, loc_sem.at[4])
    turned = lax.rem(expert_ref[rep] + zl, 2) * EDGE
    for block in range(NY):
        rows, place = slice(block * ROWS, (block + 1) * ROWS), pl.ds((block * NZL + zl) * ROWS, ROWS)
        nat[place, :MAIN] = acc[OWN, rows]
        nat[place, MAIN:] = pltpu.roll(edge[rows], turned, 1)
    main_at = pl.ds(pl.multiple_of(zl * EDGE, EDGE), MAIN)
    edge_at = pl.ds(pl.multiple_of((1 - zl) * MAIN, EDGE), EDGE)
    for half in range(2):
        rows = slice(half * QUART, (half + 1) * QUART)
        wait(precv.at[rows], or_sem.at[0, half])
        wait(erecv.at[half], or_sem.at[1, half])
        acc[OTHER, rows] = precv[rows].astype(F32)
        both = erecv[half].astype(F32)
        edge[half * QUART : half * QUART + QUART // 2] = both
        edge[half * QUART + QUART // 2 : (half + 1) * QUART] = pltpu.roll(both, EDGE, 1)
        for block in range(half * NY // 2, (half + 1) * NY // 2):
            rows, place = slice(block * ROWS, (block + 1) * ROWS), pl.ds((block * NZL + 1 - zl) * ROWS, ROWS)
            nat[place, :MAIN] = acc[OTHER, rows]
            nat[place, MAIN:] = edge[rows]
        for block in ((0, 1, 2), (3, 4, 5, 6))[half]:
            tokens = slice(block * 128, (block + 1) * 128)
            made = nat[tokens, :].T
            for at, part in ((main_at, made[:MAIN]), (edge_at, made[MAIN : MAIN + EDGE])):
                mixed = resv[0, at, tokens].astype(F32) + gate_ref[at, :] * part
                out_ref[0, at, tokens] = mixed.astype(BF16)
    for half in range(2):
        wait(psend.at[half * QUART : (half + 1) * QUART], os_sem.at[0, half])
        wait(esend.at[half], os_sem.at[1, half])


def local(queries, keys, values, residual, wo_values, wo_exponents, modulation, expert_choice, step_index, lengths):
    offset = np.arange(D) % (D // 2)
    freq = np.exp(-math.log(10000.0) * offset / (D // 2)).astype(np.float32).reshape(D // COLS, 1, COLS)
    hbm = pl.BlockSpec(memory_space=pl.ANY)
    vmem = pl.BlockSpec(memory_space=pltpu.VMEM)
    dma = pltpu.SemaphoreType.DMA
    mixed = pl.pallas_call(
        kernel,
        out_shape=pltpu.VMEM((1, COLS, SEQ), BF16),
        in_specs=[hbm] * 11,
        out_specs=vmem,
        scratch_shapes=[
            pltpu.VMEM((HEADS, 2, D // 128), jnp.int32),
            pltpu.VMEM((2, COLS), F32),
            pltpu.VMEM((1, COLS), F32),
            pltpu.SMEM((CLIPS,), jnp.int32),
            pltpu.SMEM((CLIPS,), jnp.int32),
            pltpu.SMEM((CLIPS,), jnp.int32),
            pltpu.VMEM((3, ROWS, HEADS * HEAD_DIM), BF16),
            pltpu.VMEM((3, NZL, NY, ROWS, 3 * HEAD_DIM), BF16),
            pltpu.VMEM((NZL, NZH, 2 * NX * DEPTH, PACK), BF16),
            pltpu.VMEM((2, DEPTH, COLS), BF16),
            pltpu.VMEM((NZH, 2 * NX * DEPTH, PACK), BF16),
            pltpu.VMEM((NX, NZH, DEPTH, PACK), BF16),
            pltpu.VMEM((NY, HALF, 3 * HEAD_DIM), BF16),
            pltpu.VMEM((2, HALF, MAIN), F32),
            pltpu.VMEM((HALF, 2 * EDGE), F32),
            pltpu.VMEM((HALF, MAIN), BF16),
            pltpu.VMEM((HALF, MAIN), BF16),
            pltpu.VMEM((2, QUART // 2, 2 * EDGE), BF16),
            pltpu.VMEM((2, QUART // 2, 2 * EDGE), BF16),
            pltpu.VMEM((1, COLS, SEQ), BF16),
            pltpu.VMEM((SEQ, MAIN + 2 * EDGE), F32),
            pltpu.VMEM((2, HEADS, COLS), F32),
            pltpu.VMEM((1, SEQ), F32),
            pltpu.VMEM((COLS, 128), F32),
            dma((6,)),
            dma((6,)),
            dma((2, NY)),
            dma((2, NY)),
            dma((2, NY)),
            dma((2, NY)),
            dma((2, NZ)),
            dma((NZ,)),
            dma((2, NZ)),
            dma((2, NZ)),
            dma((NZ,)),
            dma((NZ,)),
            dma((NX,)),
            dma((NX,)),
            dma((2, NY // 2, 5)),
            dma((2, NY // 2, 5)),
            dma((2, 2)),
            dma((2, 2)),
        ],
        compiler_params=pltpu.CompilerParams(
            collective_id=0, has_side_effects=True, vmem_limit_bytes=62 * 2**20
        ),
        cost_estimate=pl.CostEstimate(flops=2 * 10**9, bytes_accessed=3 * 10**6, transcendentals=10**6),
    )(
        queries,
        keys,
        values,
        jnp.swapaxes(residual, 1, 2),
        wo_values,
        jnp.swapaxes(wo_exponents, 0, 1),
        modulation,
        jnp.asarray(freq),
        expert_choice,
        step_index,
        lengths,
    )
    return jnp.swapaxes(mixed, 1, 2)


def solution(mesh):
    placed = (
        P("rep", "seq", None),
        P("rep", "seq", None),
        P("rep", "seq", None),
        P("rep", None, "seq"),
        P(None, "rep", "seq"),
        P(),
        P(None, "seq"),
        P(),
        P(),
        P(),
    )
    return jax.shard_map(
        local, mesh=mesh, in_specs=placed, out_specs=P("rep", None, "seq"), check_vma=False
    )
```
